128 devices in a mesh: vocab: 32 (over x, z, core), tok: 4 (over y).
Axes of the slice: x: 4, y: 4, z: 4, core: 2. Of those that a mesh axis runs over, the one named last changes fastest.
Arguments:
- comp_hidden: bfloat16 [4, 512, 4096], P(None, 'tok', 'vocab')
- embed: bfloat16 [65536, 4096], P('vocab')
- mix_logits: float32 [4, 512], P(None, 'tok')
- targets: int32 [512], P('tok'), may hold values from 0 to 65535
- loss_weight: float32 [512], P('tok'), may hold values from 1 to 10
Outputs:
- grad_hidden: float32 [4, 512, 4096], P(None, 'tok', 'vocab')
- grad_embed: bfloat16 [65536, 4096], P('vocab', 'tok')
- grad_mix: float32 [4, 512], P(None, 'tok')
The draws below stay inside these ranges and needn't reach their ends.
All inputs are finite; a program needn't handle non-finite values.
Results may differ from the reference program's by a relative error of at most 0.0049.
Values may be sent and summed in bfloat16 or wider, within the bound.
No kernel may reach another device: no remote copies, remote signals or barrier semaphores. Data moves between devices by JAX's collectives and lax.ppermute only.
A program may use at most 192 MiB of HBM per device.

```python
import math
import jax
import jax.numpy as jnp

COMP = 4
WIDTH = 4096
VOCAB = 65536
TOKENS = 512


def embed_rows(key, row_ids, width):

    def one_row(row_id):
        return jax.random.normal(jax.random.fold_in(key, row_id), (width,), jnp.float32)
    values = jnp.clip(jax.vmap(one_row)(row_ids), -5.0, 5.0) * (2.0 / math.sqrt(width))
    return values.astype(jnp.bfloat16).astype(jnp.float32)


def draw_embed(key, part):
    return embed_rows(key, jnp.arange(VOCAB, dtype=jnp.int32), WIDTH).astype(jnp.bfloat16)


def token_plan(key):
    keys = jax.random.split(jax.random.fold_in(key, 1073741831), 3)
    order = jax.random.permutation(keys[0], TOKENS).astype(jnp.int32)
    targets = jax.random.randint(keys[1], (TOKENS,), 0, VOCAB, dtype=jnp.int32)
    targets = targets.at[order[12]].set(0).at[order[13]].set(VOCAB - 1)
    winner = jax.random.randint(keys[2], (TOKENS,), 0, COMP, dtype=jnp.int32)
    return (order, targets, winner)


def mixture_numbers(key, winner, order):
    keys = jax.random.split(jax.random.fold_in(key, 1073741867), 8)
    spread = jnp.exp(jax.random.uniform(keys[0], (COMP, TOKENS), jnp.float32, math.log(1.0), math.log(1.5)))
    margin = jax.random.uniform(keys[1], (COMP, TOKENS), jnp.float32, 5.5, 8.0)
    level = jax.random.uniform(keys[2], (COMP, TOKENS), jnp.float32, 0.0, 3.0)
    win_margin = jax.random.uniform(keys[3], (TOKENS,), jnp.float32, 5.0, 7.0)
    comp_ids = jnp.arange(COMP, dtype=jnp.int32)[:, None]
    is_winner = comp_ids == winner[None, :]
    rank = (comp_ids - winner[None, :]) % COMP
    margin = jnp.where(is_winner, win_margin[None, :], margin)
    mix_pos = order[:4]
    in_mix = jnp.zeros((TOKENS,), jnp.bool_).at[mix_pos].set(True)
    gap = jnp.zeros((TOKENS,), jnp.float32).at[mix_pos].set(jax.random.uniform(keys[4], (4,), jnp.float32, 1.0, 3.0))
    first = (winner + 1) % COMP
    first_spread = jnp.take_along_axis(spread, first[None, :], axis=0)
    first_margin = jnp.take_along_axis(margin, first[None, :], axis=0)
    planted = in_mix[None, :] & (rank > 0)
    spread = jnp.where(planted, first_spread, spread)
    margin = jnp.where(planted, first_margin, margin)
    plant_level = 1.5 + jnp.where(rank >= 2, gap[None, :], 0.0) + jnp.where(rank == 3, 2.0, 0.0)
    level = jnp.where(planted, plant_level, level)
    score = jnp.where(is_winner, math.log(VOCAB) + 2.0 * spread * spread + margin, level)
    top_score = jax.random.uniform(keys[5], (8,), jnp.float32, 240.0, 340.0)
    top_gap = jax.random.uniform(keys[6], (8,), jnp.float32, 1.0, 2.5)
    shift = jax.random.uniform(keys[7], (4,), jnp.float32, 240.0, 340.0)
    return (is_winner, spread, margin, level, score, top_score, top_gap, shift)


def draw_targets(key, part):
    order, targets, winner = token_plan(key)
    return targets


def draw_comp_hidden(key, part):
    base_key = key
    order, targets, winner = token_plan(base_key)
    numbers = mixture_numbers(base_key, winner, order)
    spread = numbers[1]
    score = numbers[4]
    key = jax.random.fold_in(key, 1073741891)
    keys = jax.random.split(key, 1)
    target_rows = embed_rows(base_key, targets, WIDTH)
    noise = jnp.clip(jax.random.normal(keys[0], (COMP, TOKENS, WIDTH), jnp.float32), -4.0, 4.0)
    noise = noise * spread[:, :, None]
    along = jnp.sum(noise * target_rows[None, :, :], axis=-1)
    length = jnp.sum(target_rows * target_rows, axis=-1)
    factor = (score - along) / length[None, :]
    values = noise + factor[:, :, None] * target_rows[None, :, :]
    return jnp.clip(values, -24.0, 24.0).astype(jnp.bfloat16)


def draw_mix_logits(key, part):
    base_key = key
    order, targets, winner = token_plan(base_key)
    is_winner, spread, margin, level, score, top_score, top_gap, shift = mixture_numbers(base_key, winner, order)
    key = jax.random.fold_in(key, 1073741909)
    baseline = 1.2 * jnp.clip(jax.random.normal(key, (TOKENS,), jnp.float32), -4.0, 4.0)
    offset = math.log(VOCAB) + 2.0 * spread * spread - margin - level
    offset = jnp.where(is_winner, 0.0, offset)
    values = baseline[None, :] + offset
    return values


def level_of(key, shape, shards, low, top_value):
    loudness, own = 1.0, jax.random.fold_in(key, 6)
    for axis_at, parts in shards:
        heights = jnp.exp(jax.random.uniform(jax.random.fold_in(own, axis_at), (parts,), jnp.float32, low / len(shards), top_value / len(shards)))
        loudness = loudness * jnp.repeat(heights, shape[axis_at] // parts).reshape([-1 if axis == axis_at else 1 for axis in range(len(shape))])
    return loudness


def setup_inputs(seed: int = 0) -> dict:
    arg_keys = jax.random.split(jax.random.key(seed), 6)
    comp_hidden = draw_comp_hidden(jax.random.fold_in(arg_keys[5], 71), 0)
    embed = draw_embed(jax.random.fold_in(arg_keys[5], 71), 0)
    mix_logits = draw_mix_logits(jax.random.fold_in(arg_keys[5], 71), 0)
    targets = draw_targets(jax.random.fold_in(arg_keys[5], 71), 0)
    loss_weight = jnp.clip(jnp.exp(math.log(10.0) - 2.3025851 * jax.random.uniform(arg_keys[4], (TOKENS,), jnp.float32) ** level_of(arg_keys[4], (TOKENS,), ((0, 4),), -0.2, 0.2)), 1.0, 10.0)
    return dict(comp_hidden=comp_hidden, embed=embed, mix_logits=mix_logits, targets=targets, loss_weight=loss_weight)


def reference(comp_hidden, embed, mix_logits, targets, loss_weight):
    vocab_ids = jnp.arange(VOCAB, dtype=jnp.int32)
    target_mask = (vocab_ids[None, :] == targets[:, None]).astype(jnp.float32)
    lse_list = []
    target_list = []
    for index in range(COMP):
        logits = jnp.dot(comp_hidden[index], embed.T, preferred_element_type=jnp.float32)
        largest = jnp.max(logits, axis=1)
        lse_list.append(largest + jnp.log(jnp.sum(jnp.exp(logits - largest[:, None]), axis=1)))
        target_list.append(jnp.sum(logits * target_mask, axis=1))
    lse = jnp.stack(lse_list)
    target_logit = jnp.stack(target_list)
    log_mix = jax.nn.log_softmax(mix_logits, axis=0)
    resp = jax.nn.softmax(log_mix + target_logit - lse, axis=0)
    grad_mix = loss_weight[None, :] * (jnp.exp(log_mix) - resp)
    weighting = loss_weight[None, :] * resp
    grad_embed = jnp.zeros((VOCAB, WIDTH), jnp.float32)
    hidden_list = []
    for index in range(COMP):
        logits = jnp.dot(comp_hidden[index], embed.T, preferred_element_type=jnp.float32)
        probs = jnp.exp(logits - lse[index][:, None])
        token_grad = (weighting[index][:, None] * (probs - target_mask)).astype(jnp.bfloat16)
        hidden_list.append(jnp.dot(token_grad, embed, preferred_element_type=jnp.float32))
        grad_embed = grad_embed + jnp.dot(token_grad.T, comp_hidden[index], preferred_element_type=jnp.float32)
    return jnp.stack(hidden_list), grad_embed.astype(jnp.bfloat16), grad_mix
```

```python
import functools

import jax
import jax.numpy as jnp
from jax import lax
from jax.experimental import pallas as pl
from jax.experimental.pallas import tpu as pltpu
from jax.sharding import Mesh, PartitionSpec as P

BF, F32 = jnp.bfloat16, jnp.float32
ROWS = 512
WIDTH = 4096
VOC = 2048
SUB = 256
TILE = 512
VMEM = 56 * 2**20


def shift(a, axis, d):
    return lax.ppermute(a, axis, [((i + d) % 4, i) for i in range(4)])


def sibling(a):
    return lax.ppermute(a, "c", [(0, 1), (1, 0)])


def tied(a, *deps):
    return lax.optimization_barrier((a, *deps))[0]


def dot_nt(a, b):
    return lax.dot_general(a, b, (((1,), (1,)), ((), ())), preferred_element_type=F32)


def dot_nn(a, b):
    return lax.dot_general(a, b, (((1,), (0,)), ((), ())), preferred_element_type=F32)


def params(**kw):
    return pltpu.CompilerParams(vmem_limit_bytes=VMEM, **kw)


def ring_first(h, axis):
    p, m = shift(h, axis, 1), shift(h, axis, -1)
    tp = shift(p[..., :128, :], axis, 1)
    tm = shift(m[..., 128:, :], axis, -1)
    return jnp.stack([h, p, m, jnp.concatenate([tp, tm], axis=-2)], axis=-3)


def ring_second(s, axis):
    p, m = shift(s, axis, 1), shift(s, axis, -1)
    return p, m, shift(p[:2], axis, 1), shift(m[2:], axis, -1)


OFFS = (0, 1, 3, 2)


def piece_blocks():
    full = [[(a, b) for a in OFFS] for b in (0, 1, 3)]
    return full + [[(a, 2) for a in OFFS[:2]], [(a, 2) for a in OFFS[2:]]]


def logits_body(first, n_pieces, v0, steps, *refs):
    at = refs[0]
    refs = refs[1:]
    pieces, refs = refs[:n_pieces], refs[n_pieces:]
    tid, emb, refs = refs[0], refs[1], refs[2:]
    if first:
        e_out, st_out, loc_out, full_out, quarter_out, low_out, high_out, full, sem, osem = refs
    else:
        e_out, st_out, loc_out, full, sem = refs
    step = pl.program_id(0)
    x, z, c, y = at[0], at[1], at[2], at[3]

    @pl.when(step == 0)
    def _():
        copies = []
        if first:
            half = n_pieces // 2
            for n in range(n_pieces):
                core = c if n < half else 1 - c
                m = n % half
                rows = (m // 5) * 256
                for b, (o1, o2) in enumerate(piece_blocks()[m % 5]):
                    dx, dz = (o1, o2) if m < 5 else (o2, o1)
                    col = ((((x + dx) & 3) * 4 + ((z + dz) & 3)) * 2 + core) * 128
                    copies.append((pieces[n].at[b], (pl.ds(rows, 256), pl.ds(pl.multiple_of(col, 128), 128))))
            for k, (src, dst) in enumerate(copies):
                pltpu.make_async_copy(src, full.at[dst], sem.at[k]).start()
            for k, (src, dst) in enumerate(copies):
                pltpu.make_async_copy(src, full.at[dst], sem.at[k]).wait()
        else:
            copy = pltpu.make_async_copy(pieces[0], full, sem.at[0])
            copy.start()
            copy.wait()
        loc_out[...] = jnp.zeros((8, ROWS), F32)
        st_out[...] = jnp.zeros((8, ROWS), F32)

    if first:
        outs = [
            pltpu.make_async_copy(full, full_out, osem.at[0]),
            pltpu.make_async_copy(
                full.at[:, pl.ds(pl.multiple_of(y * 1024, 1024), 1024)], quarter_out, osem.at[1]
            ),
        ]
        for n, (ref, at_y) in enumerate(((low_out, (y + 3) & 3), (high_out, (y + 1) & 3))):
            for k in range(4):
                col = pl.multiple_of((at_y * 8 + k * 2 + c) * 128, 128)
                outs.append(pltpu.make_async_copy(full.at[:, pl.ds(col, 128)], ref.at[k], osem.at[2 + n * 4 + k]))

        @pl.when(step == 0)
        def _():
            for copy in outs:
                copy.start()

    tops, sums, hits = [], [], []
    for sub in range(TILE // SUB):
        logits = dot_nt(emb[pl.ds(sub * SUB, SUB), :], full[...])
        top = jnp.max(logits, axis=0, keepdims=True)
        ids = lax.broadcasted_iota(jnp.int32, logits.shape, 0) + (v0 + step * TILE + sub * SUB)
        hits.append(jnp.sum(jnp.where(ids == tid[...], logits, 0.0), axis=0, keepdims=True))
        e = jnp.exp(logits - top)
        sums.append(jnp.sum(e, axis=0, keepdims=True))
        tops.append(top)
        e_out[pl.ds(sub * SUB, SUB), :] = e.astype(BF)
    for s in range(steps):

        @pl.when(step == s)
        def _():
            for sub in range(TILE // SUB):
                st_out[pl.ds(s * (TILE // SUB) + sub, 1), :] = tops[sub]

    tile_top = jnp.maximum(tops[0], tops[1])
    tile_sum = sums[0] * jnp.exp(tops[0] - tile_top) + sums[1] * jnp.exp(tops[1] - tile_top)
    tile_hit = hits[0] + hits[1]

    @pl.when(step == 0)
    def _():
        loc_out[pl.ds(0, 1), :] = tile_top
        loc_out[pl.ds(1, 1), :] = tile_sum
        loc_out[pl.ds(2, 1), :] = tile_hit

    @pl.when(step > 0)
    def _():
        old = loc_out[pl.ds(0, 1), :]
        top = jnp.maximum(old, tile_top)
        loc_out[pl.ds(1, 1), :] = loc_out[pl.ds(1, 1), :] * jnp.exp(old - top) + tile_sum * jnp.exp(tile_top - top)
        loc_out[pl.ds(0, 1), :] = top
        loc_out[pl.ds(2, 1), :] = loc_out[pl.ds(2, 1), :] + tile_hit

    if first:

        @pl.when(step == steps - 1)
        def _():
            for copy in outs:
                copy.wait()


def logits_call(at, pieces, tid, emb, v0, rows, name):
    first = len(pieces) > 1
    steps = rows // TILE
    whole = pl.BlockSpec((8, ROWS), lambda i, at: (0, 0))
    hbm = pl.BlockSpec(memory_space=pl.ANY)
    n = 64 if first else 1
    out_shape = [
        jax.ShapeDtypeStruct((rows, ROWS), BF),
        jax.ShapeDtypeStruct((8, ROWS), F32),
        jax.ShapeDtypeStruct((8, ROWS), F32),
    ]
    out_specs = [pl.BlockSpec((TILE, ROWS), lambda i, at: (i, 0)), whole, whole]
    scratch = [pltpu.VMEM((ROWS, WIDTH), BF), pltpu.SemaphoreType.DMA((n,))]
    if first:
        out_shape += [jax.ShapeDtypeStruct((ROWS, WIDTH), BF), jax.ShapeDtypeStruct((ROWS, 1024), BF)]
        out_shape += [jax.ShapeDtypeStruct((4, ROWS, 128), BF)] * 2
        out_specs += [hbm] * 4
        scratch += [pltpu.SemaphoreType.DMA((10,))]
    base = v0 // TILE
    return pl.pallas_call(
        functools.partial(logits_body, first, len(pieces), v0, steps),
        grid_spec=pltpu.PrefetchScalarGridSpec(
            num_scalar_prefetch=1,
            grid=(steps,),
            in_specs=[hbm] * len(pieces)
            + [
                pl.BlockSpec((1, ROWS), lambda i, at: (0, 0)),
                pl.BlockSpec((TILE, WIDTH), lambda i, at: (i + base, 0)),
            ],
            out_specs=out_specs,
            scratch_shapes=scratch,
        ),
        out_shape=out_shape,
        compiler_params=params(),
        cost_estimate=pl.CostEstimate(
            flops=2 * rows * ROWS * WIDTH, bytes_accessed=2 * rows * WIDTH, transcendentals=rows * ROWS
        ),
        name=name,
    )(at, *pieces, tid, emb)


def merge(parts):
    top = functools.reduce(jnp.maximum, [p[0:1] for p in parts])
    total = sum(p[1:2] * jnp.exp(p[0:1] - top) for p in parts)
    hit = sum(p[2:3] for p in parts)
    return top, total, hit


def merge_body(*refs):
    top, total, hit = merge([r[...] for r in refs[:-1]])
    out = refs[-1]
    out[...] = jnp.zeros((8, ROWS), F32)
    out[pl.ds(0, 1), :] = top
    out[pl.ds(1, 1), :] = total
    out[pl.ds(2, 1), :] = hit


def merge_call(*parts):
    return pl.pallas_call(
        merge_body,
        out_shape=jax.ShapeDtypeStruct((8, ROWS), F32),
        compiler_params=params(),
        cost_estimate=pl.CostEstimate(flops=10000, bytes_accessed=70000, transcendentals=2000),
        name="merge",
    )(*parts)


def finish_body(a, b, st_a, st_b, tid, mix, weight, pack, grad_mix):
    top, total, hit = merge([a[...], b[...]])
    lse = top + jnp.log(total)
    gap = hit - lse
    mixes = [mix[pl.ds(k, 1), :] for k in range(4)]
    big = functools.reduce(jnp.maximum, mixes)
    norm = big + jnp.log(sum(jnp.exp(m - big) for m in mixes))
    logm = [m - norm for m in mixes]
    score = [logm[k] + gap[:, k * 128 : (k + 1) * 128] for k in range(4)]
    big = functools.reduce(jnp.maximum, score)
    ex = [jnp.exp(s - big) for s in score]
    den = sum(ex)
    w = weight[...]
    scaled = []
    for k in range(4):
        resp = ex[k] / den
        grad_mix[pl.ds(k, 1), :] = w * (jnp.exp(logm[k]) - resp)
        scaled.append(w * resp)
    d = jnp.concatenate(scaled, axis=1)
    pack[...] = jnp.zeros((16, ROWS), F32)
    pack[pl.ds(0, 4), :] = jnp.exp(st_a[pl.ds(0, 4), :] - lse) * d
    pack[pl.ds(4, 4), :] = jnp.exp(st_b[pl.ds(0, 4), :] - lse) * d
    pack[pl.ds(8, 1), :] = d
    pack[pl.ds(9, 1), :] = lse
    pack[pl.ds(10, 1), :] = tid[...].astype(F32)


def finish_call(a, b, st_a, st_b, tid, mix, weight):
    return pl.pallas_call(
        finish_body,
        out_shape=[jax.ShapeDtypeStruct((16, ROWS), F32), jax.ShapeDtypeStruct((4, 128), F32)],
        compiler_params=params(),
        cost_estimate=pl.CostEstimate(flops=20000, bytes_accessed=150000, transcendentals=10000),
        name="finish",
    )(a, b, st_a, st_b, tid, mix, weight)


def token_grad(e, pack, sub, base):
    ids = lax.broadcasted_iota(jnp.int32, e.shape, 0) + base
    tid = pack[pl.ds(10, 1), :].astype(jnp.int32)
    g = e.astype(F32) * pack[pl.ds(sub, 1), :]
    return (g - jnp.where(ids == tid, pack[pl.ds(8, 1), :], 0.0)).astype(BF)


def hidden_a_body(at, e_a, e_b, pack, w0, w1, w2, w3, out, tg_out, tgt_out):
    @pl.when(pl.program_id(0) == 0)
    def _():
        for sub in range(8):
            src = e_a if sub < 4 else e_b
            g = token_grad(src[pl.ds((sub % 4) * SUB, SUB), :], pack, sub, sub * SUB)
            tgt_out[pl.ds(sub * SUB, SUB), :] = g
            tg_out[:, pl.ds(sub * SUB, SUB)] = g.T

    w = jnp.concatenate([w0[...], w1[...], w2[...], w3[...]], axis=1)
    r = dot_nn(tg_out[...], w)
    for k in range(4):
        out[0, k] = r[:, k * 128 : (k + 1) * 128].astype(BF)


def hidden_b_body(at, tg, recv, w0, w1, w2, w3, out_a, out_b):
    w = jnp.concatenate([w0[...], w1[...], w2[...], w3[...]], axis=1)
    r = dot_nn(tg[...], w)
    for k in range(4):
        t = r[:, k * 128 : (k + 1) * 128] + recv[0, k].astype(F32)
        out_a[0, k] = t[:256].astype(BF)
        out_b[k, 0] = t[256:].astype(BF)


def weight_specs(flip):
    def spec(dz):
        def index(i, at):
            core = 1 - at[2] if flip else at[2]
            return (0, (((at[0] + i) & 3) * 4 + ((at[1] + dz) & 3)) * 2 + core)

        return pl.BlockSpec((VOC, 128), index)

    return [spec(dz) for dz in range(4)]


HALF_COST = dict(flops=VOC * ROWS * WIDTH, bytes_accessed=VOC * WIDTH, transcendentals=0)


def hidden_a_call(at, e_a, e_b, pack, emb):
    whole = lambda s: pl.BlockSpec(s, lambda i, at: (0,) * len(s))
    return pl.pallas_call(
        hidden_a_body,
        grid_spec=pltpu.PrefetchScalarGridSpec(
            num_scalar_prefetch=1,
            grid=(4,),
            in_specs=[whole((1024, ROWS)), whole((1024, ROWS)), whole((16, ROWS))] + weight_specs(True),
            out_specs=[
                pl.BlockSpec((1, 4, ROWS, 128), lambda i, at: (i, 0, 0, 0)),
                whole((ROWS, VOC)),
                whole((VOC, ROWS)),
            ],
        ),
        out_shape=[
            jax.ShapeDtypeStruct((4, 4, ROWS, 128), BF),
            jax.ShapeDtypeStruct((ROWS, VOC), BF),
            jax.ShapeDtypeStruct((VOC, ROWS), BF),
        ],
        compiler_params=params(),
        cost_estimate=pl.CostEstimate(**HALF_COST),
        name="hidden_a",
    )(at, e_a, e_b, pack, emb, emb, emb, emb)


def hidden_b_call(at, tg, recv, emb):
    return pl.pallas_call(
        hidden_b_body,
        grid_spec=pltpu.PrefetchScalarGridSpec(
            num_scalar_prefetch=1,
            grid=(4,),
            in_specs=[
                pl.BlockSpec((ROWS, VOC), lambda i, at: (0, 0)),
                pl.BlockSpec((1, 4, ROWS, 128), lambda i, at: (i, 0, 0, 0)),
            ]
            + weight_specs(False),
            out_specs=[
                pl.BlockSpec((1, 4, 256, 128), lambda i, at: (i, 0, 0, 0)),
                pl.BlockSpec((4, 1, 256, 128), lambda i, at: (0, i, 0, 0)),
            ],
        ),
        out_shape=[jax.ShapeDtypeStruct((4, 4, 256, 128), BF)] * 2,
        compiler_params=params(),
        cost_estimate=pl.CostEstimate(**HALF_COST),
        name="hidden_b",
    )(at, tg, recv, emb, emb, emb, emb)


def add(*xs):
    return sum(x.astype(F32) for x in xs)


def ring_sum(b, axis):
    n = b.shape[-2] // 2
    r1 = shift(b[2][..., :n, :], axis, -1)
    r3 = shift(b[2][..., n:, :], axis, 1)
    s1 = jnp.concatenate([add(b[1][..., :n, :], r1).astype(BF), b[1][..., n:, :]], axis=-2)
    s3 = jnp.concatenate([b[3][..., :n, :], add(b[3][..., n:, :], r3).astype(BF)], axis=-2)
    return add(b[0], shift(s1, axis, -1), shift(s3, axis, 1))


def embed_a_body(tgt, e_a, e_b, st_a, st_b, pack, q_own, q_diag, acc):
    i = pl.program_id(0)
    d = pack[pl.ds(8, 1), :]
    lse = pack[pl.ds(9, 1), :]
    tid = pack[pl.ds(10, 1), :].astype(jnp.int32)
    parts = []
    for sub in range(TILE // SUB):
        row = lax.rem(i, 2) * 2 + sub
        first = i < 2
        top = jnp.where(first, st_a[pl.ds(row, 1), :], st_b[pl.ds(row, 1), :])
        sl = pl.ds(sub * SUB, SUB)
        e = jnp.where(first, e_a[sl, :], e_b[sl, :]).astype(F32)
        ids = lax.broadcasted_iota(jnp.int32, e.shape, 0) + (i * TILE + sub * SUB)
        parts.append((e * (jnp.exp(top - lse) * d) - jnp.where(ids == tid, d, 0.0)).astype(BF))
    g = jnp.concatenate(parts, axis=0)
    acc[...] = dot_nn(tgt[...], q_own[...]) + dot_nn(g, q_diag[...])


def embed_a_call(tgt, e_a, e_b, st_a, st_b, pack, q_own, q_diag):
    whole = lambda s: pl.BlockSpec(s, lambda i: (0,) * len(s))
    return pl.pallas_call(
        embed_a_body,
        grid=(VOC // TILE,),
        in_specs=[
            pl.BlockSpec((TILE, ROWS), lambda i: (i, 0)),
            pl.BlockSpec((TILE, ROWS), lambda i: (jnp.minimum(i, 1), 0)),
            pl.BlockSpec((TILE, ROWS), lambda i: (jnp.maximum(i - 2, 0), 0)),
            whole((8, ROWS)),
            whole((8, ROWS)),
            whole((16, ROWS)),
            whole((ROWS, 1024)),
            whole((ROWS, 1024)),
        ],
        out_specs=pl.BlockSpec((TILE, 1024), lambda i: (i, 0)),
        out_shape=jax.ShapeDtypeStruct((VOC, 1024), F32),
        compiler_params=params(),
        cost_estimate=pl.CostEstimate(flops=2 * VOC * 1024 * 1024, bytes_accessed=14 * 2**20, transcendentals=0),
        name="embed_a",
    )(tgt, e_a, e_b, st_a, st_b, pack, q_own, q_diag)


def embed_b_body(at, acc, pa, pb, ma, mb, pack_p, pack_m, qp, qps, qm, qms, out, q, sem):
    i = pl.program_id(0)

    @pl.when(i == 0)
    def _():
        copies = []
        for n, (ref, other, row) in enumerate(((qp, False, 0), (qps, True, 0), (qm, False, 512), (qms, True, 512))):
            core = 1 - at[2] if other else at[2]
            for z in range(4):
                col = pl.multiple_of((z * 2 + core) * 128, 128)
                copies.append((ref.at[z], q.at[pl.ds(row, 512), pl.ds(col, 128)], sem.at[n * 4 + z]))
        for c in copies:
            pltpu.make_async_copy(*c).start()
        for c in copies:
            pltpu.make_async_copy(*c).wait()

    parts = []
    for a, b, pack in ((pa, pb, pack_p), (ma, mb, pack_m)):
        col = []
        for sub in range(TILE // SUB):
            sl = pl.ds(sub * SUB, SUB)
            e = jnp.where(i < 2, a[sl, :], b[sl, :])
            col.append(token_grad(e, pack, i * 2 + sub, i * TILE + sub * SUB))
        parts.append(jnp.concatenate(col, axis=0))
    g = jnp.concatenate(parts, axis=1)
    out[...] = (acc[...] + dot_nn(g, q[...])).astype(BF)


def embed_b_call(at, acc, pa, pb, ma, mb, pack_p, pack_m, qp, qps, qm, qms):
    low = pl.BlockSpec((TILE, ROWS), lambda i, at: (jnp.minimum(i, 1), 0))
    high = pl.BlockSpec((TILE, ROWS), lambda i, at: (jnp.maximum(i - 2, 0), 0))
    pack = pl.BlockSpec((16, ROWS), lambda i, at: (0, 0))
    hbm = pl.BlockSpec(memory_space=pl.ANY)
    tile = pl.BlockSpec((TILE, 1024), lambda i, at: (i, 0))
    return pl.pallas_call(
        embed_b_body,
        grid_spec=pltpu.PrefetchScalarGridSpec(
            num_scalar_prefetch=1,
            grid=(VOC // TILE,),
            in_specs=[tile, low, high, low, high, pack, pack] + [hbm] * 4,
            out_specs=tile,
            scratch_shapes=[pltpu.VMEM((1024, 1024), BF), pltpu.SemaphoreType.DMA((16,))],
        ),
        out_shape=jax.ShapeDtypeStruct((VOC, 1024), BF),
        compiler_params=params(),
        cost_estimate=pl.CostEstimate(flops=2 * VOC * 1024 * 1024, bytes_accessed=18 * 2**20, transcendentals=0),
        name="embed_b",
    )(at, acc, pa, pb, ma, mb, pack_p, pack_m, qp, qps, qm, qms)


def local(comp_hidden, embed, mix, targets, weight):
    x, z, c, y = (lax.axis_index(a).astype(jnp.int32) for a in ("x", "z", "c", "y"))
    at = jnp.stack([x, z, c, y])
    own = comp_hidden.reshape(ROWS, 128)
    diag = shift(own, "y", 2)
    local_ids = targets - ((x * 4 + z) * 2 + c) * VOC
    tid = jnp.tile(local_ids, 4).reshape(1, ROWS)

    def gather(block):
        sa, sb = ring_first(block[:256], "x"), ring_first(block[256:], "z")
        a2, b2 = ring_second(sa, "z"), ring_second(sb, "x")
        return [sa, *a2, sb, *b2]

    mine = gather(own)
    pieces = mine + [sibling(p) for p in mine]
    v_half = VOC // 2
    e0, st0, loc0, full, q_own, q_low, q_high = logits_call(at, pieces, tid, embed, 0, v_half, "logits_own_a")
    e1, st1, loc1 = logits_call(at, [full], tid, embed, v_half, v_half, "logits_own_b")

    qp, qm = shift(q_low, "y", 1), shift(q_high, "y", -1)
    qps, qms = sibling(qp), sibling(qm)

    ep0, em0 = shift(e0, "y", 1), shift(e0, "y", -1)
    ep1, em1 = shift(e1, "y", 1), shift(e1, "y", -1)

    s = merge_call(loc0, loc1)
    s = merge_call(s, *(shift(s, "x", d) for d in (1, 2, 3)))
    s = merge_call(s, *(shift(s, "z", d) for d in (1, 2, 3)))
    pack, grad_mix = finish_call(s, sibling(s), st0, st1, tid, mix, weight.reshape(1, 128))
    pack_p, pack_m, pack_d = shift(pack, "y", 1), shift(pack, "y", -1), shift(pack, "y", 2)

    theirs = gather(diag)
    d_pieces = theirs + [sibling(p) for p in theirs]
    f0, ds0, _, d_full, q_diag, _, _ = logits_call(at, d_pieces, tid, embed, 0, v_half, "logits_diag_a")
    f1, ds1, _ = logits_call(at, [d_full], tid, embed, v_half, v_half, "logits_diag_b")

    send, tg, tgt = hidden_a_call(at, e0, e1, pack, embed)
    ra, rb = hidden_b_call(at, tg, sibling(send), embed)
    ra = ring_sum(ra, "x").astype(BF)
    rb = ring_sum(rb, "z").astype(BF)
    grad_hidden = jnp.concatenate([ring_sum(ra, "z"), ring_sum(rb, "x")], axis=0)

    acc = embed_a_call(tgt, f0, f1, ds0, ds1, pack_d, q_own, q_diag)
    grad_embed = embed_b_call(at, acc, ep0, ep1, em0, em1, pack_p, pack_m, qp, qps, qm, qms)
    return grad_hidden.reshape(4, 128, 128), grad_embed, grad_mix


def solution(mesh):
    fine = Mesh(mesh.devices.reshape(4, 4, 2, 4), ("x", "z", "c", "y"))
    v = ("x", "z", "c")
    return jax.shard_map(
        local,
        mesh=fine,
        in_specs=(P(None, "y", v), P(v, None), P(None, "y"), P("y"), P("y")),
        out_specs=(P(None, "y", v), P(v, "y"), P(None, "y")),
        check_vma=False,
    )
```

```python
import functools

import jax
import jax.numpy as jnp
from jax import lax
from jax.experimental import pallas as pl
from jax.experimental.pallas import tpu as pltpu
from jax.sharding import Mesh, PartitionSpec as P

BF, F32 = jnp.bfloat16, jnp.float32
ROWS = 512
HALF = 256
WIDTH = 4096
VOC = 2048
TILE = 512
TILES = VOC // TILE
VMEM = 56 * 2**20


def shift(a, axis, d):
    return lax.ppermute(a, axis, [((i + d) % 4, i) for i in range(4)])


def sibling(a):
    return lax.ppermute(a, "c", [(0, 1), (1, 0)])


def cross(a, which, d):
    pairs = []
    for x in range(4):
        for z in range(4):
            for c in range(2):
                along_x = (c + which) % 2 == 0
                sx, sz = ((x + d) % 4, z) if along_x else (x, (z + d) % 4)
                pairs.append(((sx * 4 + sz) * 2 + c, (x * 4 + z) * 2 + c))
    return lax.ppermute(a, ("x", "z", "c"), pairs)


def dot_nt(a, b):
    return lax.dot_general(a, b, (((1,), (1,)), ((), ())), preferred_element_type=F32)


def dot_nn(a, b):
    return lax.dot_general(a, b, (((1,), (0,)), ((), ())), preferred_element_type=F32)


def params(**kw):
    return pltpu.CompilerParams(vmem_limit_bytes=VMEM, **kw)


SMALL = pl.CostEstimate(flops=1000, bytes_accessed=1000, transcendentals=0)
HBM = pl.BlockSpec(memory_space=pltpu.HBM)


def gate_body(*refs):
    pass


def gate(*arrays):
    n = len(arrays)
    return pl.pallas_call(
        gate_body,
        in_specs=[HBM] * n,
        out_specs=[HBM] * n,
        out_shape=[jax.ShapeDtypeStruct(a.shape, a.dtype) for a in arrays],
        input_output_aliases={i: i for i in range(n)},
        compiler_params=params(),
        cost_estimate=SMALL,
        name="gate",
    )(*arrays)


LOW = pl.BlockSpec((TILE, ROWS), lambda i, at: (0, 0))
HIGH = pl.BlockSpec((TILE, ROWS), lambda i, at: (jnp.maximum(i - 1, 0), 0))


def pick(i, low, high):
    return jnp.where(i == 0, low[...], high[...])


def gather_pieces(block):
    s = jnp.stack([block] + [cross(block, 0, d) for d in (1, 2, 3)])
    p, m = cross(s, 1, 1), cross(s, 1, 3)
    dp, dm = cross(p[:2], 1, 1), cross(m[2:], 1, 3)
    return [s, p, m, dp, dm]


PLACES = [
    [(a, 0) for a in range(4)],
    [(a, 1) for a in range(4)],
    [(a, 3) for a in range(4)],
    [(0, 2), (1, 2)],
    [(2, 2), (3, 2)],
]


def logits_body(at, *refs):
    pieces, refs = refs[:10], refs[10:]
    tid, emb, e0_out, e1_out, st_out, loc_out, full, sem = refs
    step = pl.program_id(0)
    x, z, c = at[0], at[1], at[2]

    @pl.when(step == 0)
    def _():
        copies = []
        for n in range(10):
            core = c if n < 5 else 1 - c
            row = pl.multiple_of(core * HALF, HALF)
            for b, (o1, o2) in enumerate(PLACES[n % 5]):
                dx = jnp.where(core == 0, o1, o2)
                dz = jnp.where(core == 0, o2, o1)
                col = pl.multiple_of((((x + dx) & 3) * 4 + ((z + dz) & 3)) * 256, 256)
                copies.append((pieces[n].at[b], full.at[pl.ds(row, HALF), pl.ds(col, 256)], sem.at[len(copies)]))
        for copy in copies:
            pltpu.make_async_copy(*copy).start()
        for copy in copies:
            pltpu.make_async_copy(*copy).wait()
        st_out[...] = jnp.zeros((8, ROWS), F32)
        loc_out[...] = jnp.zeros((8, ROWS), F32)

    logits = dot_nt(emb[...], full[...])
    top = jnp.max(logits, axis=0, keepdims=True)
    ids = lax.broadcasted_iota(jnp.int32, logits.shape, 0) + step * TILE
    hit = jnp.sum(jnp.where(ids == tid[...], logits, 0.0), axis=0, keepdims=True)
    e = jnp.exp(logits - top)
    total = jnp.sum(e, axis=0, keepdims=True)
    e = e.astype(BF)

    @pl.when(step == 0)
    def _():
        e0_out[...] = e

    @pl.when(step > 0)
    def _():
        e1_out[...] = e

    for s in range(TILES):

        @pl.when(step == s)
        def _():
            st_out[pl.ds(s, 1), :] = top

    @pl.when(step == 0)
    def _():
        loc_out[pl.ds(0, 1), :] = top
        loc_out[pl.ds(1, 1), :] = total
        loc_out[pl.ds(2, 1), :] = hit

    @pl.when(step > 0)
    def _():
        old = loc_out[pl.ds(0, 1), :]
        new = jnp.maximum(old, top)
        loc_out[pl.ds(1, 1), :] = loc_out[pl.ds(1, 1), :] * jnp.exp(old - new) + total * jnp.exp(top - new)
        loc_out[pl.ds(0, 1), :] = new
        loc_out[pl.ds(2, 1), :] = loc_out[pl.ds(2, 1), :] + hit


def logits_call(at, pieces, tid, emb, name):
    whole = pl.BlockSpec((8, ROWS), lambda i, at: (0, 0))
    return pl.pallas_call(
        logits_body,
        grid_spec=pltpu.PrefetchScalarGridSpec(
            num_scalar_prefetch=1,
            grid=(TILES,),
            in_specs=[HBM] * 10
            + [pl.BlockSpec((1, ROWS), lambda i, at: (0, 0)), pl.BlockSpec((TILE, WIDTH), lambda i, at: (i, 0))],
            out_specs=[LOW, HIGH, whole, whole],
            scratch_shapes=[pltpu.VMEM((ROWS, WIDTH), BF), pltpu.SemaphoreType.DMA((32,))],
        ),
        out_shape=[
            jax.ShapeDtypeStruct((TILE, ROWS), BF),
            jax.ShapeDtypeStruct((VOC - TILE, ROWS), BF),
            jax.ShapeDtypeStruct((8, ROWS), F32),
            jax.ShapeDtypeStruct((8, ROWS), F32),
        ],
        compiler_params=params(),
        cost_estimate=SMALL,
        name=name,
    )(at, *pieces, tid, emb)


def merge(parts):
    top = functools.reduce(jnp.maximum, [p[0:1] for p in parts])
    total = sum(p[1:2] * jnp.exp(p[0:1] - top) for p in parts)
    hit = sum(p[2:3] for p in parts)
    return top, total, hit


def merge_body(*refs):
    top, total, hit = merge([r[...] for r in refs[:-1]])
    out = refs[-1]
    out[...] = jnp.zeros((8, ROWS), F32)
    out[pl.ds(0, 1), :] = top
    out[pl.ds(1, 1), :] = total
    out[pl.ds(2, 1), :] = hit


def merge_call(*parts):
    return pl.pallas_call(
        merge_body,
        out_shape=jax.ShapeDtypeStruct((8, ROWS), F32),
        compiler_params=params(),
        cost_estimate=SMALL,
        name="merge",
    )(*parts)


def finish_body(a, b, st, tid, mix, weight, feats, ep0, em0, pack, grad_mix):
    top, total, hit = merge([a[...], b[...]])
    lse = top + jnp.log(total)
    gap = hit - lse
    mixes = [mix[pl.ds(k, 1), :] for k in range(4)]
    big = functools.reduce(jnp.maximum, mixes)
    norm = big + jnp.log(sum(jnp.exp(m - big) for m in mixes))
    logm = [m - norm for m in mixes]
    score = [logm[k] + gap[:, k * 128 : (k + 1) * 128] for k in range(4)]
    big = functools.reduce(jnp.maximum, score)
    ex = [jnp.exp(s - big) for s in score]
    den = sum(ex)
    w = weight[...]
    scaled = []
    for k in range(4):
        resp = ex[k] / den
        grad_mix[pl.ds(k, 1), :] = w * (jnp.exp(logm[k]) - resp)
        scaled.append(w * resp)
    d = jnp.concatenate(scaled, axis=1)
    pack[...] = jnp.zeros((8, ROWS), F32)
    pack[pl.ds(0, TILES), :] = jnp.exp(st[pl.ds(0, TILES), :] - lse) * d
    pack[pl.ds(4, 1), :] = d
    pack[pl.ds(5, 1), :] = lse
    pack[pl.ds(6, 1), :] = tid[...].astype(F32)


def finish_call(a, b, st, tid, mix, weight, *awaited):
    return pl.pallas_call(
        finish_body,
        in_specs=[pl.BlockSpec(memory_space=pltpu.VMEM)] * 6 + [HBM] * 3,
        out_shape=[jax.ShapeDtypeStruct((8, ROWS), F32), jax.ShapeDtypeStruct((4, 128), F32)],
        compiler_params=params(),
        cost_estimate=SMALL,
        name="finish",
    )(a, b, st, tid, mix, weight, *awaited)


def token_grad(e, pack, scale, base):
    ids = lax.broadcasted_iota(jnp.int32, e.shape, 0) + base
    tid = pack[pl.ds(6, 1), :].astype(jnp.int32)
    g = e.astype(F32) * scale
    return (g - jnp.where(ids == tid, pack[pl.ds(4, 1), :], 0.0)).astype(BF)


def hidden_body(at, e0, e1, pack, w0, w1, w2, w3, keep, send0, send1, tgt_out, tg):
    @pl.when(pl.program_id(0) == 0)
    def _():
        for t in range(TILES):
            rows = pl.ds(t * TILE, TILE)
            e = e0[...] if t == 0 else e1[pl.ds((t - 1) * TILE, TILE), :]
            g = token_grad(e, pack, pack[pl.ds(t, 1), :], t * TILE)
            tgt_out[rows, :] = g
            tg[:, rows] = g.T

    w = jnp.concatenate([w0[...], w1[...], w2[...], w3[...]], axis=1)
    r = dot_nn(tg[...], w)
    first = at[2] == 0
    for k in range(4):
        cols = slice(k * 256, (k + 1) * 256)
        a, b = r[:HALF, cols], r[HALF:, cols]
        keep[0, k] = jnp.where(first, a, b)
        (send0, send1)[k // 2][k % 2, 0] = jnp.where(first, b, a).astype(BF)


def hidden_call(at, e0, e1, pack, emb):
    whole = lambda s: pl.BlockSpec(s, lambda i, at: (0,) * len(s))

    def weight(k):
        def index(i, at):
            dx = jnp.where(at[2] == 0, i, k)
            dz = jnp.where(at[2] == 0, k, i)
            return (0, ((at[0] + dx) & 3) * 4 + ((at[1] + dz) & 3))

        return pl.BlockSpec((VOC, 256), index)

    return pl.pallas_call(
        hidden_body,
        grid_spec=pltpu.PrefetchScalarGridSpec(
            num_scalar_prefetch=1,
            grid=(4,),
            in_specs=[whole((TILE, ROWS)), whole((VOC - TILE, ROWS)), whole((8, ROWS))] + [weight(k) for k in range(4)],
            out_specs=[
                pl.BlockSpec((1, 4, HALF, 256), lambda i, at: (i, 0, 0, 0)),
                pl.BlockSpec((2, 1, HALF, 256), lambda i, at: (0, i, 0, 0)),
                pl.BlockSpec((2, 1, HALF, 256), lambda i, at: (0, i, 0, 0)),
                whole((VOC, ROWS)),
            ],
            scratch_shapes=[pltpu.VMEM((ROWS, VOC), BF)],
        ),
        out_shape=[
            jax.ShapeDtypeStruct((4, 4, HALF, 256), F32),
            jax.ShapeDtypeStruct((2, 4, HALF, 256), BF),
            jax.ShapeDtypeStruct((2, 4, HALF, 256), BF),
            jax.ShapeDtypeStruct((VOC, ROWS), BF),
        ],
        compiler_params=params(),
        cost_estimate=SMALL,
        name="hidden",
    )(at, e0, e1, pack, emb, emb, emb, emb)


def add(*xs):
    return sum(x.astype(F32) for x in xs)


def scatter(keep, recv, c):
    b = [add(keep[d], recv[d // 2][d % 2]) for d in range(4)]
    n = HALF // 2
    r1 = cross(b[2][:, :n].astype(BF), 0, 3)
    r3 = cross(b[2][:, n:].astype(BF), 0, 1)
    s1 = jnp.concatenate([add(b[1][:, :n], r1).astype(BF), b[1][:, n:].astype(BF)], axis=1)
    s3 = jnp.concatenate([b[3][:, :n].astype(BF), add(b[3][:, n:], r3).astype(BF)], axis=1)
    t = add(b[0], cross(s1, 0, 3), cross(s3, 0, 1))
    u = [cross(t[d].astype(BF), 1, 4 - d) for d in (1, 2, 3)]
    f = add(t[0], *u)
    low, high = f[:, :128], f[:, 128:]
    mine, other = jnp.where(c == 0, low, high), jnp.where(c == 0, high, low)
    got = sibling(other)
    return jnp.where(c == 0, jnp.concatenate([mine, got]), jnp.concatenate([got, mine]))


def quarter_copies(at, feats, offsets, q, sem):
    copies = []
    for n, d in enumerate(offsets):
        group = (at[3] + d) & 3
        for k in range(8):
            dst = q.at[pl.ds(n * ROWS, ROWS), pl.ds(k * 128, 128)]
            copies.append(pltpu.make_async_copy(feats.at[group, k // 2, k % 2], dst, sem.at[n * 8 + k]))
    return copies


def embed_a_body(at, tgt, ep0, ep1, em0, em1, pack_p, pack_m, feats, acc, q, sem):
    i = pl.program_id(0)

    @pl.when(i == 0)
    def _():
        copies = quarter_copies(at, feats, (0, 1, 3), q, sem)
        for copy in copies:
            copy.start()
        for copy in copies:
            copy.wait()

    parts = [tgt[...]]
    for e, pack in ((pick(i, ep0, ep1), pack_p), (pick(i, em0, em1), pack_m)):
        parts.append(token_grad(e, pack, pack[pl.ds(i, 1), :], i * TILE))
    acc[...] = dot_nn(jnp.concatenate(parts, axis=1), q[...])


def embed_a_call(at, tgt, ep0, ep1, em0, em1, pack_p, pack_m, feats):
    tile = pl.BlockSpec((TILE, ROWS), lambda i, at: (i, 0))
    pack = pl.BlockSpec((8, ROWS), lambda i, at: (0, 0))
    return pl.pallas_call(
        embed_a_body,
        grid_spec=pltpu.PrefetchScalarGridSpec(
            num_scalar_prefetch=1,
            grid=(TILES,),
            in_specs=[tile, LOW, HIGH, LOW, HIGH, pack, pack, HBM],
            out_specs=pl.BlockSpec((TILE, 1024), lambda i, at: (i, 0)),
            scratch_shapes=[pltpu.VMEM((3 * ROWS, 1024), BF), pltpu.SemaphoreType.DMA((24,))],
        ),
        out_shape=jax.ShapeDtypeStruct((VOC, 1024), F32),
        compiler_params=params(),
        cost_estimate=SMALL,
        name="embed_a",
    )(at, tgt, ep0, ep1, em0, em1, pack_p, pack_m, feats)


def embed_b_body(at, acc, ea, eb, ec, pack_d, feats, out, q, sem):
    i = pl.program_id(0)

    @pl.when(i == 0)
    def _():
        copies = quarter_copies(at, feats, (2,), q, sem)
        for copy in copies:
            copy.start()
        for copy in copies:
            copy.wait()

    g = token_grad(jnp.where(i == 0, ea[...], jnp.where(i == 1, eb[...], ec[...])), pack_d, pack_d[pl.ds(i, 1), :], i * TILE)
    out[...] = (acc[...] + dot_nn(g, q[...])).astype(BF)


def embed_b_call(at, acc, ea, eb, ec, pack_d, feats):
    tile = pl.BlockSpec((TILE, 1024), lambda i, at: (i, 0))
    return pl.pallas_call(
        embed_b_body,
        grid_spec=pltpu.PrefetchScalarGridSpec(
            num_scalar_prefetch=1,
            grid=(TILES,),
            in_specs=[
                tile,
                LOW,
                LOW,
                pl.BlockSpec((TILE, ROWS), lambda i, at: (jnp.maximum(i - 2, 0), 0)),
                pl.BlockSpec((8, ROWS), lambda i, at: (0, 0)),
                HBM,
            ],
            out_specs=tile,
            scratch_shapes=[pltpu.VMEM((ROWS, 1024), BF), pltpu.SemaphoreType.DMA((8,))],
        ),
        out_shape=jax.ShapeDtypeStruct((VOC, 1024), BF),
        compiler_params=params(),
        cost_estimate=SMALL,
        name="embed_b",
    )(at, acc, ea, eb, ec, pack_d, feats)


def local(comp_hidden, embed, mix, targets, weight):
    x, z, c, y = (lax.axis_index(a).astype(jnp.int32) for a in ("x", "z", "c", "y"))
    at = jnp.stack([x, z, c, y])
    own = comp_hidden.reshape(ROWS, 128)
    tid = jnp.tile(targets - ((x * 4 + z) * 2 + c) * VOC, 4).reshape(1, ROWS)

    swap = [(a * 4 + b, b * 4 + a) for a in range(4) for b in range(4)]
    turned = lax.ppermute(own, ("x", "y"), swap)

    low, high = own[:HALF], own[HALF:]
    mine, other = jnp.where(c == 0, low, high), jnp.where(c == 0, high, low)
    got = sibling(other)
    block = jnp.where(c == 0, jnp.concatenate([mine, got], axis=1), jnp.concatenate([got, mine], axis=1))
    pieces = gather_pieces(block)
    pieces = pieces + [sibling(p) for p in pieces]
    feats = lax.all_gather(turned, ("x", "z", "c")).reshape(4, 4, 2, ROWS, 128)

    e0, e1, st, loc = logits_call(at, pieces, tid, embed, "logits")
    ep0, em0 = shift(e0, "y", 1), shift(e0, "y", 3)
    ep1, em1 = shift(e1, "y", 1), shift(e1, "y", 3)

    s = merge_call(loc, *(shift(loc, "x", d) for d in (1, 2, 3)))
    s = merge_call(s, *(shift(s, "z", d) for d in (1, 2, 3)))
    pack, grad_mix = finish_call(s, sibling(s), st, tid, mix, weight.reshape(1, 128), feats, ep0, em0)
    pack_p, pack_m, pack_d = shift(pack, "y", 1), shift(pack, "y", 3), shift(pack, "y", 2)

    keep, send0, send1, tgt = hidden_call(at, e0, e1, pack, embed)
    recv0, recv1, ep1, em1 = gate(sibling(send0), sibling(send1), ep1, em1)
    diag = [shift(ep0, "y", 1), shift(ep1[:TILE], "y", 1), shift(em1[TILE:], "y", 3)]
    grad_hidden = scatter(keep, (recv0, recv1), c)

    acc = embed_a_call(at, tgt, ep0, ep1, em0, em1, pack_p, pack_m, feats)
    grad_embed = embed_b_call(at, acc, *diag, pack_d, feats)
    return grad_hidden.reshape(4, 128, 128), grad_embed, grad_mix


def solution(mesh):
    fine = Mesh(mesh.devices.reshape(4, 4, 2, 4), ("x", "z", "c", "y"))
    v = ("x", "z", "c")
    return jax.shard_map(
        local,
        mesh=fine,
        in_specs=(P(None, "y", v), P(v, None), P(None, "y"), P("y"), P("y")),
        out_specs=(P(None, "y", v), P(v, "y"), P(None, "y")),
        check_vma=False,
    )
```

```python
import functools

import jax
import jax.numpy as jnp
from jax import lax
from jax.experimental import pallas as pl
from jax.experimental.pallas import tpu as pltpu
from jax.sharding import Mesh, PartitionSpec as P

BF, F32 = jnp.bfloat16, jnp.float32
ROWS = 512
HALF = 256
WIDTH = 4096
VOC = 2048
TILE = 512
TILES = VOC // TILE
VMEM = 56 * 2**20


def shift(a, axis, d):
    return lax.ppermute(a, axis, [((i + d) % 4, i) for i in range(4)])


def sibling(a):
    return lax.ppermute(a, "c", [(0, 1), (1, 0)])


def cross(a, which, d):
    pairs = []
    for x in range(4):
        for z in range(4):
            for c in range(2):
                along_x = (c + which) % 2 == 0
                sx, sz = ((x + d) % 4, z) if along_x else (x, (z + d) % 4)
                pairs.append(((sx * 4 + sz) * 2 + c, (x * 4 + z) * 2 + c))
    return lax.ppermute(a, ("x", "z", "c"), pairs)


def dot_nt(a, b):
    return lax.dot_general(a, b, (((1,), (1,)), ((), ())), preferred_element_type=F32)


def dot_nn(a, b):
    return lax.dot_general(a, b, (((1,), (0,)), ((), ())), preferred_element_type=F32)


def params(**kw):
    return pltpu.CompilerParams(vmem_limit_bytes=VMEM, **kw)


SMALL = pl.CostEstimate(flops=1000, bytes_accessed=1000, transcendentals=0)
HBM = pl.BlockSpec(memory_space=pltpu.HBM)


def gate_body(*refs):
    pass


def gate(*arrays):
    n = len(arrays)
    return pl.pallas_call(
        gate_body,
        in_specs=[HBM] * n,
        out_specs=[HBM] * n,
        out_shape=[jax.ShapeDtypeStruct(a.shape, a.dtype) for a in arrays],
        input_output_aliases={i: i for i in range(n)},
        compiler_params=params(),
        cost_estimate=SMALL,
        name="gate",
    )(*arrays)


CUT = 768
SUB = 256


def sub_specs():
    low = [pl.BlockSpec((SUB, ROWS), lambda i, at, k=k: (jnp.minimum(2 * i + k, CUT // SUB - 1), 0)) for k in (0, 1)]
    high = [pl.BlockSpec((SUB, ROWS), lambda i, at, k=k: (jnp.maximum(2 * i + k - CUT // SUB, 0), 0)) for k in (0, 1)]
    return low + high


def pick(i, low0, low1, high0, high1):
    n = CUT // SUB
    return jnp.concatenate(
        [jnp.where(2 * i < n, low0[...], high0[...]), jnp.where(2 * i + 1 < n, low1[...], high1[...])], axis=0
    )


def gather_pieces(block):
    s = jnp.stack([block] + [cross(block, 0, d) for d in (1, 2, 3)])
    p, m = cross(s, 1, 1), cross(s, 1, 3)
    dp, dm = cross(p[:2], 1, 1), cross(m[2:], 1, 3)
    return [s, p, m, dp, dm]


PLACES = [
    [(a, 0) for a in range(4)],
    [(a, 1) for a in range(4)],
    [(a, 3) for a in range(4)],
    [(0, 2), (1, 2)],
    [(2, 2), (3, 2)],
]


def logits_body(at, *refs):
    pieces, refs = refs[:10], refs[10:]
    tid, emb, _, e0_out, e1_out, st_out, loc_out, _, full, sem = refs
    step = pl.program_id(0)
    x, z, c = at[0], at[1], at[2]

    @pl.when(step == 0)
    def _():
        copies = []
        for n in range(10):
            core = c if n < 5 else 1 - c
            row = pl.multiple_of(core * HALF, HALF)
            for b, (o1, o2) in enumerate(PLACES[n % 5]):
                dx = jnp.where(core == 0, o1, o2)
                dz = jnp.where(core == 0, o2, o1)
                col = pl.multiple_of((((x + dx) & 3) * 4 + ((z + dz) & 3)) * 256, 256)
                copies.append((pieces[n].at[b], full.at[pl.ds(row, HALF), pl.ds(col, 256)], sem.at[len(copies)]))
        for copy in copies:
            pltpu.make_async_copy(*copy).start()
        for copy in copies:
            pltpu.make_async_copy(*copy).wait()
        st_out[...] = jnp.zeros((8, ROWS), F32)
        loc_out[...] = jnp.zeros((8, ROWS), F32)

    logits = dot_nt(emb[...], full[...])
    top = jnp.max(logits, axis=0, keepdims=True)
    ids = lax.broadcasted_iota(jnp.int32, logits.shape, 0) + step * TILE
    hit = jnp.sum(jnp.where(ids == tid[...], logits, 0.0), axis=0, keepdims=True)
    e = jnp.exp(logits - top)
    total = jnp.sum(e, axis=0, keepdims=True)
    e = e.astype(BF)

    for s in range(TILES):

        @pl.when(step == s)
        def _():
            st_out[pl.ds(s, 1), :] = top
            for k in (0, 1):
                row = s * TILE + k * SUB
                ref, row = (e0_out, row) if row < CUT else (e1_out, row - CUT)
                ref[pl.ds(row, SUB), :] = e[k * SUB : (k + 1) * SUB]

    @pl.when(step == 0)
    def _():
        loc_out[pl.ds(0, 1), :] = top
        loc_out[pl.ds(1, 1), :] = total
        loc_out[pl.ds(2, 1), :] = hit

    @pl.when(step > 0)
    def _():
        old = loc_out[pl.ds(0, 1), :]
        new = jnp.maximum(old, top)
        loc_out[pl.ds(1, 1), :] = loc_out[pl.ds(1, 1), :] * jnp.exp(old - new) + total * jnp.exp(top - new)
        loc_out[pl.ds(0, 1), :] = new
        loc_out[pl.ds(2, 1), :] = loc_out[pl.ds(2, 1), :] + hit


def logits_call(at, pieces, tid, emb, later):
    whole = pl.BlockSpec((8, ROWS), lambda i, at: (0, 0))
    return pl.pallas_call(
        logits_body,
        grid_spec=pltpu.PrefetchScalarGridSpec(
            num_scalar_prefetch=1,
            grid=(TILES,),
            in_specs=[HBM] * 10
            + [pl.BlockSpec((1, ROWS), lambda i, at: (0, 0)), pl.BlockSpec((TILE, WIDTH), lambda i, at: (i, 0)), HBM],
            out_specs=[
                pl.BlockSpec((CUT, ROWS), lambda i, at: (0, 0)),
                pl.BlockSpec((VOC - CUT, ROWS), lambda i, at: (0, 0)),
                whole,
                whole,
                HBM,
            ],
            scratch_shapes=[pltpu.VMEM((ROWS, WIDTH), BF), pltpu.SemaphoreType.DMA((32,))],
        ),
        out_shape=[
            jax.ShapeDtypeStruct((CUT, ROWS), BF),
            jax.ShapeDtypeStruct((VOC - CUT, ROWS), BF),
            jax.ShapeDtypeStruct((8, ROWS), F32),
            jax.ShapeDtypeStruct((8, ROWS), F32),
            jax.ShapeDtypeStruct(later.shape, later.dtype),
        ],
        input_output_aliases={13: 4},
        compiler_params=params(),
        cost_estimate=SMALL,
        name="logits",
    )(at, *pieces, tid, emb, later)


def merge(parts):
    top = functools.reduce(jnp.maximum, [p[0:1] for p in parts])
    total = sum(p[1:2] * jnp.exp(p[0:1] - top) for p in parts)
    hit = sum(p[2:3] for p in parts)
    return top, total, hit


def merge_body(*refs):
    top, total, hit = merge([r[...] for r in refs[:-1]])
    out = refs[-1]
    out[...] = jnp.zeros((8, ROWS), F32)
    out[pl.ds(0, 1), :] = top
    out[pl.ds(1, 1), :] = total
    out[pl.ds(2, 1), :] = hit


def merge_call(*parts):
    return pl.pallas_call(
        merge_body,
        out_shape=jax.ShapeDtypeStruct((8, ROWS), F32),
        compiler_params=params(),
        cost_estimate=SMALL,
        name="merge",
    )(*parts)


def finish_body(a, b, st, tid, mix, weight, ep0, em0, e1, pack, grad_mix, e1_out):
    top, total, hit = merge([a[...], b[...]])
    lse = top + jnp.log(total)
    gap = hit - lse
    mixes = [mix[pl.ds(k, 1), :] for k in range(4)]
    big = functools.reduce(jnp.maximum, mixes)
    norm = big + jnp.log(sum(jnp.exp(m - big) for m in mixes))
    logm = [m - norm for m in mixes]
    score = [logm[k] + gap[:, k * 128 : (k + 1) * 128] for k in range(4)]
    big = functools.reduce(jnp.maximum, score)
    ex = [jnp.exp(s - big) for s in score]
    den = sum(ex)
    w = weight[...]
    scaled = []
    for k in range(4):
        resp = ex[k] / den
        grad_mix[pl.ds(k, 1), :] = w * (jnp.exp(logm[k]) - resp)
        scaled.append(w * resp)
    d = jnp.concatenate(scaled, axis=1)
    pack[...] = jnp.zeros((8, ROWS), F32)
    pack[pl.ds(0, TILES), :] = jnp.exp(st[pl.ds(0, TILES), :] - lse) * d
    pack[pl.ds(4, 1), :] = d
    pack[pl.ds(5, 1), :] = lse
    pack[pl.ds(6, 1), :] = tid[...].astype(F32)


def finish_call(a, b, st, tid, mix, weight, *awaited):
    return pl.pallas_call(
        finish_body,
        in_specs=[pl.BlockSpec(memory_space=pltpu.VMEM)] * 6 + [HBM] * 3,
        out_specs=[pl.BlockSpec(memory_space=pltpu.VMEM)] * 2 + [HBM],
        out_shape=[
            jax.ShapeDtypeStruct((8, ROWS), F32),
            jax.ShapeDtypeStruct((4, 128), F32),
            jax.ShapeDtypeStruct((VOC - CUT, ROWS), BF),
        ],
        input_output_aliases={8: 2},
        compiler_params=params(),
        cost_estimate=SMALL,
        name="finish",
    )(a, b, st, tid, mix, weight, *awaited)


def token_grad(e, pack, scale, base):
    ids = lax.broadcasted_iota(jnp.int32, e.shape, 0) + base
    tid = pack[pl.ds(6, 1), :].astype(jnp.int32)
    g = e.astype(F32) * scale
    return (g - jnp.where(ids == tid, pack[pl.ds(4, 1), :], 0.0)).astype(BF)


def hidden_body(at, e0, e1, pack, w0, w1, w2, w3, keep, send0, send1, tgt_out, tg):
    @pl.when(pl.program_id(0) == 0)
    def _():
        for t in range(VOC // SUB):
            rows = pl.ds(t * SUB, SUB)
            e = e0[rows, :] if t * SUB < CUT else e1[pl.ds(t * SUB - CUT, SUB), :]
            g = token_grad(e, pack, pack[pl.ds(t * SUB // TILE, 1), :], t * SUB)
            tgt_out[rows, :] = g
            tg[:, rows] = g.T

    w = jnp.concatenate([w0[...], w1[...], w2[...], w3[...]], axis=1)
    r = dot_nn(tg[...], w)
    first = at[2] == 0
    for k in range(4):
        cols = slice(k * 256, (k + 1) * 256)
        a, b = r[:HALF, cols], r[HALF:, cols]
        keep[0, k] = jnp.where(first, a, b)
        (send0, send1)[k // 2][k % 2, 0] = jnp.where(first, b, a).astype(BF)


def hidden_call(at, e0, e1, pack, emb):
    whole = lambda s: pl.BlockSpec(s, lambda i, at: (0,) * len(s))

    def weight(k):
        def index(i, at):
            dx = jnp.where(at[2] == 0, i, k)
            dz = jnp.where(at[2] == 0, k, i)
            return (0, ((at[0] + dx) & 3) * 4 + ((at[1] + dz) & 3))

        return pl.BlockSpec((VOC, 256), index)

    return pl.pallas_call(
        hidden_body,
        grid_spec=pltpu.PrefetchScalarGridSpec(
            num_scalar_prefetch=1,
            grid=(4,),
            in_specs=[whole((CUT, ROWS)), whole((VOC - CUT, ROWS)), whole((8, ROWS))] + [weight(k) for k in range(4)],
            out_specs=[
                pl.BlockSpec((1, 4, HALF, 256), lambda i, at: (i, 0, 0, 0)),
            ]
            + [pl.BlockSpec((2, 1, HALF, 256), lambda i, at: (0, i, 0, 0))] * 2
            + [
                whole((VOC, ROWS)),
            ],
            scratch_shapes=[pltpu.VMEM((ROWS, VOC), BF)],
        ),
        out_shape=[
            jax.ShapeDtypeStruct((4, 4, HALF, 256), F32),
        ]
        + [jax.ShapeDtypeStruct((2, 4, HALF, 256), BF)] * 2
        + [jax.ShapeDtypeStruct((VOC, ROWS), BF)],
        compiler_params=params(),
        cost_estimate=SMALL,
        name="hidden",
    )(at, e0, e1, pack, emb, emb, emb, emb)


def add(*xs):
    return sum(x.astype(F32) for x in xs)


def scatter(keep, recv, c):
    b = [add(keep[d], recv[d // 2][d % 2]) for d in range(4)]
    n = HALF // 2
    r1 = cross(b[2][:, :n].astype(BF), 0, 3)
    r3 = cross(b[2][:, n:].astype(BF), 0, 1)
    s1 = jnp.concatenate([add(b[1][:, :n], r1).astype(BF), b[1][:, n:].astype(BF)], axis=1)
    s3 = jnp.concatenate([b[3][:, :n].astype(BF), add(b[3][:, n:], r3).astype(BF)], axis=1)
    t = add(b[0], cross(s1, 0, 3), cross(s3, 0, 1))
    u = [cross(t[d].astype(BF), 1, 4 - d) for d in (1, 2, 3)]
    f = add(t[0], *u)
    low, high = f[:, :128], f[:, 128:]
    mine, other = jnp.where(c == 0, low, high), jnp.where(c == 0, high, low)
    got = sibling(other)
    return jnp.where(c == 0, jnp.concatenate([mine, got]), jnp.concatenate([got, mine]))


def quarter_copies(at, feats, offsets, q, sem):
    copies = []
    for n, d in enumerate(offsets):
        group = (at[3] + d) & 3
        for k in range(8):
            dst = q.at[pl.ds(n * ROWS, ROWS), pl.ds(k * 128, 128)]
            copies.append(pltpu.make_async_copy(feats.at[group, k // 2, k % 2], dst, sem.at[n * 8 + k]))
    return copies


def embed_a_body(at, tgt, *refs):
    ep, em, (pack_p, pack_m, feats, acc, q, sem) = refs[:4], refs[4:8], refs[8:]
    i = pl.program_id(0)

    @pl.when(i == 0)
    def _():
        copies = quarter_copies(at, feats, (0, 1, 3), q, sem)
        for copy in copies:
            copy.start()
        for copy in copies:
            copy.wait()

    parts = [tgt[...]]
    for e, pack in ((pick(i, *ep), pack_p), (pick(i, *em), pack_m)):
        parts.append(token_grad(e, pack, pack[pl.ds(i, 1), :], i * TILE))
    acc[...] = dot_nn(jnp.concatenate(parts, axis=1), q[...])


def embed_a_call(at, tgt, ep0, ep1, em0, em1, pack_p, pack_m, feats):
    tile = pl.BlockSpec((TILE, ROWS), lambda i, at: (i, 0))
    pack = pl.BlockSpec((8, ROWS), lambda i, at: (0, 0))
    return pl.pallas_call(
        embed_a_body,
        grid_spec=pltpu.PrefetchScalarGridSpec(
            num_scalar_prefetch=1,
            grid=(TILES,),
            in_specs=[tile, *sub_specs(), *sub_specs(), pack, pack, HBM],
            out_specs=pl.BlockSpec((TILE, 1024), lambda i, at: (i, 0)),
            scratch_shapes=[pltpu.VMEM((3 * ROWS, 1024), BF), pltpu.SemaphoreType.DMA((24,))],
        ),
        out_shape=jax.ShapeDtypeStruct((VOC, 1024), F32),
        compiler_params=params(),
        cost_estimate=SMALL,
        name="embed_a",
    )(at, tgt, ep0, ep0, ep1, ep1, em0, em0, em1, em1, pack_p, pack_m, feats)


def embed_b_body(at, acc, ea0, ea1, eb0, eb1, pack_d, feats, out, q, sem):
    i = pl.program_id(0)

    @pl.when(i == 0)
    def _():
        copies = quarter_copies(at, feats, (2,), q, sem)
        for copy in copies:
            copy.start()
        for copy in copies:
            copy.wait()

    g = token_grad(pick(i, ea0, ea1, eb0, eb1), pack_d, pack_d[pl.ds(i, 1), :], i * TILE)
    out[...] = (acc[...] + dot_nn(g, q[...])).astype(BF)


def embed_b_call(at, acc, ea, eb, pack_d, feats):
    tile = pl.BlockSpec((TILE, 1024), lambda i, at: (i, 0))
    return pl.pallas_call(
        embed_b_body,
        grid_spec=pltpu.PrefetchScalarGridSpec(
            num_scalar_prefetch=1,
            grid=(TILES,),
            in_specs=[
                tile,
                *sub_specs(),
                pl.BlockSpec((8, ROWS), lambda i, at: (0, 0)),
                HBM,
            ],
            out_specs=tile,
            scratch_shapes=[pltpu.VMEM((ROWS, 1024), BF), pltpu.SemaphoreType.DMA((8,))],
        ),
        out_shape=jax.ShapeDtypeStruct((VOC, 1024), BF),
        compiler_params=params(),
        cost_estimate=SMALL,
        name="embed_b",
    )(at, acc, ea, ea, eb, eb, pack_d, feats)


def local(comp_hidden, embed, mix, targets, weight):
    x, z, c, y = (lax.axis_index(a).astype(jnp.int32) for a in ("x", "z", "c", "y"))
    at = jnp.stack([x, z, c, y])
    own = comp_hidden.reshape(ROWS, 128)
    tid = jnp.tile(targets - ((x * 4 + z) * 2 + c) * VOC, 4).reshape(1, ROWS)

    swap = [(a * 4 + b, b * 4 + a) for a in range(4) for b in range(4)]
    turned = lax.ppermute(own, ("x", "y"), swap)

    low, high = own[:HALF], own[HALF:]
    mine, other = jnp.where(c == 0, low, high), jnp.where(c == 0, high, low)
    got = sibling(other)
    block = jnp.where(c == 0, jnp.concatenate([mine, got], axis=1), jnp.concatenate([got, mine], axis=1))
    pieces = gather_pieces(block)
    pieces = pieces + [sibling(p) for p in pieces]

    e0, e1, st, loc, turned = logits_call(at, pieces, tid, embed, turned)
    feats = lax.all_gather(turned, ("x", "z", "c")).reshape(4, 4, 2, ROWS, 128)
    ep0, em0 = shift(e0, "y", 1), shift(e0, "y", 3)

    s = merge_call(loc, *(shift(loc, "x", d) for d in (1, 2, 3)))
    s = merge_call(s, *(shift(s, "z", d) for d in (1, 2, 3)))
    pack, grad_mix, e1 = finish_call(s, sibling(s), st, tid, mix, weight.reshape(1, 128), ep0, em0, e1)
    pack, pack_p, pack_m, pack_d, e1 = gate(pack, shift(pack, "y", 1), shift(pack, "y", 3), shift(pack, "y", 2), e1)
    ep1, em1 = shift(e1, "y", 1), shift(e1, "y", 3)

    keep, *send, tgt = hidden_call(at, e0, e1, pack, embed)
    *recv, ep1, em1, feats = gate(*(sibling(t) for t in send), ep1, em1, feats)
    diag = shift(ep0, "y", 1), shift(em1, "y", 3)
    grad_hidden = scatter(keep, recv, c)

    acc = embed_a_call(at, tgt, ep0, ep1, em0, em1, pack_p, pack_m, feats)
    grad_embed = embed_b_call(at, acc, *diag, pack_d, feats)
    return grad_hidden.reshape(4, 128, 128), grad_embed, grad_mix


def solution(mesh):
    fine = Mesh(mesh.devices.reshape(4, 4, 2, 4), ("x", "z", "c", "y"))
    v = ("x", "z", "c")
    return jax.shard_map(
        local,
        mesh=fine,
        in_specs=(P(None, "y", v), P(v, None), P(None, "y"), P("y"), P("y")),
        out_specs=(P(None, "y", v), P(v, "y"), P(None, "y")),
        check_vma=False,
    )
```

```python
import functools

import jax
import jax.numpy as jnp
from jax import lax
from jax.experimental import pallas as pl
from jax.experimental.pallas import tpu as pltpu
from jax.sharding import Mesh, PartitionSpec as P

BF, F32 = jnp.bfloat16, jnp.float32
ROWS = 512
HALF = 256
WIDTH = 4096
VOC = 2048
TILE = 512
TILES = VOC // TILE
VMEM = 56 * 2**20


def shift(a, axis, d):
    return lax.ppermute(a, axis, [((i + d) % 4, i) for i in range(4)])


def sibling(a):
    return lax.ppermute(a, "c", [(0, 1), (1, 0)])


def cross(a, which, d):
    pairs = []
    for x in range(4):
        for z in range(4):
            for c in range(2):
                along_x = (c + which) % 2 == 0
                sx, sz = ((x + d) % 4, z) if along_x else (x, (z + d) % 4)
                pairs.append(((sx * 4 + sz) * 2 + c, (x * 4 + z) * 2 + c))
    return lax.ppermute(a, ("x", "z", "c"), pairs)


def dot_nt(a, b):
    return lax.dot_general(a, b, (((1,), (1,)), ((), ())), preferred_element_type=F32)


def dot_nn(a, b):
    return lax.dot_general(a, b, (((1,), (0,)), ((), ())), preferred_element_type=F32)


def params(**kw):
    return pltpu.CompilerParams(vmem_limit_bytes=VMEM, **kw)


SMALL = pl.CostEstimate(flops=1000, bytes_accessed=1000, transcendentals=0)
HBM = pl.BlockSpec(memory_space=pltpu.HBM)


def gate_body(*refs):
    pass


def gate(*arrays):
    n = len(arrays)
    return pl.pallas_call(
        gate_body,
        in_specs=[HBM] * n,
        out_specs=[HBM] * n,
        out_shape=[jax.ShapeDtypeStruct(a.shape, a.dtype) for a in arrays],
        input_output_aliases={i: i for i in range(n)},
        compiler_params=params(),
        cost_estimate=SMALL,
        name="gate",
    )(*arrays)


CUT = 1024
SUB = 256


def sub_specs():
    low = [pl.BlockSpec((SUB, ROWS), lambda i, at, k=k: (jnp.minimum(2 * i + k, CUT // SUB - 1), 0)) for k in (0, 1)]
    high = [pl.BlockSpec((SUB, ROWS), lambda i, at, k=k: (jnp.maximum(2 * i + k - CUT // SUB, 0), 0)) for k in (0, 1)]
    return low + high


def pick(i, low0, low1, high0, high1):
    n = CUT // SUB
    return jnp.concatenate(
        [jnp.where(2 * i < n, low0[...], high0[...]), jnp.where(2 * i + 1 < n, low1[...], high1[...])], axis=0
    )


def gather_pieces(block):
    s = jnp.stack([block] + [cross(block, 0, d) for d in (1, 2, 3)])
    return [s] + [cross(s, 1, d) for d in (1, 2, 3)]


def logits_body(at, *refs):
    pieces, refs = refs[:8], refs[8:]
    tid, emb, _, e0_out, e1_out, st_out, loc_out, _, full, sem = refs
    step = pl.program_id(0)
    x, z, c = at[0], at[1], at[2]

    @pl.when(step == 0)
    def _():
        copies = []
        for n in range(8):
            core = c if n < 4 else 1 - c
            row = pl.multiple_of(core * HALF, HALF)
            for b in range(4):
                dx = jnp.where(core == 0, b, n % 4)
                dz = jnp.where(core == 0, n % 4, b)
                col = pl.multiple_of((((x + dx) & 3) * 4 + ((z + dz) & 3)) * 256, 256)
                copies.append((pieces[n].at[b], full.at[pl.ds(row, HALF), pl.ds(col, 256)], sem.at[len(copies)]))
        for copy in copies:
            pltpu.make_async_copy(*copy).start()
        for copy in copies:
            pltpu.make_async_copy(*copy).wait()
        st_out[...] = jnp.zeros((8, ROWS), F32)
        loc_out[...] = jnp.zeros((8, ROWS), F32)

    logits = dot_nt(emb[...], full[...])
    top = jnp.max(logits, axis=0, keepdims=True)
    ids = lax.broadcasted_iota(jnp.int32, logits.shape, 0) + step * TILE
    hit = jnp.sum(jnp.where(ids == tid[...], logits, 0.0), axis=0, keepdims=True)
    e = jnp.exp(logits - top)
    total = jnp.sum(e, axis=0, keepdims=True)
    e = e.astype(BF)

    for s in range(TILES):

        @pl.when(step == s)
        def _():
            st_out[pl.ds(s, 1), :] = top
            for k in (0, 1):
                row = s * TILE + k * SUB
                ref, row = (e0_out, row) if row < CUT else (e1_out, row - CUT)
                ref[pl.ds(row, SUB), :] = e[k * SUB : (k + 1) * SUB]

    @pl.when(step == 0)
    def _():
        loc_out[pl.ds(0, 1), :] = top
        loc_out[pl.ds(1, 1), :] = total
        loc_out[pl.ds(2, 1), :] = hit

    @pl.when(step > 0)
    def _():
        old = loc_out[pl.ds(0, 1), :]
        new = jnp.maximum(old, top)
        loc_out[pl.ds(1, 1), :] = loc_out[pl.ds(1, 1), :] * jnp.exp(old - new) + total * jnp.exp(top - new)
        loc_out[pl.ds(0, 1), :] = new
        loc_out[pl.ds(2, 1), :] = loc_out[pl.ds(2, 1), :] + hit


def logits_call(at, pieces, tid, emb, later):
    whole = pl.BlockSpec((8, ROWS), lambda i, at: (0, 0))
    return pl.pallas_call(
        logits_body,
        grid_spec=pltpu.PrefetchScalarGridSpec(
            num_scalar_prefetch=1,
            grid=(TILES,),
            in_specs=[HBM] * 8
            + [pl.BlockSpec((1, ROWS), lambda i, at: (0, 0)), pl.BlockSpec((TILE, WIDTH), lambda i, at: (i, 0)), HBM],
            out_specs=[
                pl.BlockSpec((CUT, ROWS), lambda i, at: (0, 0)),
                pl.BlockSpec((VOC - CUT, ROWS), lambda i, at: (0, 0)),
                whole,
                whole,
                HBM,
            ],
            scratch_shapes=[pltpu.VMEM((ROWS, WIDTH), BF), pltpu.SemaphoreType.DMA((32,))],
        ),
        out_shape=[
            jax.ShapeDtypeStruct((CUT, ROWS), BF),
            jax.ShapeDtypeStruct((VOC - CUT, ROWS), BF),
            jax.ShapeDtypeStruct((8, ROWS), F32),
            jax.ShapeDtypeStruct((8, ROWS), F32),
            jax.ShapeDtypeStruct(later.shape, later.dtype),
        ],
        input_output_aliases={11: 4},
        compiler_params=params(),
        cost_estimate=SMALL,
        name="logits",
    )(at, *pieces, tid, emb, later)


def merge(parts):
    top = functools.reduce(jnp.maximum, [p[0:1] for p in parts])
    total = sum(p[1:2] * jnp.exp(p[0:1] - top) for p in parts)
    hit = sum(p[2:3] for p in parts)
    return top, total, hit


def merge_body(*refs):
    top, total, hit = merge([r[...] for r in refs[:-1]])
    out = refs[-1]
    out[...] = jnp.zeros((8, ROWS), F32)
    out[pl.ds(0, 1), :] = top
    out[pl.ds(1, 1), :] = total
    out[pl.ds(2, 1), :] = hit


def merge_call(*parts):
    return pl.pallas_call(
        merge_body,
        out_shape=jax.ShapeDtypeStruct((8, ROWS), F32),
        compiler_params=params(),
        cost_estimate=SMALL,
        name="merge",
    )(*parts)


def finish_body(a, b, st, tid, mix, weight, ep0, em0, e1, pack, grad_mix, e1_out):
    top, total, hit = merge([a[...], b[...]])
    lse = top + jnp.log(total)
    gap = hit - lse
    mixes = [mix[pl.ds(k, 1), :] for k in range(4)]
    big = functools.reduce(jnp.maximum, mixes)
    norm = big + jnp.log(sum(jnp.exp(m - big) for m in mixes))
    logm = [m - norm for m in mixes]
    score = [logm[k] + gap[:, k * 128 : (k + 1) * 128] for k in range(4)]
    big = functools.reduce(jnp.maximum, score)
    ex = [jnp.exp(s - big) for s in score]
    den = sum(ex)
    w = weight[...]
    scaled = []
    for k in range(4):
        resp = ex[k] / den
        grad_mix[pl.ds(k, 1), :] = w * (jnp.exp(logm[k]) - resp)
        scaled.append(w * resp)
    d = jnp.concatenate(scaled, axis=1)
    pack[...] = jnp.zeros((8, ROWS), F32)
    pack[pl.ds(0, TILES), :] = jnp.exp(st[pl.ds(0, TILES), :] - lse) * d
    pack[pl.ds(4, 1), :] = d
    pack[pl.ds(5, 1), :] = lse
    pack[pl.ds(6, 1), :] = tid[...].astype(F32)


def finish_call(a, b, st, tid, mix, weight, *awaited):
    return pl.pallas_call(
        finish_body,
        in_specs=[pl.BlockSpec(memory_space=pltpu.VMEM)] * 6 + [HBM] * 3,
        out_specs=[pl.BlockSpec(memory_space=pltpu.VMEM)] * 2 + [HBM],
        out_shape=[
            jax.ShapeDtypeStruct((8, ROWS), F32),
            jax.ShapeDtypeStruct((4, 128), F32),
            jax.ShapeDtypeStruct((VOC - CUT, ROWS), BF),
        ],
        input_output_aliases={8: 2},
        compiler_params=params(),
        cost_estimate=SMALL,
        name="finish",
    )(a, b, st, tid, mix, weight, *awaited)


def token_grad(e, pack, scale, base):
    ids = lax.broadcasted_iota(jnp.int32, e.shape, 0) + base
    tid = pack[pl.ds(6, 1), :].astype(jnp.int32)
    g = e.astype(F32) * scale
    return (g - jnp.where(ids == tid, pack[pl.ds(4, 1), :], 0.0)).astype(BF)


def hidden_body(at, e0, e1, pack, w0, w1, w2, w3, keep, send0, send1, tgt_out, tg):
    @pl.when(pl.program_id(0) == 0)
    def _():
        for t in range(VOC // SUB):
            rows = pl.ds(t * SUB, SUB)
            e = e0[rows, :] if t * SUB < CUT else e1[pl.ds(t * SUB - CUT, SUB), :]
            g = token_grad(e, pack, pack[pl.ds(t * SUB // TILE, 1), :], t * SUB)
            tgt_out[rows, :] = g
            tg[:, rows] = g.T

    w = jnp.concatenate([w0[...], w1[...], w2[...], w3[...]], axis=1)
    r = dot_nn(tg[...], w)
    first = at[2] == 0
    for k in range(4):
        cols = slice(k * 256, (k + 1) * 256)
        a, b = r[:HALF, cols], r[HALF:, cols]
        keep[0, k] = jnp.where(first, a, b)
        (send0, send1)[k // 2][k % 2, 0] = jnp.where(first, b, a).astype(BF)


def hidden_call(at, e0, e1, pack, emb):
    whole = lambda s: pl.BlockSpec(s, lambda i, at: (0,) * len(s))

    def weight(k):
        def index(i, at):
            dx = jnp.where(at[2] == 0, i, k)
            dz = jnp.where(at[2] == 0, k, i)
            return (0, ((at[0] + dx) & 3) * 4 + ((at[1] + dz) & 3))

        return pl.BlockSpec((VOC, 256), index)

    return pl.pallas_call(
        hidden_body,
        grid_spec=pltpu.PrefetchScalarGridSpec(
            num_scalar_prefetch=1,
            grid=(4,),
            in_specs=[whole((CUT, ROWS)), whole((VOC - CUT, ROWS)), whole((8, ROWS))] + [weight(k) for k in range(4)],
            out_specs=[
                pl.BlockSpec((1, 4, HALF, 256), lambda i, at: (i, 0, 0, 0)),
            ]
            + [pl.BlockSpec((2, 1, HALF, 256), lambda i, at: (0, i, 0, 0))] * 2
            + [
                whole((VOC, ROWS)),
            ],
            scratch_shapes=[pltpu.VMEM((ROWS, VOC), BF)],
        ),
        out_shape=[
            jax.ShapeDtypeStruct((4, 4, HALF, 256), F32),
        ]
        + [jax.ShapeDtypeStruct((2, 4, HALF, 256), BF)] * 2
        + [jax.ShapeDtypeStruct((VOC, ROWS), BF)],
        compiler_params=params(),
        cost_estimate=SMALL,
        name="hidden",
    )(at, e0, e1, pack, emb, emb, emb, emb)


def add(*xs):
    return sum(x.astype(F32) for x in xs)


def scatter(keep, recv, c, acc):
    b = [add(keep[d], recv[d // 2][d % 2]) for d in range(4)]
    u = [cross(b[d].astype(BF), 0, 4 - d) for d in (1, 2, 3)]
    *u, acc = gate(*u, acc)
    t = add(b[0], *u)
    u = [cross(t[d].astype(BF), 1, 4 - d) for d in (1, 2, 3)]
    f = add(t[0], *u)
    low, high = f[:, :128], f[:, 128:]
    mine, other = jnp.where(c == 0, low, high), jnp.where(c == 0, high, low)
    got = sibling(other)
    return jnp.where(c == 0, jnp.concatenate([mine, got]), jnp.concatenate([got, mine])), acc


def quarter_copies(at, feats, offsets, q, sem):
    copies = []
    for n, d in enumerate(offsets):
        group = (at[3] + d) & 3
        for k in range(8):
            dst = q.at[pl.ds(n * ROWS, ROWS), pl.ds(k * 128, 128)]
            copies.append(pltpu.make_async_copy(feats.at[group, k // 2, k % 2], dst, sem.at[n * 8 + k]))
    return copies


def embed_a_body(at, tgt, *refs):
    ep, em, (pack_p, pack_m, feats, acc, q, sem) = refs[:4], refs[4:8], refs[8:]
    i = pl.program_id(0)

    @pl.when(i == 0)
    def _():
        copies = quarter_copies(at, feats, (0, 1, 3), q, sem)
        for copy in copies:
            copy.start()
        for copy in copies:
            copy.wait()

    parts = [tgt[...]]
    for e, pack in ((pick(i, *ep), pack_p), (pick(i, *em), pack_m)):
        parts.append(token_grad(e, pack, pack[pl.ds(i, 1), :], i * TILE))
    acc[...] = dot_nn(jnp.concatenate(parts, axis=1), q[...])


def embed_a_call(at, tgt, ep0, ep1, em0, em1, pack_p, pack_m, feats):
    tile = pl.BlockSpec((TILE, ROWS), lambda i, at: (i, 0))
    pack = pl.BlockSpec((8, ROWS), lambda i, at: (0, 0))
    return pl.pallas_call(
        embed_a_body,
        grid_spec=pltpu.PrefetchScalarGridSpec(
            num_scalar_prefetch=1,
            grid=(TILES,),
            in_specs=[tile, *sub_specs(), *sub_specs(), pack, pack, HBM],
            out_specs=pl.BlockSpec((TILE, 1024), lambda i, at: (i, 0)),
            scratch_shapes=[pltpu.VMEM((3 * ROWS, 1024), BF), pltpu.SemaphoreType.DMA((24,))],
        ),
        out_shape=jax.ShapeDtypeStruct((VOC, 1024), F32),
        compiler_params=params(),
        cost_estimate=SMALL,
        name="embed_a",
    )(at, tgt, ep0, ep0, ep1, ep1, em0, em0, em1, em1, pack_p, pack_m, feats)


def embed_b_body(at, acc, ea0, ea1, eb0, eb1, pack_d, feats, out, q, sem):
    i = pl.program_id(0)

    @pl.when(i == 0)
    def _():
        copies = quarter_copies(at, feats, (2,), q, sem)
        for copy in copies:
            copy.start()
        for copy in copies:
            copy.wait()

    g = token_grad(pick(i, ea0, ea1, eb0, eb1), pack_d, pack_d[pl.ds(i, 1), :], i * TILE)
    out[...] = (acc[...] + dot_nn(g, q[...])).astype(BF)


def embed_b_call(at, acc, ea, eb, pack_d, feats):
    tile = pl.BlockSpec((TILE, 1024), lambda i, at: (i, 0))
    return pl.pallas_call(
        embed_b_body,
        grid_spec=pltpu.PrefetchScalarGridSpec(
            num_scalar_prefetch=1,
            grid=(TILES,),
            in_specs=[
                tile,
                *sub_specs(),
                pl.BlockSpec((8, ROWS), lambda i, at: (0, 0)),
                HBM,
            ],
            out_specs=tile,
            scratch_shapes=[pltpu.VMEM((ROWS, 1024), BF), pltpu.SemaphoreType.DMA((8,))],
        ),
        out_shape=jax.ShapeDtypeStruct((VOC, 1024), BF),
        compiler_params=params(),
        cost_estimate=SMALL,
        name="embed_b",
    )(at, acc, ea, ea, eb, eb, pack_d, feats)


def local(comp_hidden, embed, mix, targets, weight):
    x, z, c, y = (lax.axis_index(a).astype(jnp.int32) for a in ("x", "z", "c", "y"))
    at = jnp.stack([x, z, c, y])
    own = comp_hidden.reshape(ROWS, 128)
    tid = jnp.tile(targets - ((x * 4 + z) * 2 + c) * VOC, 4).reshape(1, ROWS)

    swap = [(a * 4 + b, b * 4 + a) for a in range(4) for b in range(4)]
    turned = lax.ppermute(own, ("x", "y"), swap)

    low, high = own[:HALF], own[HALF:]
    mine, other = jnp.where(c == 0, low, high), jnp.where(c == 0, high, low)
    got = sibling(other)
    block = jnp.where(c == 0, jnp.concatenate([mine, got], axis=1), jnp.concatenate([got, mine], axis=1))
    pieces = gather_pieces(block)
    pieces = pieces + [sibling(p) for p in pieces]

    e0, e1, st, loc, turned = logits_call(at, pieces, tid, embed, turned)
    feats = lax.all_gather(turned, ("x", "z", "c")).reshape(4, 4, 2, ROWS, 128)
    ep0, em0 = shift(e0, "y", 1), shift(e0, "y", 3)

    s = merge_call(loc, *(shift(loc, "x", d) for d in (1, 2, 3)))
    s = merge_call(s, *(shift(s, "z", d) for d in (1, 2, 3)))
    pack, grad_mix, e1 = finish_call(s, sibling(s), st, tid, mix, weight.reshape(1, 128), ep0, em0, e1)
    ep1, em1 = shift(e1, "y", 1), shift(e1, "y", 3)
    keep, send0, send1, tgt = hidden_call(at, e0, e1, pack, embed)
    send0, send1, pack, ep1, em1 = gate(send0, send1, pack, ep1, em1)
    recv0, recv1, pack_p, pack_m, pack_d, ep0, em1 = gate(
        sibling(send0), sibling(send1), *(shift(pack, "y", d) for d in (1, 3, 2)), ep0, em1
    )
    diag = shift(ep0, "y", 1), shift(em1, "y", 3)

    acc = embed_a_call(at, tgt, ep0, ep1, em0, em1, pack_p, pack_m, feats)
    grad_hidden, acc = scatter(keep, (recv0, recv1), c, acc)
    grad_embed = embed_b_call(at, acc, *diag, pack_d, feats)
    return grad_hidden.reshape(4, 128, 128), grad_embed, grad_mix


def solution(mesh):
    fine = Mesh(mesh.devices.reshape(4, 4, 2, 4), ("x", "z", "c", "y"))
    v = ("x", "z", "c")
    return jax.shard_map(
        local,
        mesh=fine,
        in_specs=(P(None, "y", v), P(v, None), P(None, "y"), P("y"), P("y")),
        out_specs=(P(None, "y", v), P(v, "y"), P(None, "y")),
        check_vma=False,
    )
```

```python
import functools

import jax
import jax.numpy as jnp
from jax import lax
from jax.experimental import pallas as pl
from jax.experimental.pallas import tpu as pltpu
from jax.sharding import Mesh, PartitionSpec as P

BF, F32 = jnp.bfloat16, jnp.float32
ROWS = 512
HALF = 256
WIDTH = 4096
VOC = 2048
TILE = 512
TILES = VOC // TILE
VMEM = 56 * 2**20


def shift(a, axis, d):
    return lax.ppermute(a, axis, [((i + d) % 4, i) for i in range(4)])


def sibling(a):
    return lax.ppermute(a, "c", [(0, 1), (1, 0)])


def cross(a, which, d):
    pairs = []
    for x in range(4):
        for z in range(4):
            for c in range(2):
                along_x = (c + which) % 2 == 0
                sx, sz = ((x + d) % 4, z) if along_x else (x, (z + d) % 4)
                pairs.append(((sx * 4 + sz) * 2 + c, (x * 4 + z) * 2 + c))
    return lax.ppermute(a, ("x", "z", "c"), pairs)


def dot_nt(a, b):
    return lax.dot_general(a, b, (((1,), (1,)), ((), ())), preferred_element_type=F32)


def dot_nn(a, b):
    return lax.dot_general(a, b, (((1,), (0,)), ((), ())), preferred_element_type=F32)


def params(**kw):
    return pltpu.CompilerParams(vmem_limit_bytes=VMEM, **kw)


SMALL = pl.CostEstimate(flops=1000, bytes_accessed=1000, transcendentals=0)
HBM = pl.BlockSpec(memory_space=pltpu.HBM)


def gate_body(*refs):
    pass


def gate(*arrays):
    n = len(arrays)
    return pl.pallas_call(
        gate_body,
        in_specs=[HBM] * n,
        out_specs=[HBM] * n,
        out_shape=[jax.ShapeDtypeStruct(a.shape, a.dtype) for a in arrays],
        input_output_aliases={i: i for i in range(n)},
        compiler_params=params(),
        cost_estimate=SMALL,
        name="gate",
    )(*arrays)


CUT = VOC // 2
SUB = 256


def gather_pieces(block, other):
    *ring, other = gate(*(cross(block, 0, d) for d in (1, 2, 3)), other)
    s = jnp.stack([block, *ring])
    return [s] + [cross(s, 1, d) for d in (1, 2, 3)], other


def logits_body(at, *refs):
    pieces, refs = refs[:8], refs[8:]
    tid, emb, _, e0_out, e1_out, st_out, loc_out, _, full, sem = refs
    step = pl.program_id(0)
    x, z, c = at[0], at[1], at[2]

    @pl.when(step == 0)
    def _():
        copies = []
        for n in range(8):
            core = c if n < 4 else 1 - c
            row = pl.multiple_of(core * HALF, HALF)
            for b in range(4):
                dx = jnp.where(core == 0, b, n % 4)
                dz = jnp.where(core == 0, n % 4, b)
                col = pl.multiple_of((((x + dx) & 3) * 4 + ((z + dz) & 3)) * 256, 256)
                copies.append((pieces[n].at[b], full.at[pl.ds(row, HALF), pl.ds(col, 256)], sem.at[len(copies)]))
        for copy in copies:
            pltpu.make_async_copy(*copy).start()
        for copy in copies:
            pltpu.make_async_copy(*copy).wait()
        st_out[...] = jnp.zeros((8, ROWS), F32)
        loc_out[...] = jnp.zeros((8, ROWS), F32)

    logits = dot_nt(emb[...], full[...])
    top = jnp.max(logits, axis=0, keepdims=True)
    ids = lax.broadcasted_iota(jnp.int32, logits.shape, 0) + step * TILE
    hit = jnp.sum(jnp.where(ids == tid[...], logits, 0.0), axis=0, keepdims=True)
    e = jnp.exp(logits - top)
    total = jnp.sum(e, axis=0, keepdims=True)
    e = e.astype(BF)

    for s in range(TILES):

        @pl.when(step == s)
        def _():
            st_out[pl.ds(s, 1), :] = top
            for k in (0, 1):
                row = s * TILE + k * SUB
                ref, row = (e0_out, row) if row < CUT else (e1_out, row - CUT)
                ref[pl.ds(row, SUB), :] = e[k * SUB : (k + 1) * SUB]

    @pl.when(step == 0)
    def _():
        loc_out[pl.ds(0, 1), :] = top
        loc_out[pl.ds(1, 1), :] = total
        loc_out[pl.ds(2, 1), :] = hit

    @pl.when(step > 0)
    def _():
        old = loc_out[pl.ds(0, 1), :]
        new = jnp.maximum(old, top)
        loc_out[pl.ds(1, 1), :] = loc_out[pl.ds(1, 1), :] * jnp.exp(old - new) + total * jnp.exp(top - new)
        loc_out[pl.ds(0, 1), :] = new
        loc_out[pl.ds(2, 1), :] = loc_out[pl.ds(2, 1), :] + hit


def logits_call(at, pieces, tid, emb, later):
    whole = pl.BlockSpec((8, ROWS), lambda i, at: (0, 0))
    return pl.pallas_call(
        logits_body,
        grid_spec=pltpu.PrefetchScalarGridSpec(
            num_scalar_prefetch=1,
            grid=(TILES,),
            in_specs=[HBM] * 8
            + [pl.BlockSpec((1, ROWS), lambda i, at: (0, 0)), pl.BlockSpec((TILE, WIDTH), lambda i, at: (i, 0)), HBM],
            out_specs=[
                pl.BlockSpec((CUT, ROWS), lambda i, at: (0, 0)),
                pl.BlockSpec((VOC - CUT, ROWS), lambda i, at: (0, 0)),
                whole,
                whole,
                HBM,
            ],
            scratch_shapes=[pltpu.VMEM((ROWS, WIDTH), BF), pltpu.SemaphoreType.DMA((32,))],
        ),
        out_shape=[
            jax.ShapeDtypeStruct((CUT, ROWS), BF),
            jax.ShapeDtypeStruct((VOC - CUT, ROWS), BF),
            jax.ShapeDtypeStruct((8, ROWS), F32),
            jax.ShapeDtypeStruct((8, ROWS), F32),
            jax.ShapeDtypeStruct(later.shape, later.dtype),
        ],
        input_output_aliases={11: 4},
        compiler_params=params(),
        cost_estimate=SMALL,
        name="logits",
    )(at, *pieces, tid, emb, later)


def merge(parts):
    top = functools.reduce(jnp.maximum, [p[0:1] for p in parts])
    total = sum(p[1:2] * jnp.exp(p[0:1] - top) for p in parts)
    hit = sum(p[2:3] for p in parts)
    return top, total, hit


def merge_body(*refs):
    top, total, hit = merge([r[...] for r in refs[:-1]])
    out = refs[-1]
    out[...] = jnp.zeros((8, ROWS), F32)
    out[pl.ds(0, 1), :] = top
    out[pl.ds(1, 1), :] = total
    out[pl.ds(2, 1), :] = hit


def merge_call(*parts):
    return pl.pallas_call(
        merge_body,
        out_shape=jax.ShapeDtypeStruct((8, ROWS), F32),
        compiler_params=params(),
        cost_estimate=SMALL,
        name="merge",
    )(*parts)


def finish_body(a, b, st, tid, mix, weight, ep0, em0, e1, pack, grad_mix, e1_out):
    top, total, hit = merge([a[...], b[...]])
    lse = top + jnp.log(total)
    gap = hit - lse
    mixes = [mix[pl.ds(k, 1), :] for k in range(4)]
    big = functools.reduce(jnp.maximum, mixes)
    norm = big + jnp.log(sum(jnp.exp(m - big) for m in mixes))
    logm = [m - norm for m in mixes]
    score = [logm[k] + gap[:, k * 128 : (k + 1) * 128] for k in range(4)]
    big = functools.reduce(jnp.maximum, score)
    ex = [jnp.exp(s - big) for s in score]
    den = sum(ex)
    w = weight[...]
    scaled = []
    for k in range(4):
        resp = ex[k] / den
        grad_mix[pl.ds(k, 1), :] = w * (jnp.exp(logm[k]) - resp)
        scaled.append(w * resp)
    d = jnp.concatenate(scaled, axis=1)
    pack[...] = jnp.zeros((8, ROWS), F32)
    pack[pl.ds(0, TILES), :] = jnp.exp(st[pl.ds(0, TILES), :] - lse) * d
    pack[pl.ds(4, 1), :] = d
    pack[pl.ds(5, 1), :] = lse
    pack[pl.ds(6, 1), :] = tid[...].astype(F32)


def finish_call(a, b, st, tid, mix, weight, *awaited):
    return pl.pallas_call(
        finish_body,
        in_specs=[pl.BlockSpec(memory_space=pltpu.VMEM)] * 6 + [HBM] * 3,
        out_specs=[pl.BlockSpec(memory_space=pltpu.VMEM)] * 2 + [HBM],
        out_shape=[
            jax.ShapeDtypeStruct((8, ROWS), F32),
            jax.ShapeDtypeStruct((4, 128), F32),
            jax.ShapeDtypeStruct((VOC - CUT, ROWS), BF),
        ],
        input_output_aliases={8: 2},
        compiler_params=params(),
        cost_estimate=SMALL,
        name="finish",
    )(a, b, st, tid, mix, weight, *awaited)


def token_grad(e, pack, scale, base):
    ids = lax.broadcasted_iota(jnp.int32, e.shape, 0) + base
    tid = pack[pl.ds(6, 1), :].astype(jnp.int32)
    g = e.astype(F32) * scale
    return (g - jnp.where(ids == tid, pack[pl.ds(4, 1), :], 0.0)).astype(BF)


def hidden_body(at, e0, e1, pack, w0, w1, w2, w3, keep, send0, send1, tgt_out, tg):
    @pl.when(pl.program_id(0) == 0)
    def _():
        for t in range(VOC // SUB):
            rows = pl.ds(t * SUB, SUB)
            e = e0[rows, :] if t * SUB < CUT else e1[pl.ds(t * SUB - CUT, SUB), :]
            g = token_grad(e, pack, pack[pl.ds(t * SUB // TILE, 1), :], t * SUB)
            tgt_out[rows, :] = g
            tg[:, rows] = g.T

    w = jnp.concatenate([w0[...], w1[...], w2[...], w3[...]], axis=1)
    r = dot_nn(tg[...], w)
    first = at[2] == 0
    for k in range(4):
        cols = slice(k * 256, (k + 1) * 256)
        a, b = r[:HALF, cols], r[HALF:, cols]
        keep[0, k] = jnp.where(first, a, b)
        (send0, send1)[k // 2][k % 2, 0] = jnp.where(first, b, a).astype(BF)


def hidden_call(at, e0, e1, pack, emb):
    whole = lambda s: pl.BlockSpec(s, lambda i, at: (0,) * len(s))

    def weight(k):
        def index(i, at):
            dx = jnp.where(at[2] == 0, i, k)
            dz = jnp.where(at[2] == 0, k, i)
            return (0, ((at[0] + dx) & 3) * 4 + ((at[1] + dz) & 3))

        return pl.BlockSpec((VOC, 256), index)

    return pl.pallas_call(
        hidden_body,
        grid_spec=pltpu.PrefetchScalarGridSpec(
            num_scalar_prefetch=1,
            grid=(4,),
            in_specs=[whole((CUT, ROWS)), whole((VOC - CUT, ROWS)), whole((8, ROWS))] + [weight(k) for k in range(4)],
            out_specs=[
                pl.BlockSpec((1, 4, HALF, 256), lambda i, at: (i, 0, 0, 0)),
            ]
            + [pl.BlockSpec((2, 1, HALF, 256), lambda i, at: (0, i, 0, 0))] * 2
            + [
                whole((VOC, ROWS)),
            ],
            scratch_shapes=[pltpu.VMEM((ROWS, VOC), BF)],
        ),
        out_shape=[
            jax.ShapeDtypeStruct((4, 4, HALF, 256), F32),
        ]
        + [jax.ShapeDtypeStruct((2, 4, HALF, 256), BF)] * 2
        + [jax.ShapeDtypeStruct((VOC, ROWS), BF)],
        compiler_params=params(),
        cost_estimate=SMALL,
        name="hidden",
    )(at, e0, e1, pack, emb, emb, emb, emb)


def add(*xs):
    return sum(x.astype(F32) for x in xs)


def scatter(keep, recv, c, acc):
    b = [add(keep[d], recv[d // 2][d % 2]) for d in range(4)]
    u = [cross(b[d].astype(BF), 0, 4 - d) for d in (1, 2, 3)]
    *u, acc = gate(*u, acc)
    t = add(b[0], *u)
    u = [cross(t[d].astype(BF), 1, 4 - d) for d in (1, 2, 3)]
    f = add(t[0], *u)
    low, high = f[:, :128], f[:, 128:]
    mine, other = jnp.where(c == 0, low, high), jnp.where(c == 0, high, low)
    got = sibling(other)
    return jnp.where(c == 0, jnp.concatenate([mine, got]), jnp.concatenate([got, mine])), acc


def embed_body(base, at, tgt, ep, em, ed, pack_p, pack_m, pack_d, feats, *refs):
    out, q, sem = refs[-3:]
    i = pl.program_id(0)

    def copies(n, d):
        group = (at[3] + d) & 3
        for k in range(8):
            dst = q.at[pl.ds(n * ROWS, ROWS), pl.ds(k * 128, 128)]
            yield pltpu.make_async_copy(feats.at[group, k // 2, k % 2], dst, sem.at[n * 8 + k])

    @pl.when(i == 0)
    def _():
        for n, d in enumerate((0, 1, 3, 2)):
            for copy in copies(n, d):
                copy.start()
        for n, d in enumerate((0, 1, 3, 2)):
            for copy in copies(n, d):
                copy.wait()

    parts = [tgt[...]]
    tile = base // TILE + i
    for e, pack in ((ep, pack_p), (em, pack_m), (ed, pack_d)):
        parts.append(token_grad(e[...], pack, pack[pl.ds(tile, 1), :], tile * TILE))
    out[...] = dot_nn(jnp.concatenate(parts, axis=1), q[...]).astype(BF)


def embed_call(at, base, tgt, ep, em, ed, packs, feats, into, name):
    first = base // TILE
    tile = pl.BlockSpec((TILE, ROWS), lambda i, at: (i, 0))
    pack = pl.BlockSpec((8, ROWS), lambda i, at: (0, 0))
    more = [] if into is None else [into]
    return pl.pallas_call(
        functools.partial(embed_body, base),
        grid_spec=pltpu.PrefetchScalarGridSpec(
            num_scalar_prefetch=1,
            grid=(CUT // TILE,),
            in_specs=[pl.BlockSpec((TILE, ROWS), lambda i, at: (i + first, 0)), tile, tile, tile, pack, pack, pack, HBM]
            + [HBM] * len(more),
            out_specs=pl.BlockSpec((TILE, 1024), lambda i, at: (i + first, 0)),
            scratch_shapes=[pltpu.VMEM((4 * ROWS, 1024), BF), pltpu.SemaphoreType.DMA((32,))],
        ),
        out_shape=jax.ShapeDtypeStruct((VOC, 1024), BF),
        input_output_aliases={9: 0} if more else {},
        compiler_params=params(),
        cost_estimate=SMALL,
        name=name,
    )(at, tgt, ep, em, ed, *packs, feats, *more)


def local(comp_hidden, embed, mix, targets, weight):
    x, z, c, y = (lax.axis_index(a).astype(jnp.int32) for a in ("x", "z", "c", "y"))
    at = jnp.stack([x, z, c, y])
    own = comp_hidden.reshape(ROWS, 128)
    tid = jnp.tile(targets - ((x * 4 + z) * 2 + c) * VOC, 4).reshape(1, ROWS)

    swap = [(a * 4 + b, b * 4 + a) for a in range(4) for b in range(4)]
    turned = lax.ppermute(own, ("x", "y"), swap)

    low, high = own[:HALF], own[HALF:]
    mine, other = jnp.where(c == 0, low, high), jnp.where(c == 0, high, low)
    got = sibling(other)
    block = jnp.where(c == 0, jnp.concatenate([mine, got], axis=1), jnp.concatenate([got, mine], axis=1))
    pieces, turned = gather_pieces(block, turned)
    pieces = pieces + [sibling(p) for p in pieces]

    e0, e1, st, loc, turned = logits_call(at, pieces, tid, embed, turned)
    feats = lax.all_gather(turned, ("x", "z", "c")).reshape(4, 4, 2, ROWS, 128)
    ep0, em0 = shift(e0, "y", 1), shift(e0, "y", 3)

    s = merge_call(loc, *(shift(loc, "x", d) for d in (1, 2, 3)))
    s = merge_call(s, *(shift(s, "z", d) for d in (1, 2, 3)))
    pack, grad_mix, e1 = finish_call(s, sibling(s), st, tid, mix, weight.reshape(1, 128), ep0, em0, e1)
    packs = [shift(pack, "y", d) for d in (1, 3, 2)]
    em1, ed0 = shift(e1, "y", 3), shift(ep0, "y", 1)
    keep, send0, send1, tgt = hidden_call(at, e0, e1, pack, embed)
    send0, send1, e1, em1, ed0, *packs = gate(send0, send1, e1, em1, ed0, *packs)
    ep1, ed1 = shift(e1, "y", 1), shift(em1, "y", 3)
    recv = sibling(send0), sibling(send1)

    grad_embed = embed_call(at, 0, tgt, ep0, em0, ed0, packs, feats, None, "embed_a")
    grad_hidden, grad_embed = scatter(keep, recv, c, grad_embed)
    grad_embed = embed_call(at, CUT, tgt, ep1, em1, ed1, packs, feats, grad_embed, "embed_b")
    return grad_hidden.reshape(4, 128, 128), grad_embed, grad_mix


def solution(mesh):
    fine = Mesh(mesh.devices.reshape(4, 4, 2, 4), ("x", "z", "c", "y"))
    v = ("x", "z", "c")
    return jax.shard_map(
        local,
        mesh=fine,
        in_specs=(P(None, "y", v), P(v, None), P(None, "y"), P("y"), P("y")),
        out_specs=(P(None, "y", v), P(v, "y"), P(None, "y")),
        check_vma=False,
    )
```

```python
import functools

import jax
import jax.numpy as jnp
from jax import lax
from jax.experimental import pallas as pl
from jax.experimental.pallas import tpu as pltpu
from jax.sharding import Mesh, PartitionSpec as P

BF, F32 = jnp.bfloat16, jnp.float32
ROWS = 512
HALF = 256
WIDTH = 4096
VOC = 2048
TILE = 512
TILES = VOC // TILE
VMEM = 56 * 2**20


def shift(a, axis, d):
    return lax.ppermute(a, axis, [((i + d) % 4, i) for i in range(4)])


def sibling(a):
    return lax.ppermute(a, "c", [(0, 1), (1, 0)])


def cross(a, which, d):
    pairs = []
    for x in range(4):
        for z in range(4):
            for c in range(2):
                along_x = (c + which) % 2 == 0
                sx, sz = ((x + d) % 4, z) if along_x else (x, (z + d) % 4)
                pairs.append(((sx * 4 + sz) * 2 + c, (x * 4 + z) * 2 + c))
    return lax.ppermute(a, ("x", "z", "c"), pairs)


def dot_nt(a, b):
    return lax.dot_general(a, b, (((1,), (1,)), ((), ())), preferred_element_type=F32)


def dot_nn(a, b):
    return lax.dot_general(a, b, (((1,), (0,)), ((), ())), preferred_element_type=F32)


def params(**kw):
    return pltpu.CompilerParams(vmem_limit_bytes=VMEM, **kw)


SMALL = pl.CostEstimate(flops=1000, bytes_accessed=1000, transcendentals=0)
HBM = pl.BlockSpec(memory_space=pltpu.HBM)


def gate_body(*refs):
    pass


def gate(*arrays):
    n = len(arrays)
    return pl.pallas_call(
        gate_body,
        in_specs=[HBM] * n,
        out_specs=[HBM] * n,
        out_shape=[jax.ShapeDtypeStruct(a.shape, a.dtype) for a in arrays],
        input_output_aliases={i: i for i in range(n)},
        compiler_params=params(),
        cost_estimate=SMALL,
        name="gate",
    )(*arrays)


CUT = VOC // 2
SUB = 256


def gather_pieces(block):
    s = jnp.stack([block] + [cross(block, 0, d) for d in (1, 2, 3)])
    return [s] + [cross(s, 1, d) for d in (1, 2, 3)]


def logits_body(at, *refs):
    pieces, refs = refs[:8], refs[8:]
    tid, emb, e0_out, e1_out, st_out, loc_out, full, sem = refs
    step = pl.program_id(0)
    x, z, c = at[0], at[1], at[2]

    @pl.when(step == 0)
    def _():
        copies = []
        for n in range(8):
            core = c if n < 4 else 1 - c
            row = pl.multiple_of(core * HALF, HALF)
            for b in range(4):
                dx = jnp.where(core == 0, b, n % 4)
                dz = jnp.where(core == 0, n % 4, b)
                col = pl.multiple_of((((x + dx) & 3) * 4 + ((z + dz) & 3)) * 256, 256)
                copies.append((pieces[n].at[b], full.at[pl.ds(row, HALF), pl.ds(col, 256)], sem.at[len(copies)]))
        for copy in copies:
            pltpu.make_async_copy(*copy).start()
        for copy in copies:
            pltpu.make_async_copy(*copy).wait()
        st_out[...] = jnp.zeros((8, ROWS), F32)
        loc_out[...] = jnp.zeros((8, ROWS), F32)

    logits = dot_nt(emb[...], full[...])
    top = jnp.max(logits, axis=0, keepdims=True)
    ids = lax.broadcasted_iota(jnp.int32, logits.shape, 0) + step * TILE
    hit = jnp.sum(jnp.where(ids == tid[...], logits, 0.0), axis=0, keepdims=True)
    e = jnp.exp(logits - top)
    total = jnp.sum(e, axis=0, keepdims=True)
    e = e.astype(BF)

    for s in range(TILES):

        @pl.when(step == s)
        def _():
            st_out[pl.ds(s, 1), :] = top
            for k in (0, 1):
                row = s * TILE + k * SUB
                ref, row = (e0_out, row) if row < CUT else (e1_out, row - CUT)
                ref[pl.ds(row, SUB), :] = e[k * SUB : (k + 1) * SUB]

    @pl.when(step == 0)
    def _():
        loc_out[pl.ds(0, 1), :] = top
        loc_out[pl.ds(1, 1), :] = total
        loc_out[pl.ds(2, 1), :] = hit

    @pl.when(step > 0)
    def _():
        old = loc_out[pl.ds(0, 1), :]
        new = jnp.maximum(old, top)
        loc_out[pl.ds(1, 1), :] = loc_out[pl.ds(1, 1), :] * jnp.exp(old - new) + total * jnp.exp(top - new)
        loc_out[pl.ds(0, 1), :] = new
        loc_out[pl.ds(2, 1), :] = loc_out[pl.ds(2, 1), :] + hit


def logits_call(at, pieces, tid, emb):
    whole = pl.BlockSpec((8, ROWS), lambda i, at: (0, 0))
    return pl.pallas_call(
        logits_body,
        grid_spec=pltpu.PrefetchScalarGridSpec(
            num_scalar_prefetch=1,
            grid=(TILES,),
            in_specs=[HBM] * 8
            + [pl.BlockSpec((1, ROWS), lambda i, at: (0, 0)), pl.BlockSpec((TILE, WIDTH), lambda i, at: (i, 0))],
            out_specs=[
                pl.BlockSpec((CUT, ROWS), lambda i, at: (0, 0)),
                pl.BlockSpec((VOC - CUT, ROWS), lambda i, at: (0, 0)),
                whole,
                whole,
            ],
            scratch_shapes=[pltpu.VMEM((ROWS, WIDTH), BF), pltpu.SemaphoreType.DMA((32,))],
        ),
        out_shape=[
            jax.ShapeDtypeStruct((CUT, ROWS), BF),
            jax.ShapeDtypeStruct((VOC - CUT, ROWS), BF),
            jax.ShapeDtypeStruct((8, ROWS), F32),
            jax.ShapeDtypeStruct((8, ROWS), F32),
        ],
        compiler_params=params(),
        cost_estimate=SMALL,
        name="logits",
    )(at, *pieces, tid, emb)


def merge(parts):
    top = functools.reduce(jnp.maximum, [p[0:1] for p in parts])
    total = sum(p[1:2] * jnp.exp(p[0:1] - top) for p in parts)
    hit = sum(p[2:3] for p in parts)
    return top, total, hit


def merge_body(*refs):
    top, total, hit = merge([r[...] for r in refs[:-1]])
    out = refs[-1]
    out[...] = jnp.zeros((8, ROWS), F32)
    out[pl.ds(0, 1), :] = top
    out[pl.ds(1, 1), :] = total
    out[pl.ds(2, 1), :] = hit


def merge_call(*parts):
    stat = pl.BlockSpec((8, ROWS), lambda i: (0, 0))
    return pl.pallas_call(
        merge_body,
        grid=(1,),
        in_specs=[stat] * len(parts),
        out_specs=stat,
        out_shape=jax.ShapeDtypeStruct((8, ROWS), F32),
        compiler_params=params(),
        cost_estimate=SMALL,
        name="merge",
    )(*parts)


def finish_body(a, b, st, tid, mix, weight, ep0, em0, e1, pack, grad_mix, e1_out):
    top, total, hit = merge([a[...], b[...]])
    lse = top + jnp.log(total)
    gap = hit - lse
    mixes = [mix[pl.ds(k, 1), :] for k in range(4)]
    big = functools.reduce(jnp.maximum, mixes)
    norm = big + jnp.log(sum(jnp.exp(m - big) for m in mixes))
    logm = [m - norm for m in mixes]
    score = [logm[k] + gap[:, k * 128 : (k + 1) * 128] for k in range(4)]
    big = functools.reduce(jnp.maximum, score)
    ex = [jnp.exp(s - big) for s in score]
    den = sum(ex)
    w = weight[...]
    scaled = []
    for k in range(4):
        resp = ex[k] / den
        grad_mix[pl.ds(k, 1), :] = w * (jnp.exp(logm[k]) - resp)
        scaled.append(w * resp)
    d = jnp.concatenate(scaled, axis=1)
    pack[...] = jnp.zeros((8, ROWS), F32)
    pack[pl.ds(0, TILES), :] = jnp.exp(st[pl.ds(0, TILES), :] - lse) * d
    pack[pl.ds(4, 1), :] = d
    pack[pl.ds(5, 1), :] = lse
    pack[pl.ds(6, 1), :] = tid[...].astype(F32)


def finish_call(a, b, st, tid, mix, weight, *awaited):
    stat = pl.BlockSpec((8, ROWS), lambda i: (0, 0))
    part = pl.BlockSpec((4, 128), lambda i: (0, 0))
    return pl.pallas_call(
        finish_body,
        grid=(1,),
        in_specs=[stat] * 3
        + [pl.BlockSpec((1, ROWS), lambda i: (0, 0)), part, pl.BlockSpec((1, 128), lambda i: (0, 0))]
        + [HBM] * 3,
        out_specs=[stat, part, HBM],
        out_shape=[
            jax.ShapeDtypeStruct((8, ROWS), F32),
            jax.ShapeDtypeStruct((4, 128), F32),
            jax.ShapeDtypeStruct((VOC - CUT, ROWS), BF),
        ],
        input_output_aliases={8: 2},
        compiler_params=params(),
        cost_estimate=SMALL,
        name="finish",
    )(a, b, st, tid, mix, weight, *awaited)


def token_grad(e, pack, scale, base):
    ids = lax.broadcasted_iota(jnp.int32, e.shape, 0) + base
    tid = pack[pl.ds(6, 1), :].astype(jnp.int32)
    g = e.astype(F32) * scale
    return (g - jnp.where(ids == tid, pack[pl.ds(4, 1), :], 0.0)).astype(BF)


def hidden_body(at, e0, e1, pack, w0, w1, w2, w3, keep, send0, send1, tgt_out, tg):
    @pl.when(pl.program_id(0) == 0)
    def _():
        for t in range(VOC // SUB):
            rows = pl.ds(t * SUB, SUB)
            e = e0[rows, :] if t * SUB < CUT else e1[pl.ds(t * SUB - CUT, SUB), :]
            g = token_grad(e, pack, pack[pl.ds(t * SUB // TILE, 1), :], t * SUB)
            tgt_out[rows, :] = g
            tg[:, rows] = g.T

    w = jnp.concatenate([w0[...], w1[...], w2[...], w3[...]], axis=1)
    r = dot_nn(tg[...], w)
    first = at[2] == 0
    for k in range(4):
        cols = slice(k * 256, (k + 1) * 256)
        a, b = r[:HALF, cols], r[HALF:, cols]
        keep[0, k] = jnp.where(first, a, b)
        (send0, send1)[k // 2][k % 2, 0] = jnp.where(first, b, a).astype(BF)


def hidden_call(at, e0, e1, pack, emb):
    whole = lambda s: pl.BlockSpec(s, lambda i, at: (0,) * len(s))

    def weight(k):
        def index(i, at):
            dx = jnp.where(at[2] == 0, i, k)
            dz = jnp.where(at[2] == 0, k, i)
            return (0, ((at[0] + dx) & 3) * 4 + ((at[1] + dz) & 3))

        return pl.BlockSpec((VOC, 256), index)

    return pl.pallas_call(
        hidden_body,
        grid_spec=pltpu.PrefetchScalarGridSpec(
            num_scalar_prefetch=1,
            grid=(4,),
            in_specs=[whole((CUT, ROWS)), whole((VOC - CUT, ROWS)), whole((8, ROWS))] + [weight(k) for k in range(4)],
            out_specs=[
                pl.BlockSpec((1, 4, HALF, 256), lambda i, at: (i, 0, 0, 0)),
            ]
            + [pl.BlockSpec((2, 1, HALF, 256), lambda i, at: (0, i, 0, 0))] * 2
            + [
                whole((VOC, ROWS)),
            ],
            scratch_shapes=[pltpu.VMEM((ROWS, VOC), BF)],
        ),
        out_shape=[
            jax.ShapeDtypeStruct((4, 4, HALF, 256), F32),
        ]
        + [jax.ShapeDtypeStruct((2, 4, HALF, 256), BF)] * 2
        + [jax.ShapeDtypeStruct((VOC, ROWS), BF)],
        compiler_params=params(),
        cost_estimate=SMALL,
        name="hidden",
    )(at, e0, e1, pack, emb, emb, emb, emb)


def add(*xs):
    return sum(x.astype(F32) for x in xs)


def scatter(keep, recv, c, first, second):
    b = [add(keep[d], recv[d // 2][d % 2]) for d in range(4)]
    u = [cross(b[d].astype(BF), 0, 4 - d) for d in (1, 2, 3)]
    *u, work = gate(*u, first())
    t = add(b[0], *u)
    u = [cross(t[d].astype(BF), 1, 4 - d) for d in (1, 2, 3)]
    *u, work = gate(*u, second(work))
    f = add(t[0], *u)
    low, high = f[:, :128], f[:, 128:]
    mine, other = jnp.where(c == 0, low, high), jnp.where(c == 0, high, low)
    got = sibling(other)
    return jnp.where(c == 0, jnp.concatenate([mine, got]), jnp.concatenate([got, mine])), work


def embed_body(base, at, tgt, ep, em, ed, pack_p, pack_m, pack_d, feats, *refs):
    out, q, sem = refs[-3:]
    i = pl.program_id(0)

    def copies(n, d):
        group = (at[3] + d) & 3
        for k in range(8):
            dst = q.at[pl.ds(n * ROWS, ROWS), pl.ds(k * 128, 128)]
            yield pltpu.make_async_copy(feats.at[group, k // 2, k % 2], dst, sem.at[n * 8 + k])

    @pl.when(i == 0)
    def _():
        for n, d in enumerate((0, 1, 3, 2)):
            for copy in copies(n, d):
                copy.start()
        for n, d in enumerate((0, 1, 3, 2)):
            for copy in copies(n, d):
                copy.wait()

    parts = [tgt[...]]
    tile = base // TILE + i
    for e, pack in ((ep, pack_p), (em, pack_m), (ed, pack_d)):
        parts.append(token_grad(e[...], pack, pack[pl.ds(tile, 1), :], tile * TILE))
    out[...] = dot_nn(jnp.concatenate(parts, axis=1), q[...]).astype(BF)


def embed_call(at, base, tgt, ep, em, ed, packs, feats, into, name):
    first = base // TILE
    tile = pl.BlockSpec((TILE, ROWS), lambda i, at: (i, 0))
    pack = pl.BlockSpec((8, ROWS), lambda i, at: (0, 0))
    more = [] if into is None else [into]
    return pl.pallas_call(
        functools.partial(embed_body, base),
        grid_spec=pltpu.PrefetchScalarGridSpec(
            num_scalar_prefetch=1,
            grid=(CUT // TILE,),
            in_specs=[pl.BlockSpec((TILE, ROWS), lambda i, at: (i + first, 0)), tile, tile, tile, pack, pack, pack, HBM]
            + [HBM] * len(more),
            out_specs=pl.BlockSpec((TILE, 1024), lambda i, at: (i + first, 0)),
            scratch_shapes=[pltpu.VMEM((4 * ROWS, 1024), BF), pltpu.SemaphoreType.DMA((32,))],
        ),
        out_shape=jax.ShapeDtypeStruct((VOC, 1024), BF),
        input_output_aliases={9: 0} if more else {},
        compiler_params=params(),
        cost_estimate=SMALL,
        name=name,
    )(at, tgt, ep, em, ed, *packs, feats, *more)


def local(comp_hidden, embed, mix, targets, weight):
    x, z, c, y = (lax.axis_index(a).astype(jnp.int32) for a in ("x", "z", "c", "y"))
    at = jnp.stack([x, z, c, y])
    own = comp_hidden.reshape(ROWS, 128)
    tid = jnp.tile(targets - ((x * 4 + z) * 2 + c) * VOC, 4).reshape(1, ROWS)

    swap = [(a * 4 + b, b * 4 + a) for a in range(4) for b in range(4)]
    turned = lax.ppermute(own, ("x", "y"), swap)

    low, high = own[:HALF], own[HALF:]
    mine, other = jnp.where(c == 0, low, high), jnp.where(c == 0, high, low)
    got = sibling(other)
    block = jnp.where(c == 0, jnp.concatenate([mine, got], axis=1), jnp.concatenate([got, mine], axis=1))
    pieces = gather_pieces(block)
    pieces = pieces + [sibling(p) for p in pieces]

    e0, e1, st, loc = logits_call(at, pieces, tid, embed)
    loc, turned = gate(loc, turned)
    feats = lax.all_gather(turned, ("x", "z", "c")).reshape(4, 4, 2, ROWS, 128)
    ep0, em0 = shift(e0, "y", 1), shift(e0, "y", 3)

    s = merge_call(loc, *(shift(loc, "x", d) for d in (1, 2, 3)))
    s = merge_call(s, *(shift(s, "z", d) for d in (1, 2, 3)))
    pack, grad_mix, e1 = finish_call(s, sibling(s), st, tid, mix, weight.reshape(1, 128), ep0, em0, e1)
    packs = [shift(pack, "y", d) for d in (1, 3, 2)]
    em1, ed0 = shift(e1, "y", 3), shift(ep0, "y", 1)
    keep, send0, send1, tgt = hidden_call(at, e0, e1, pack, embed)
    send0, send1, e1, em1, ed0, *packs = gate(send0, send1, e1, em1, ed0, *packs)
    ep1, ed1 = shift(e1, "y", 1), shift(em1, "y", 3)
    recv = sibling(send0), sibling(send1)

    grad_hidden, grad_embed = scatter(
        keep,
        recv,
        c,
        lambda: embed_call(at, 0, tgt, ep0, em0, ed0, packs, feats, None, "embed_a"),
        lambda made: embed_call(at, CUT, tgt, ep1, em1, ed1, packs, feats, made, "embed_b"),
    )
    return grad_hidden.reshape(4, 128, 128), grad_embed, grad_mix


def solution(mesh):
    fine = Mesh(mesh.devices.reshape(4, 4, 2, 4), ("x", "z", "c", "y"))
    v = ("x", "z", "c")
    return jax.shard_map(
        local,
        mesh=fine,
        in_specs=(P(None, "y", v), P(v, None), P(None, "y"), P("y"), P("y")),
        out_specs=(P(None, "y", v), P(v, "y"), P(None, "y")),
        check_vma=False,
    )
```

```python
import functools

import jax
import jax.numpy as jnp
from jax import lax
from jax.experimental import pallas as pl
from jax.experimental.pallas import tpu as pltpu
from jax.sharding import Mesh, PartitionSpec as P

BF, F32 = jnp.bfloat16, jnp.float32
ROWS = 512
HALF = 256
WIDTH = 4096
VOC = 2048
TILE = 512
TILES = VOC // TILE
VMEM = 56 * 2**20


def shift(a, axis, d):
    return lax.ppermute(a, axis, [((i + d) % 4, i) for i in range(4)])


def sibling(a):
    return lax.ppermute(a, "c", [(0, 1), (1, 0)])


def cross(a, which, d):
    pairs = []
    for x in range(4):
        for z in range(4):
            for c in range(2):
                along_x = (c + which) % 2 == 0
                sx, sz = ((x + d) % 4, z) if along_x else (x, (z + d) % 4)
                pairs.append(((sx * 4 + sz) * 2 + c, (x * 4 + z) * 2 + c))
    return lax.ppermute(a, ("x", "z", "c"), pairs)


def dot_nt(a, b):
    return lax.dot_general(a, b, (((1,), (1,)), ((), ())), preferred_element_type=F32)


def dot_nn(a, b):
    return lax.dot_general(a, b, (((1,), (0,)), ((), ())), preferred_element_type=F32)


def params(**kw):
    return pltpu.CompilerParams(vmem_limit_bytes=VMEM, **kw)


SMALL = pl.CostEstimate(flops=1000, bytes_accessed=1000, transcendentals=0)
HBM = pl.BlockSpec(memory_space=pltpu.HBM)


def gate_body(*refs):
    pass


def gate(*arrays):
    n = len(arrays)
    return pl.pallas_call(
        gate_body,
        in_specs=[HBM] * n,
        out_specs=[HBM] * n,
        out_shape=[jax.ShapeDtypeStruct(a.shape, a.dtype) for a in arrays],
        input_output_aliases={i: i for i in range(n)},
        compiler_params=params(),
        cost_estimate=SMALL,
        name="gate",
    )(*arrays)


CUT = VOC // 2
SUB = 256


def gather_pieces(block):
    s = jnp.stack([block] + [cross(block, 0, d) for d in (1, 2, 3)])
    return [s] + [cross(s, 1, d) for d in (1, 2, 3)]


def logits_body(at, *refs):
    pieces, refs = refs[:8], refs[8:]
    tid, emb, e0_out, e1_out, st_out, loc_out, full = refs
    step = pl.program_id(0)
    x, z, c = at[0], at[1], at[2]

    @pl.when(step == 0)
    def _():
        for n in range(8):
            core = c if n < 4 else 1 - c
            row = pl.multiple_of(core * HALF, HALF)
            for b in range(4):
                dx = jnp.where(core == 0, b, n % 4)
                dz = jnp.where(core == 0, n % 4, b)
                col = pl.multiple_of((((x + dx) & 3) * 4 + ((z + dz) & 3)) * 256, 256)
                full[pl.ds(row, HALF), pl.ds(col, 256)] = pieces[n][b]
        st_out[...] = jnp.zeros((8, ROWS), F32)
        loc_out[...] = jnp.zeros((8, ROWS), F32)

    logits = dot_nt(emb[...], full[...])
    top = jnp.max(logits, axis=0, keepdims=True)
    ids = lax.broadcasted_iota(jnp.int32, logits.shape, 0) + step * TILE
    hit = jnp.sum(jnp.where(ids == tid[...], logits, 0.0), axis=0, keepdims=True)
    e = jnp.exp(logits - top)
    total = jnp.sum(e, axis=0, keepdims=True)
    e = e.astype(BF)

    for s in range(TILES):

        @pl.when(step == s)
        def _():
            st_out[pl.ds(s, 1), :] = top
            for k in (0, 1):
                row = s * TILE + k * SUB
                ref, row = (e0_out, row) if row < CUT else (e1_out, row - CUT)
                ref[pl.ds(row, SUB), :] = e[k * SUB : (k + 1) * SUB]

    @pl.when(step == 0)
    def _():
        loc_out[pl.ds(0, 1), :] = top
        loc_out[pl.ds(1, 1), :] = total
        loc_out[pl.ds(2, 1), :] = hit

    @pl.when(step > 0)
    def _():
        old = loc_out[pl.ds(0, 1), :]
        new = jnp.maximum(old, top)
        loc_out[pl.ds(1, 1), :] = loc_out[pl.ds(1, 1), :] * jnp.exp(old - new) + total * jnp.exp(top - new)
        loc_out[pl.ds(0, 1), :] = new
        loc_out[pl.ds(2, 1), :] = loc_out[pl.ds(2, 1), :] + hit


def logits_call(at, pieces, tid, emb):
    whole = pl.BlockSpec((8, ROWS), lambda i, at: (0, 0))
    return pl.pallas_call(
        logits_body,
        grid_spec=pltpu.PrefetchScalarGridSpec(
            num_scalar_prefetch=1,
            grid=(TILES,),
            in_specs=[pl.BlockSpec((4, HALF, 256), lambda i, at: (0, 0, 0))] * 8
            + [pl.BlockSpec((1, ROWS), lambda i, at: (0, 0)), pl.BlockSpec((TILE, WIDTH), lambda i, at: (i, 0))],
            out_specs=[
                pl.BlockSpec((CUT, ROWS), lambda i, at: (0, 0)),
                pl.BlockSpec((VOC - CUT, ROWS), lambda i, at: (0, 0)),
                whole,
                whole,
            ],
            scratch_shapes=[pltpu.VMEM((ROWS, WIDTH), BF)],
        ),
        out_shape=[
            jax.ShapeDtypeStruct((CUT, ROWS), BF),
            jax.ShapeDtypeStruct((VOC - CUT, ROWS), BF),
            jax.ShapeDtypeStruct((8, ROWS), F32),
            jax.ShapeDtypeStruct((8, ROWS), F32),
        ],
        compiler_params=params(),
        cost_estimate=SMALL,
        name="logits",
    )(at, *pieces, tid, emb)


def merge(parts):
    top = functools.reduce(jnp.maximum, [p[0:1] for p in parts])
    total = sum(p[1:2] * jnp.exp(p[0:1] - top) for p in parts)
    hit = sum(p[2:3] for p in parts)
    return top, total, hit


def merge_call(*parts):
    return jnp.concatenate([*merge(parts), jnp.zeros((5, ROWS), F32)])


def finish_body(a, b, st, tid, mix, weight, ep0, em0, e1, pack, grad_mix, e1_out):
    top, total, hit = merge([a[...], b[...]])
    lse = top + jnp.log(total)
    gap = hit - lse
    mixes = [mix[pl.ds(k, 1), :] for k in range(4)]
    big = functools.reduce(jnp.maximum, mixes)
    norm = big + jnp.log(sum(jnp.exp(m - big) for m in mixes))
    logm = [m - norm for m in mixes]
    score = [logm[k] + gap[:, k * 128 : (k + 1) * 128] for k in range(4)]
    big = functools.reduce(jnp.maximum, score)
    ex = [jnp.exp(s - big) for s in score]
    den = sum(ex)
    w = weight[...]
    scaled = []
    for k in range(4):
        resp = ex[k] / den
        grad_mix[pl.ds(k, 1), :] = w * (jnp.exp(logm[k]) - resp)
        scaled.append(w * resp)
    d = jnp.concatenate(scaled, axis=1)
    pack[...] = jnp.zeros((8, ROWS), F32)
    pack[pl.ds(0, TILES), :] = jnp.exp(st[pl.ds(0, TILES), :] - lse) * d
    pack[pl.ds(4, 1), :] = d
    pack[pl.ds(5, 1), :] = lse
    pack[pl.ds(6, 1), :] = tid[...].astype(F32)


def finish_call(a, b, st, tid, mix, weight, *awaited):
    stat = pl.BlockSpec((8, ROWS), lambda i: (0, 0))
    part = pl.BlockSpec((4, 128), lambda i: (0, 0))
    return pl.pallas_call(
        finish_body,
        grid=(1,),
        in_specs=[stat] * 3
        + [pl.BlockSpec((1, ROWS), lambda i: (0, 0)), part, pl.BlockSpec((1, 128), lambda i: (0, 0))]
        + [HBM] * 3,
        out_specs=[stat, part, HBM],
        out_shape=[
            jax.ShapeDtypeStruct((8, ROWS), F32),
            jax.ShapeDtypeStruct((4, 128), F32),
            jax.ShapeDtypeStruct((VOC - CUT, ROWS), BF),
        ],
        input_output_aliases={8: 2},
        compiler_params=params(),
        cost_estimate=SMALL,
        name="finish",
    )(a, b, st, tid, mix, weight, *awaited)


def token_grad(e, pack, scale, base):
    ids = lax.broadcasted_iota(jnp.int32, e.shape, 0) + base
    tid = pack[pl.ds(6, 1), :].astype(jnp.int32)
    g = e.astype(F32) * scale
    return (g - jnp.where(ids == tid, pack[pl.ds(4, 1), :], 0.0)).astype(BF)


def hidden_body(at, e0, e1, pack, w0, w1, w2, w3, keep, send0, send1, tgt_out, tg):
    @pl.when(pl.program_id(0) == 0)
    def _():
        for t in range(VOC // SUB):
            rows = pl.ds(t * SUB, SUB)
            e = e0[rows, :] if t * SUB < CUT else e1[pl.ds(t * SUB - CUT, SUB), :]
            g = token_grad(e, pack, pack[pl.ds(t * SUB // TILE, 1), :], t * SUB)
            tgt_out[rows, :] = g
            tg[:, rows] = g.T

    w = jnp.concatenate([w0[...], w1[...], w2[...], w3[...]], axis=1)
    r = dot_nn(tg[...], w)
    first = at[2] == 0
    for k in range(4):
        cols = slice(k * 256, (k + 1) * 256)
        a, b = r[:HALF, cols], r[HALF:, cols]
        keep[0, k] = jnp.where(first, a, b)
        (send0, send1)[k // 2][k % 2, 0] = jnp.where(first, b, a).astype(BF)


def hidden_call(at, e0, e1, pack, emb):
    whole = lambda s: pl.BlockSpec(s, lambda i, at: (0,) * len(s))

    def weight(k):
        def index(i, at):
            dx = jnp.where(at[2] == 0, i, k)
            dz = jnp.where(at[2] == 0, k, i)
            return (0, ((at[0] + dx) & 3) * 4 + ((at[1] + dz) & 3))

        return pl.BlockSpec((VOC, 256), index)

    return pl.pallas_call(
        hidden_body,
        grid_spec=pltpu.PrefetchScalarGridSpec(
            num_scalar_prefetch=1,
            grid=(4,),
            in_specs=[whole((CUT, ROWS)), whole((VOC - CUT, ROWS)), whole((8, ROWS))] + [weight(k) for k in range(4)],
            out_specs=[
                pl.BlockSpec((1, 4, HALF, 256), lambda i, at: (i, 0, 0, 0)),
            ]
            + [pl.BlockSpec((2, 1, HALF, 256), lambda i, at: (0, i, 0, 0))] * 2
            + [
                whole((VOC, ROWS)),
            ],
            scratch_shapes=[pltpu.VMEM((ROWS, VOC), BF)],
        ),
        out_shape=[
            jax.ShapeDtypeStruct((4, 4, HALF, 256), F32),
        ]
        + [jax.ShapeDtypeStruct((2, 4, HALF, 256), BF)] * 2
        + [jax.ShapeDtypeStruct((VOC, ROWS), BF)],
        compiler_params=params(),
        cost_estimate=SMALL,
        name="hidden",
    )(at, e0, e1, pack, emb, emb, emb, emb)


def add(*xs):
    return sum(x.astype(F32) for x in xs)


def scatter(keep, recv, c, first, second, others):
    b = [add(keep[d], recv[d // 2][d % 2]) for d in range(4)]
    u = [cross(b[d].astype(BF), 0, 4 - d) for d in (1, 2, 3)]
    u1, u2, u3, work, *others = gate(*u, first(), *others)
    u = [u1, u2, u3]
    t = add(b[0], *u)
    u = [cross(t[d].astype(BF), 1, 4 - d) for d in (1, 2, 3)]
    *u, work = gate(*u, second(work, *others))
    f = add(t[0], *u)
    low, high = f[:, :128], f[:, 128:]
    mine, other = jnp.where(c == 0, low, high), jnp.where(c == 0, high, low)
    got = sibling(other)
    return jnp.where(c == 0, jnp.concatenate([mine, got]), jnp.concatenate([got, mine])), work


def embed_body(base, at, tgt, ep, em, ed, pack_p, pack_m, pack_d, *refs):
    feats, out = refs[:4], refs[-1]
    i = pl.program_id(0)

    parts = [tgt[...]]
    tile = base // TILE + i
    for e, pack in ((ep, pack_p), (em, pack_m), (ed, pack_d)):
        parts.append(token_grad(e[...], pack, pack[pl.ds(tile, 1), :], tile * TILE))
    q = [jnp.concatenate([f[0, k // 2, k % 2] for k in range(8)], axis=1) for f in feats]
    out[...] = dot_nn(jnp.concatenate(parts, axis=1), jnp.concatenate(q, axis=0)).astype(BF)


def embed_call(at, base, tgt, ep, em, ed, packs, feats, into, name):
    first = base // TILE
    tile = pl.BlockSpec((TILE, ROWS), lambda i, at: (i, 0))
    pack = pl.BlockSpec((8, ROWS), lambda i, at: (0, 0))
    feat = lambda d: pl.BlockSpec((1, 4, 2, ROWS, 128), lambda i, at: ((at[3] + d) & 3, 0, 0, 0, 0))
    more = [] if into is None else [into]
    return pl.pallas_call(
        functools.partial(embed_body, base),
        grid_spec=pltpu.PrefetchScalarGridSpec(
            num_scalar_prefetch=1,
            grid=(CUT // TILE,),
            in_specs=[pl.BlockSpec((TILE, ROWS), lambda i, at: (i + first, 0)), tile, tile, tile, pack, pack, pack]
            + [feat(d) for d in (0, 1, 3, 2)]
            + [HBM] * len(more),
            out_specs=pl.BlockSpec((TILE, 1024), lambda i, at: (i + first, 0)),
        ),
        out_shape=jax.ShapeDtypeStruct((VOC, 1024), BF),
        input_output_aliases={12: 0} if more else {},
        compiler_params=params(),
        cost_estimate=SMALL,
        name=name,
    )(at, tgt, ep, em, ed, *packs, *[feats] * 4, *more)


def local(comp_hidden, embed, mix, targets, weight):
    x, z, c, y = (lax.axis_index(a).astype(jnp.int32) for a in ("x", "z", "c", "y"))
    at = jnp.stack([x, z, c, y])
    own = comp_hidden.reshape(ROWS, 128)
    tid = jnp.tile(targets - ((x * 4 + z) * 2 + c) * VOC, 4).reshape(1, ROWS)

    swap = [(a * 4 + b, b * 4 + a) for a in range(4) for b in range(4)]
    turned = lax.ppermute(own, ("x", "y"), swap)

    low, high = own[:HALF], own[HALF:]
    mine, other = jnp.where(c == 0, low, high), jnp.where(c == 0, high, low)
    got = sibling(other)
    block = jnp.where(c == 0, jnp.concatenate([mine, got], axis=1), jnp.concatenate([got, mine], axis=1))
    pieces = gather_pieces(block)
    pieces = pieces + [sibling(p) for p in pieces]

    e0, e1, st, loc = logits_call(at, pieces, tid, embed)
    loc, turned = gate(loc, turned)
    feats = lax.all_gather(turned, ("x", "z", "c")).reshape(4, 4, 2, ROWS, 128)
    ep0, em0 = shift(e0, "y", 1), shift(e0, "y", 3)

    s = merge_call(loc, *(shift(loc, "x", d) for d in (1, 2, 3)))
    s = merge_call(s, *(shift(s, "z", d) for d in (1, 2, 3)))
    pack, grad_mix, e1 = finish_call(s, sibling(s), st, tid, mix, weight.reshape(1, 128), ep0, em0, e1)
    packs = [shift(pack, "y", d) for d in (1, 3, 2)]
    em1, ed0 = shift(e1, "y", 3), shift(ep0, "y", 1)
    keep, send0, send1, tgt = hidden_call(at, e0, e1, pack, embed)
    send0, send1, e1, em1, ed0, *packs = gate(send0, send1, e1, em1, ed0, *packs)
    ep1, ed1 = shift(e1, "y", 1), shift(em1, "y", 3)
    recv = sibling(send0), sibling(send1)

    grad_hidden, grad_embed = scatter(
        keep,
        recv,
        c,
        lambda: embed_call(at, 0, tgt, ep0, em0, ed0, packs, feats, None, "embed_a"),
        lambda made, ep1, ed1: embed_call(at, CUT, tgt, ep1, em1, ed1, packs, feats, made, "embed_b"),
        (ep1, ed1),
    )
    return grad_hidden.reshape(4, 128, 128), grad_embed, grad_mix


def solution(mesh):
    fine = Mesh(mesh.devices.reshape(4, 4, 2, 4), ("x", "z", "c", "y"))
    v = ("x", "z", "c")
    return jax.shard_map(
        local,
        mesh=fine,
        in_specs=(P(None, "y", v), P(v, None), P(None, "y"), P("y"), P("y")),
        out_specs=(P(None, "y", v), P(v, "y"), P(None, "y")),
        check_vma=False,
    )
```

```python
import functools

import jax
import jax.numpy as jnp
from jax import lax
from jax.experimental import pallas as pl
from jax.experimental.pallas import tpu as pltpu
from jax.sharding import Mesh, PartitionSpec as P

BF, F32 = jnp.bfloat16, jnp.float32
ROWS = 512
HALF = 256
WIDTH = 4096
VOC = 2048
TILE = 512
TILES = VOC // TILE
VMEM = 56 * 2**20


def shift(a, axis, d):
    return lax.ppermute(a, axis, [((i + d) % 4, i) for i in range(4)])


def sibling(a):
    return lax.ppermute(a, "c", [(0, 1), (1, 0)])


def cross(a, which, d):
    pairs = []
    for x in range(4):
        for z in range(4):
            for c in range(2):
                along_x = (c + which) % 2 == 0
                sx, sz = ((x + d) % 4, z) if along_x else (x, (z + d) % 4)
                pairs.append(((sx * 4 + sz) * 2 + c, (x * 4 + z) * 2 + c))
    return lax.ppermute(a, ("x", "z", "c"), pairs)


def dot_nt(a, b):
    return lax.dot_general(a, b, (((1,), (1,)), ((), ())), preferred_element_type=F32)


def dot_nn(a, b):
    return lax.dot_general(a, b, (((1,), (0,)), ((), ())), preferred_element_type=F32)


def params(**kw):
    return pltpu.CompilerParams(vmem_limit_bytes=VMEM, **kw)


SMALL = pl.CostEstimate(flops=1000, bytes_accessed=1000, transcendentals=0)
HBM = pl.BlockSpec(memory_space=pltpu.HBM)


def gate_body(*refs):
    pass


def gate(*arrays):
    n = len(arrays)
    return pl.pallas_call(
        gate_body,
        in_specs=[HBM] * n,
        out_specs=[HBM] * n,
        out_shape=[jax.ShapeDtypeStruct(a.shape, a.dtype) for a in arrays],
        input_output_aliases={i: i for i in range(n)},
        compiler_params=params(),
        cost_estimate=SMALL,
        name="gate",
    )(*arrays)


CUT = VOC // 2
SUB = 256


def gather_pieces(block, *others):
    s = jnp.stack([block] + [cross(block, 0, d) for d in (1, 2, 3)])
    far = [cross(s, 1, d) for d in (1, 2, 3)]
    far[2], *others = gate(far[2], *others)
    return [s] + far, others


def logits_body(v0, at, *refs):
    pieces, refs = refs[:8], refs[8:]
    tid, emb, before, e_out, st_out, loc_out, full = refs
    step = pl.program_id(0)
    x, z, c = at[0], at[1], at[2]

    @pl.when(step == 0)
    def _():
        for n in range(8):
            core = c if n < 4 else 1 - c
            row = pl.multiple_of(core * HALF, HALF)
            for b in range(4):
                dx = jnp.where(core == 0, b, n % 4)
                dz = jnp.where(core == 0, n % 4, b)
                col = pl.multiple_of((((x + dx) & 3) * 4 + ((z + dz) & 3)) * 256, 256)
                full[pl.ds(row, HALF), pl.ds(col, 256)] = pieces[n][b]
        st_out[...] = jnp.zeros((8, ROWS), F32)
        loc_out[...] = before[...]

    logits = dot_nt(emb[...], full[...])
    top = jnp.max(logits, axis=0, keepdims=True)
    ids = lax.broadcasted_iota(jnp.int32, logits.shape, 0) + (v0 + step * TILE)
    hit = jnp.sum(jnp.where(ids == tid[...], logits, 0.0), axis=0, keepdims=True)
    e = jnp.exp(logits - top)
    total = jnp.sum(e, axis=0, keepdims=True)
    e_out[...] = e.astype(BF)
    for s in range(CUT // TILE):

        @pl.when(step == s)
        def _():
            st_out[pl.ds(s, 1), :] = top

    old = loc_out[pl.ds(0, 1), :]
    new = jnp.maximum(old, top)
    loc_out[pl.ds(1, 1), :] = loc_out[pl.ds(1, 1), :] * jnp.exp(old - new) + total * jnp.exp(top - new)
    loc_out[pl.ds(0, 1), :] = new
    loc_out[pl.ds(2, 1), :] = loc_out[pl.ds(2, 1), :] + hit


def logits_call(at, pieces, tid, emb, v0, before, name):
    first = v0 // TILE
    stat = pl.BlockSpec((8, ROWS), lambda i, at: (0, 0))
    return pl.pallas_call(
        functools.partial(logits_body, v0),
        grid_spec=pltpu.PrefetchScalarGridSpec(
            num_scalar_prefetch=1,
            grid=(CUT // TILE,),
            in_specs=[pl.BlockSpec((4, HALF, 256), lambda i, at: (0, 0, 0))] * 8
            + [
                pl.BlockSpec((1, ROWS), lambda i, at: (0, 0)),
                pl.BlockSpec((TILE, WIDTH), lambda i, at: (i + first, 0)),
                stat,
            ],
            out_specs=[pl.BlockSpec((TILE, ROWS), lambda i, at: (i, 0)), stat, stat],
            scratch_shapes=[pltpu.VMEM((ROWS, WIDTH), BF)],
        ),
        out_shape=[
            jax.ShapeDtypeStruct((CUT, ROWS), BF),
            jax.ShapeDtypeStruct((8, ROWS), F32),
            jax.ShapeDtypeStruct((8, ROWS), F32),
        ],
        compiler_params=params(),
        cost_estimate=SMALL,
        name=name,
    )(at, *pieces, tid, emb, before)


def merge(parts):
    top = functools.reduce(jnp.maximum, [p[0:1] for p in parts])
    total = sum(p[1:2] * jnp.exp(p[0:1] - top) for p in parts)
    hit = sum(p[2:3] for p in parts)
    return top, total, hit


def merge_call(*parts):
    return jnp.concatenate([*merge(parts), jnp.zeros((5, ROWS), F32)])


def finish_body(a, b, st0, st1, tid, mix, weight, ep0, em0, e1, pack, grad_mix, e1_out):
    top, total, hit = merge([a[...], b[...]])
    lse = top + jnp.log(total)
    gap = hit - lse
    mixes = [mix[pl.ds(k, 1), :] for k in range(4)]
    big = functools.reduce(jnp.maximum, mixes)
    norm = big + jnp.log(sum(jnp.exp(m - big) for m in mixes))
    logm = [m - norm for m in mixes]
    score = [logm[k] + gap[:, k * 128 : (k + 1) * 128] for k in range(4)]
    big = functools.reduce(jnp.maximum, score)
    ex = [jnp.exp(s - big) for s in score]
    den = sum(ex)
    w = weight[...]
    scaled = []
    for k in range(4):
        resp = ex[k] / den
        grad_mix[pl.ds(k, 1), :] = w * (jnp.exp(logm[k]) - resp)
        scaled.append(w * resp)
    d = jnp.concatenate(scaled, axis=1)
    pack[...] = jnp.zeros((8, ROWS), F32)
    n = CUT // TILE
    pack[pl.ds(0, n), :] = jnp.exp(st0[pl.ds(0, n), :] - lse) * d
    pack[pl.ds(n, n), :] = jnp.exp(st1[pl.ds(0, n), :] - lse) * d
    pack[pl.ds(4, 1), :] = d
    pack[pl.ds(5, 1), :] = lse
    pack[pl.ds(6, 1), :] = tid[...].astype(F32)


def finish_call(a, b, st0, st1, tid, mix, weight, *awaited):
    stat = pl.BlockSpec((8, ROWS), lambda i: (0, 0))
    part = pl.BlockSpec((4, 128), lambda i: (0, 0))
    return pl.pallas_call(
        finish_body,
        grid=(1,),
        in_specs=[stat] * 4
        + [pl.BlockSpec((1, ROWS), lambda i: (0, 0)), part, pl.BlockSpec((1, 128), lambda i: (0, 0))]
        + [HBM] * 3,
        out_specs=[stat, part, HBM],
        out_shape=[
            jax.ShapeDtypeStruct((8, ROWS), F32),
            jax.ShapeDtypeStruct((4, 128), F32),
            jax.ShapeDtypeStruct((VOC - CUT, ROWS), BF),
        ],
        input_output_aliases={9: 2},
        compiler_params=params(),
        cost_estimate=SMALL,
        name="finish",
    )(a, b, st0, st1, tid, mix, weight, *awaited)


def token_grad(e, pack, scale, base):
    ids = lax.broadcasted_iota(jnp.int32, e.shape, 0) + base
    tid = pack[pl.ds(6, 1), :].astype(jnp.int32)
    g = e.astype(F32) * scale
    return (g - jnp.where(ids == tid, pack[pl.ds(4, 1), :], 0.0)).astype(BF)


def hidden_body(at, e0, e1, pack, w0, w1, w2, w3, keep, send0, send1, tgt_out, tg):
    @pl.when(pl.program_id(0) == 0)
    def _():
        for t in range(VOC // SUB):
            rows = pl.ds(t * SUB, SUB)
            e = e0[rows, :] if t * SUB < CUT else e1[pl.ds(t * SUB - CUT, SUB), :]
            g = token_grad(e, pack, pack[pl.ds(t * SUB // TILE, 1), :], t * SUB)
            tgt_out[rows, :] = g
            tg[:, rows] = g.T

    w = jnp.concatenate([w0[...], w1[...], w2[...], w3[...]], axis=1)
    r = dot_nn(tg[...], w)
    first = at[2] == 0
    for k in range(4):
        cols = slice(k * 256, (k + 1) * 256)
        a, b = r[:HALF, cols], r[HALF:, cols]
        keep[0, k] = jnp.where(first, a, b).astype(BF)
        (send0, send1)[k // 2][k % 2, 0] = jnp.where(first, b, a).astype(BF)


def hidden_call(at, e0, e1, pack, emb):
    whole = lambda s: pl.BlockSpec(s, lambda i, at: (0,) * len(s))

    def weight(k):
        def index(i, at):
            dx = jnp.where(at[2] == 0, i, k)
            dz = jnp.where(at[2] == 0, k, i)
            return (0, ((at[0] + dx) & 3) * 4 + ((at[1] + dz) & 3))

        return pl.BlockSpec((VOC, 256), index)

    return pl.pallas_call(
        hidden_body,
        grid_spec=pltpu.PrefetchScalarGridSpec(
            num_scalar_prefetch=1,
            grid=(4,),
            in_specs=[whole((CUT, ROWS)), whole((VOC - CUT, ROWS)), whole((8, ROWS))] + [weight(k) for k in range(4)],
            out_specs=[
                pl.BlockSpec((1, 4, HALF, 256), lambda i, at: (i, 0, 0, 0)),
            ]
            + [pl.BlockSpec((2, 1, HALF, 256), lambda i, at: (0, i, 0, 0))] * 2
            + [
                whole((VOC, ROWS)),
            ],
            scratch_shapes=[pltpu.VMEM((ROWS, VOC), BF)],
        ),
        out_shape=[
            jax.ShapeDtypeStruct((4, 4, HALF, 256), BF),
        ]
        + [jax.ShapeDtypeStruct((2, 4, HALF, 256), BF)] * 2
        + [jax.ShapeDtypeStruct((VOC, ROWS), BF)],
        compiler_params=params(),
        cost_estimate=SMALL,
        name="hidden",
    )(at, e0, e1, pack, emb, emb, emb, emb)


def add(*xs):
    return sum(x.astype(F32) for x in xs)


def scatter(keep, recv, c, first, second, others):
    b = [add(keep[d], recv[d // 2][d % 2]) for d in range(4)]
    u = [cross(b[d].astype(BF), 0, 4 - d) for d in (1, 2, 3)]
    u1, u2, u3, work, *others = gate(*u, first(), *others)
    u = [u1, u2, u3]
    t = add(b[0], *u)
    u = [cross(t[d].astype(BF), 1, 4 - d) for d in (1, 2, 3)]
    *u, work = gate(*u, second(work, *others))
    f = add(t[0], *u)
    low, high = f[:, :128], f[:, 128:]
    mine, other = jnp.where(c == 0, low, high), jnp.where(c == 0, high, low)
    got = sibling(other)
    return jnp.where(c == 0, jnp.concatenate([mine, got]), jnp.concatenate([got, mine])), work


def embed_body(base, at, tgt, ep, em, ed, pack_p, pack_m, pack_d, *refs):
    feats, out = refs[:4], refs[-1]
    i = pl.program_id(0)

    parts = [tgt[...]]
    tile = base // TILE + i
    for e, pack in ((ep, pack_p), (em, pack_m), (ed, pack_d)):
        parts.append(token_grad(e[...], pack, pack[pl.ds(tile, 1), :], tile * TILE))
    q = [jnp.concatenate([f[0, k // 2, k % 2] for k in range(8)], axis=1) for f in feats]
    out[...] = dot_nn(jnp.concatenate(parts, axis=1), jnp.concatenate(q, axis=0)).astype(BF)


def embed_call(at, base, tgt, ep, em, ed, packs, feats, into, name):
    first = base // TILE
    tile = pl.BlockSpec((TILE, ROWS), lambda i, at: (i, 0))
    pack = pl.BlockSpec((8, ROWS), lambda i, at: (0, 0))
    feat = lambda d: pl.BlockSpec((1, 4, 2, ROWS, 128), lambda i, at: ((at[3] + d) & 3, 0, 0, 0, 0))
    more = [] if into is None else [into]
    return pl.pallas_call(
        functools.partial(embed_body, base),
        grid_spec=pltpu.PrefetchScalarGridSpec(
            num_scalar_prefetch=1,
            grid=(CUT // TILE,),
            in_specs=[pl.BlockSpec((TILE, ROWS), lambda i, at: (i + first, 0)), tile, tile, tile, pack, pack, pack]
            + [feat(d) for d in (0, 1, 3, 2)]
            + [HBM] * len(more),
            out_specs=pl.BlockSpec((TILE, 1024), lambda i, at: (i + first, 0)),
        ),
        out_shape=jax.ShapeDtypeStruct((VOC, 1024), BF),
        input_output_aliases={12: 0} if more else {},
        compiler_params=params(),
        cost_estimate=SMALL,
        name=name,
    )(at, tgt, ep, em, ed, *packs, *[feats] * 4, *more)


def local(comp_hidden, embed, mix, targets, weight):
    x, z, c, y = (lax.axis_index(a).astype(jnp.int32) for a in ("x", "z", "c", "y"))
    at = jnp.stack([x, z, c, y])
    own = comp_hidden.reshape(ROWS, 128)
    tid = jnp.tile(targets - ((x * 4 + z) * 2 + c) * VOC, 4).reshape(1, ROWS)

    swap = [(a * 4 + b, b * 4 + a) for a in range(4) for b in range(4)]
    turned = lax.ppermute(own, ("x", "y"), swap)

    low, high = own[:HALF], own[HALF:]
    mine, other = jnp.where(c == 0, low, high), jnp.where(c == 0, high, low)
    got = sibling(other)
    block = jnp.where(c == 0, jnp.concatenate([mine, got], axis=1), jnp.concatenate([got, mine], axis=1))
    pieces, (turned, at, tid) = gather_pieces(block, turned, at, tid)
    pieces = pieces + [sibling(p) for p in pieces]

    none = jnp.zeros((8, ROWS), F32).at[0].set(-3e38)
    e0, st0, loc = logits_call(at, pieces, tid, embed, 0, none, "logits_a")
    e1, st1, loc = logits_call(at, pieces, tid, embed, CUT, loc, "logits_b")
    feats = lax.all_gather(turned, ("x", "z", "c")).reshape(4, 4, 2, ROWS, 128)
    ep0, em0 = shift(e0, "y", 1), shift(e0, "y", 3)

    s = merge_call(loc, *(shift(loc, "x", d) for d in (1, 2, 3)))
    s = merge_call(s, *(shift(s, "z", d) for d in (1, 2, 3)))
    pack, grad_mix, e1 = finish_call(s, sibling(s), st0, st1, tid, mix, weight.reshape(1, 128), ep0, em0, e1)
    packs = [shift(pack, "y", d) for d in (1, 3, 2)]
    em1, ed0 = shift(e1, "y", 3), shift(ep0, "y", 1)
    keep, send0, send1, tgt = hidden_call(at, e0, e1, pack, embed)
    send0, send1, e1, em1, ed0, *packs = gate(send0, send1, e1, em1, ed0, *packs)
    ep1, ed1 = shift(e1, "y", 1), shift(em1, "y", 3)
    recv = sibling(send0), sibling(send1)

    grad_hidden, grad_embed = scatter(
        keep,
        recv,
        c,
        lambda: embed_call(at, 0, tgt, ep0, em0, ed0, packs, feats, None, "embed_a"),
        lambda made, ep1, ed1: embed_call(at, CUT, tgt, ep1, em1, ed1, packs, feats, made, "embed_b"),
        (ep1, ed1),
    )
    return grad_hidden.reshape(4, 128, 128), grad_embed, grad_mix


def solution(mesh):
    fine = Mesh(mesh.devices.reshape(4, 4, 2, 4), ("x", "z", "c", "y"))
    v = ("x", "z", "c")
    return jax.shard_map(
        local,
        mesh=fine,
        in_specs=(P(None, "y", v), P(v, None), P(None, "y"), P("y"), P("y")),
        out_specs=(P(None, "y", v), P(v, "y"), P(None, "y")),
        check_vma=False,
    )
```

```python
import functools

import jax
import jax.numpy as jnp
from jax import lax
from jax.experimental import pallas as pl
from jax.experimental.pallas import tpu as pltpu
from jax.sharding import Mesh, PartitionSpec as P

BF, F32 = jnp.bfloat16, jnp.float32
ROWS = 512
HALF = 256
WIDTH = 4096
VOC = 2048
TILE = 512
TILES = VOC // TILE
VMEM = 56 * 2**20


def shift(a, axis, d):
    return lax.ppermute(a, axis, [((i + d) % 4, i) for i in range(4)])


def sibling(a):
    return lax.ppermute(a, "c", [(0, 1), (1, 0)])


def cross(a, which, d):
    pairs = []
    for x in range(4):
        for z in range(4):
            for c in range(2):
                along_x = (c + which) % 2 == 0
                sx, sz = ((x + d) % 4, z) if along_x else (x, (z + d) % 4)
                pairs.append(((sx * 4 + sz) * 2 + c, (x * 4 + z) * 2 + c))
    return lax.ppermute(a, ("x", "z", "c"), pairs)


def dot_nt(a, b):
    return lax.dot_general(a, b, (((1,), (1,)), ((), ())), preferred_element_type=F32)


def dot_nn(a, b):
    return lax.dot_general(a, b, (((1,), (0,)), ((), ())), preferred_element_type=F32)


def params(**kw):
    return pltpu.CompilerParams(vmem_limit_bytes=VMEM, **kw)


SMALL = pl.CostEstimate(flops=1000, bytes_accessed=1000, transcendentals=0)
HBM = pl.BlockSpec(memory_space=pltpu.HBM)


def gate_body(*refs):
    pass


def gate(*arrays):
    n = len(arrays)
    return pl.pallas_call(
        gate_body,
        in_specs=[HBM] * n,
        out_specs=[HBM] * n,
        out_shape=[jax.ShapeDtypeStruct(a.shape, a.dtype) for a in arrays],
        input_output_aliases={i: i for i in range(n)},
        compiler_params=params(),
        cost_estimate=SMALL,
        name="gate",
    )(*arrays)


CUT = VOC // 2
SUB = 256


def gather_pieces(block, *early):
    near = [cross(block, 0, d) for d in (1, 2, 3)]
    near[2], *early = gate(near[2], *early)
    s = jnp.stack([block, *near])
    far = [cross(s, 1, d) for d in (1, 2, 3)]
    return [s] + far, *early


def logits_body(at, *refs):
    pieces, refs = refs[:8], refs[8:]
    tid, emb, e0_out, e1_out, st_out, loc_out, full = refs
    step = pl.program_id(0)
    x, z, c = at[0], at[1], at[2]

    @pl.when(step == 0)
    def _():
        for n in range(8):
            core = c if n < 4 else 1 - c
            row = pl.multiple_of(core * HALF, HALF)
            for b in range(4):
                dx = jnp.where(core == 0, b, n % 4)
                dz = jnp.where(core == 0, n % 4, b)
                col = pl.multiple_of((((x + dx) & 3) * 4 + ((z + dz) & 3)) * 256, 256)
                full[pl.ds(row, HALF), pl.ds(col, 256)] = pieces[n][b]
        st_out[...] = jnp.zeros((8, ROWS), F32)
        loc_out[...] = jnp.zeros((8, ROWS), F32)

    logits = dot_nt(emb[...], full[...])
    top = jnp.max(logits, axis=0, keepdims=True)
    ids = lax.broadcasted_iota(jnp.int32, logits.shape, 0) + step * TILE
    hit = jnp.sum(jnp.where(ids == tid[...], logits, 0.0), axis=0, keepdims=True)
    e = jnp.exp(logits - top)
    total = jnp.sum(e, axis=0, keepdims=True)
    e = e.astype(BF)

    for s in range(TILES):

        @pl.when(step == s)
        def _():
            st_out[pl.ds(s, 1), :] = top
            for k in (0, 1):
                row = s * TILE + k * SUB
                ref, row = (e0_out, row) if row < CUT else (e1_out, row - CUT)
                ref[pl.ds(row, SUB), :] = e[k * SUB : (k + 1) * SUB]

    @pl.when(step == 0)
    def _():
        loc_out[pl.ds(0, 1), :] = top
        loc_out[pl.ds(1, 1), :] = total
        loc_out[pl.ds(2, 1), :] = hit

    @pl.when(step > 0)
    def _():
        old = loc_out[pl.ds(0, 1), :]
        new = jnp.maximum(old, top)
        loc_out[pl.ds(1, 1), :] = loc_out[pl.ds(1, 1), :] * jnp.exp(old - new) + total * jnp.exp(top - new)
        loc_out[pl.ds(0, 1), :] = new
        loc_out[pl.ds(2, 1), :] = loc_out[pl.ds(2, 1), :] + hit


def logits_call(at, pieces, tid, emb):
    whole = pl.BlockSpec((8, ROWS), lambda i, at: (0, 0))
    return pl.pallas_call(
        logits_body,
        grid_spec=pltpu.PrefetchScalarGridSpec(
            num_scalar_prefetch=1,
            grid=(TILES,),
            in_specs=[pl.BlockSpec((4, HALF, 256), lambda i, at: (0, 0, 0))] * 8
            + [pl.BlockSpec((1, ROWS), lambda i, at: (0, 0)), pl.BlockSpec((TILE, WIDTH), lambda i, at: (i, 0))],
            out_specs=[
                pl.BlockSpec((CUT, ROWS), lambda i, at: (0, 0)),
                pl.BlockSpec((VOC - CUT, ROWS), lambda i, at: (0, 0)),
                whole,
                whole,
            ],
            scratch_shapes=[pltpu.VMEM((ROWS, WIDTH), BF)],
        ),
        out_shape=[
            jax.ShapeDtypeStruct((CUT, ROWS), BF),
            jax.ShapeDtypeStruct((VOC - CUT, ROWS), BF),
            jax.ShapeDtypeStruct((8, ROWS), F32),
            jax.ShapeDtypeStruct((8, ROWS), F32),
        ],
        compiler_params=params(),
        cost_estimate=SMALL,
        name="logits",
    )(at, *pieces, tid, emb)


def merge(parts):
    top = functools.reduce(jnp.maximum, [p[0:1] for p in parts])
    total = sum(p[1:2] * jnp.exp(p[0:1] - top) for p in parts)
    hit = sum(p[2:3] for p in parts)
    return top, total, hit


def merge_call(*parts):
    return jnp.concatenate([*merge(parts), jnp.zeros((5, ROWS), F32)])


def finish_body(a, b, st, tid, mix, weight, pack, grad_mix):
    top, total, hit = merge([a[...], b[...]])
    lse = top + jnp.log(total)
    gap = hit - lse
    mixes = [mix[pl.ds(k, 1), :] for k in range(4)]
    big = functools.reduce(jnp.maximum, mixes)
    norm = big + jnp.log(sum(jnp.exp(m - big) for m in mixes))
    logm = [m - norm for m in mixes]
    score = [logm[k] + gap[:, k * 128 : (k + 1) * 128] for k in range(4)]
    big = functools.reduce(jnp.maximum, score)
    ex = [jnp.exp(s - big) for s in score]
    den = sum(ex)
    w = weight[...]
    scaled = []
    for k in range(4):
        resp = ex[k] / den
        grad_mix[pl.ds(k, 1), :] = w * (jnp.exp(logm[k]) - resp)
        scaled.append(w * resp)
    d = jnp.concatenate(scaled, axis=1)
    pack[...] = jnp.zeros((8, ROWS), F32)
    pack[pl.ds(0, TILES), :] = jnp.exp(st[pl.ds(0, TILES), :] - lse) * d
    pack[pl.ds(4, 1), :] = d
    pack[pl.ds(5, 1), :] = lse
    pack[pl.ds(6, 1), :] = tid[...].astype(F32)


def finish_call(a, b, st, tid, mix, weight):
    stat = pl.BlockSpec((8, ROWS), lambda i: (0, 0))
    part = pl.BlockSpec((4, 128), lambda i: (0, 0))
    return pl.pallas_call(
        finish_body,
        grid=(1,),
        in_specs=[stat] * 3
        + [pl.BlockSpec((1, ROWS), lambda i: (0, 0)), part, pl.BlockSpec((1, 128), lambda i: (0, 0))],
        out_specs=[stat, part],
        out_shape=[
            jax.ShapeDtypeStruct((8, ROWS), F32),
            jax.ShapeDtypeStruct((4, 128), F32),
        ],
        compiler_params=params(),
        cost_estimate=SMALL,
        name="finish",
    )(a, b, st, tid, mix, weight)


def token_grad(e, pack, scale, base):
    ids = lax.broadcasted_iota(jnp.int32, e.shape, 0) + base
    tid = pack[pl.ds(6, 1), :].astype(jnp.int32)
    g = e.astype(F32) * scale
    return (g - jnp.where(ids == tid, pack[pl.ds(4, 1), :], 0.0)).astype(BF)


def hidden_body(at, e0, e1, pack, w0, w1, w2, w3, keep, send0, send1, tgt_out, tg):
    @pl.when(pl.program_id(0) == 0)
    def _():
        for t in range(VOC // SUB):
            rows = pl.ds(t * SUB, SUB)
            e = e0[rows, :] if t * SUB < CUT else e1[pl.ds(t * SUB - CUT, SUB), :]
            g = token_grad(e, pack, pack[pl.ds(t * SUB // TILE, 1), :], t * SUB)
            tgt_out[rows, :] = g
            tg[:, rows] = g.T

    w = jnp.concatenate([w0[...], w1[...], w2[...], w3[...]], axis=1)
    r = dot_nn(tg[...], w)
    first = at[2] == 0
    for k in range(4):
        cols = slice(k * 256, (k + 1) * 256)
        a, b = r[:HALF, cols], r[HALF:, cols]
        keep[0, k] = jnp.where(first, a, b).astype(BF)
        (send0, send1)[k // 2][k % 2, 0] = jnp.where(first, b, a).astype(BF)


def hidden_call(at, e0, e1, pack, emb):
    whole = lambda s: pl.BlockSpec(s, lambda i, at: (0,) * len(s))

    def weight(k):
        def index(i, at):
            dx = jnp.where(at[2] == 0, i, k)
            dz = jnp.where(at[2] == 0, k, i)
            return (0, ((at[0] + dx) & 3) * 4 + ((at[1] + dz) & 3))

        return pl.BlockSpec((VOC, 256), index)

    return pl.pallas_call(
        hidden_body,
        grid_spec=pltpu.PrefetchScalarGridSpec(
            num_scalar_prefetch=1,
            grid=(4,),
            in_specs=[whole((CUT, ROWS)), whole((VOC - CUT, ROWS)), whole((8, ROWS))] + [weight(k) for k in range(4)],
            out_specs=[
                pl.BlockSpec((1, 4, HALF, 256), lambda i, at: (i, 0, 0, 0)),
            ]
            + [pl.BlockSpec((2, 1, HALF, 256), lambda i, at: (0, i, 0, 0))] * 2
            + [
                whole((VOC, ROWS)),
            ],
            scratch_shapes=[pltpu.VMEM((ROWS, VOC), BF)],
        ),
        out_shape=[
            jax.ShapeDtypeStruct((4, 4, HALF, 256), BF),
        ]
        + [jax.ShapeDtypeStruct((2, 4, HALF, 256), BF)] * 2
        + [jax.ShapeDtypeStruct((VOC, ROWS), BF)],
        compiler_params=params(),
        cost_estimate=SMALL,
        name="hidden",
    )(at, e0, e1, pack, emb, emb, emb, emb)


def add(*xs):
    return sum(x.astype(F32) for x in xs)


def scatter(keep, recv, c, first, second, others):
    b = [add(keep[d], recv[d // 2][d % 2]) for d in range(4)]
    u = [cross(b[d].astype(BF), 0, 4 - d) for d in (1, 2, 3)]
    u1, u2, u3, work, *others = gate(*u, first(), *others)
    t = add(b[0], u1, u2, u3)
    u = [cross(t[d].astype(BF), 1, 4 - d) for d in (1, 2, 3)]
    *u, work = gate(*u, second(work, *others))
    f = add(t[0], *u)
    low, high = f[:, :128], f[:, 128:]
    mine, other = jnp.where(c == 0, low, high), jnp.where(c == 0, high, low)
    got = sibling(other)
    return jnp.where(c == 0, jnp.concatenate([mine, got]), jnp.concatenate([got, mine])), work


def embed_body(base, at, tgt, ep, em, ed, pack_p, pack_m, pack_d, *refs):
    feats, out = refs[:4], refs[-1]
    i = pl.program_id(0)

    parts = [tgt[...]]
    tile = base // TILE + i
    for e, pack in ((ep, pack_p), (em, pack_m), (ed, pack_d)):
        parts.append(token_grad(e[...], pack, pack[pl.ds(tile, 1), :], tile * TILE))
    q = [jnp.concatenate([f[0, k // 2, k % 2] for k in range(8)], axis=1) for f in feats]
    out[...] = dot_nn(jnp.concatenate(parts, axis=1), jnp.concatenate(q, axis=0)).astype(BF)


def embed_call(at, base, tgt, ep, em, ed, packs, feats, into, name):
    first = base // TILE
    tile = pl.BlockSpec((TILE, ROWS), lambda i, at: (i, 0))
    pack = pl.BlockSpec((8, ROWS), lambda i, at: (0, 0))
    feat = lambda d: pl.BlockSpec((1, 4, 2, ROWS, 128), lambda i, at: ((at[3] + d) & 3, 0, 0, 0, 0))
    more = [] if into is None else [into]
    return pl.pallas_call(
        functools.partial(embed_body, base),
        grid_spec=pltpu.PrefetchScalarGridSpec(
            num_scalar_prefetch=1,
            grid=(CUT // TILE,),
            in_specs=[pl.BlockSpec((TILE, ROWS), lambda i, at: (i + first, 0)), tile, tile, tile, pack, pack, pack]
            + [feat(d) for d in (0, 1, 3, 2)]
            + [HBM] * len(more),
            out_specs=pl.BlockSpec((TILE, 1024), lambda i, at: (i + first, 0)),
        ),
        out_shape=jax.ShapeDtypeStruct((VOC, 1024), BF),
        input_output_aliases={12: 0} if more else {},
        compiler_params=params(),
        cost_estimate=SMALL,
        name=name,
    )(at, tgt, ep, em, ed, *packs, *[feats] * 4, *more)


def local(comp_hidden, embed, mix, targets, weight):
    x, z, c, y = (lax.axis_index(a).astype(jnp.int32) for a in ("x", "z", "c", "y"))
    at = jnp.stack([x, z, c, y])
    own = comp_hidden.reshape(ROWS, 128)
    tid = jnp.tile(targets - ((x * 4 + z) * 2 + c) * VOC, 4).reshape(1, ROWS)

    swap = [(a * 4 + b, b * 4 + a) for a in range(4) for b in range(4)]
    turned = lax.ppermute(own, ("x", "y"), swap)

    low, high = own[:HALF], own[HALF:]
    mine, other = jnp.where(c == 0, low, high), jnp.where(c == 0, high, low)
    got = sibling(other)
    block = jnp.where(c == 0, jnp.concatenate([mine, got], axis=1), jnp.concatenate([got, mine], axis=1))
    pieces, at, tid = gather_pieces(block, at, tid)
    pieces = pieces + [sibling(p) for p in pieces]

    e0, e1, st, loc = logits_call(at, pieces, tid, embed)
    loc, turned = gate(loc, turned)
    feats = lax.all_gather(turned, ("x", "z", "c")).reshape(4, 4, 2, ROWS, 128)
    ep0, em0 = shift(e0, "y", 1), shift(e0, "y", 3)

    s = merge_call(loc, *(shift(loc, "x", d) for d in (1, 2, 3)))
    s = merge_call(s, *(shift(s, "z", d) for d in (1, 2, 3)))
    pack, grad_mix = finish_call(s, sibling(s), st, tid, mix, weight.reshape(1, 128))
    packs = [shift(pack, "y", d) for d in (1, 3, 2)]
    pack, e1, ep0, em0, *packs = gate(pack, e1, ep0, em0, *packs)
    em1, ed0 = shift(e1, "y", 3), shift(ep0, "y", 1)
    keep, send0, send1, tgt = hidden_call(at, e0, e1, pack, embed)
    send0, send1, e1, em1, ed0 = gate(send0, send1, e1, em1, ed0)
    ep1, ed1 = shift(e1, "y", 1), shift(em1, "y", 3)
    recv = sibling(send0), sibling(send1)

    grad_hidden, grad_embed = scatter(
        keep,
        recv,
        c,
        lambda: embed_call(at, 0, tgt, ep0, em0, ed0, packs, feats, None, "embed_a"),
        lambda made, ep1, ed1: embed_call(at, CUT, tgt, ep1, em1, ed1, packs, feats, made, "embed_b"),
        (ep1, ed1),
    )
    return grad_hidden.reshape(4, 128, 128), grad_embed, grad_mix


def solution(mesh):
    fine = Mesh(mesh.devices.reshape(4, 4, 2, 4), ("x", "z", "c", "y"))
    v = ("x", "z", "c")
    return jax.shard_map(
        local,
        mesh=fine,
        in_specs=(P(None, "y", v), P(v, None), P(None, "y"), P("y"), P("y")),
        out_specs=(P(None, "y", v), P(v, "y"), P(None, "y")),
        check_vma=False,
    )
```

```python
import functools

import jax
import jax.numpy as jnp
from jax import lax
from jax.experimental import pallas as pl
from jax.experimental.pallas import tpu as pltpu
from jax.sharding import Mesh, PartitionSpec as P

BF, F32 = jnp.bfloat16, jnp.float32
ROWS = 512
HALF = 256
WIDTH = 4096
VOC = 2048
TILE = 512
TILES = VOC // TILE
VMEM = 56 * 2**20


def shift(a, axis, d):
    return lax.ppermute(a, axis, [((i + d) % 4, i) for i in range(4)])


def sibling(a):
    return lax.ppermute(a, "c", [(0, 1), (1, 0)])


def cross(a, which, d):
    pairs = []
    for x in range(4):
        for z in range(4):
            for c in range(2):
                along_x = (c + which) % 2 == 0
                sx, sz = ((x + d) % 4, z) if along_x else (x, (z + d) % 4)
                pairs.append(((sx * 4 + sz) * 2 + c, (x * 4 + z) * 2 + c))
    return lax.ppermute(a, ("x", "z", "c"), pairs)


def dot_nt(a, b):
    return lax.dot_general(a, b, (((1,), (1,)), ((), ())), preferred_element_type=F32)


def dot_nn(a, b):
    return lax.dot_general(a, b, (((1,), (0,)), ((), ())), preferred_element_type=F32)


def params(**kw):
    return pltpu.CompilerParams(vmem_limit_bytes=VMEM, **kw)


SMALL = pl.CostEstimate(flops=1000, bytes_accessed=1000, transcendentals=0)
HBM = pl.BlockSpec(memory_space=pltpu.HBM)


def gate_body(*refs):
    pass


def gate(*arrays):
    n = len(arrays)
    return pl.pallas_call(
        gate_body,
        in_specs=[HBM] * n,
        out_specs=[HBM] * n,
        out_shape=[jax.ShapeDtypeStruct(a.shape, a.dtype) for a in arrays],
        input_output_aliases={i: i for i in range(n)},
        compiler_params=params(),
        cost_estimate=SMALL,
        name="gate",
    )(*arrays)


SUB = 256
CUT = VOC // 2


def gather_pieces(block, *early):
    near = [cross(block, 0, d) for d in (1, 2, 3)]
    near[2], *early = gate(near[2], *early)
    s = jnp.stack([block, *near])
    far = [cross(s, 1, d) for d in (1, 2, 3)]
    return [s] + far, *early


def logits_body(at, *refs):
    pieces, refs = refs[:8], refs[8:]
    tid, emb, e_out, st_out, loc_out, full = refs
    step = pl.program_id(0)
    x, z, c = at[0], at[1], at[2]

    @pl.when(step == 0)
    def _():
        for n in range(8):
            core = c if n < 4 else 1 - c
            row = pl.multiple_of(core * HALF, HALF)
            for b in range(4):
                dx = jnp.where(core == 0, b, n % 4)
                dz = jnp.where(core == 0, n % 4, b)
                col = pl.multiple_of((((x + dx) & 3) * 4 + ((z + dz) & 3)) * 256, 256)
                full[pl.ds(row, HALF), pl.ds(col, 256)] = pieces[n][b]
        st_out[...] = jnp.zeros((8, ROWS), F32)
        loc_out[...] = jnp.zeros((8, ROWS), F32)

    logits = dot_nt(emb[...], full[...])
    top = jnp.max(logits, axis=0, keepdims=True)
    ids = lax.broadcasted_iota(jnp.int32, logits.shape, 0) + step * TILE
    hit = jnp.sum(jnp.where(ids == tid[...], logits, 0.0), axis=0, keepdims=True)
    e = jnp.exp(logits - top)
    total = jnp.sum(e, axis=0, keepdims=True)
    e_out[...] = e.astype(BF)
    for s in range(TILES):

        @pl.when(step == s)
        def _():
            st_out[pl.ds(s, 1), :] = top

    @pl.when(step == 0)
    def _():
        loc_out[pl.ds(0, 1), :] = top
        loc_out[pl.ds(1, 1), :] = total
        loc_out[pl.ds(2, 1), :] = hit

    @pl.when(step > 0)
    def _():
        old = loc_out[pl.ds(0, 1), :]
        new = jnp.maximum(old, top)
        loc_out[pl.ds(1, 1), :] = loc_out[pl.ds(1, 1), :] * jnp.exp(old - new) + total * jnp.exp(top - new)
        loc_out[pl.ds(0, 1), :] = new
        loc_out[pl.ds(2, 1), :] = loc_out[pl.ds(2, 1), :] + hit


def logits_call(at, pieces, tid, emb):
    whole = pl.BlockSpec((8, ROWS), lambda i, at: (0, 0))
    return pl.pallas_call(
        logits_body,
        grid_spec=pltpu.PrefetchScalarGridSpec(
            num_scalar_prefetch=1,
            grid=(TILES,),
            in_specs=[pl.BlockSpec((4, HALF, 256), lambda i, at: (0, 0, 0))] * 8
            + [pl.BlockSpec((1, ROWS), lambda i, at: (0, 0)), pl.BlockSpec((TILE, WIDTH), lambda i, at: (i, 0))],
            out_specs=[
                pl.BlockSpec((TILE, ROWS), lambda i, at: (i, 0)),
                whole,
                whole,
            ],
            scratch_shapes=[pltpu.VMEM((ROWS, WIDTH), BF)],
        ),
        out_shape=[
            jax.ShapeDtypeStruct((VOC, ROWS), BF),
            jax.ShapeDtypeStruct((8, ROWS), F32),
            jax.ShapeDtypeStruct((8, ROWS), F32),
        ],
        compiler_params=params(),
        cost_estimate=SMALL,
        name="logits",
    )(at, *pieces, tid, emb)


def merge(parts):
    top = functools.reduce(jnp.maximum, [p[0:1] for p in parts])
    total = sum(p[1:2] * jnp.exp(p[0:1] - top) for p in parts)
    hit = sum(p[2:3] for p in parts)
    return top, total, hit


def merge_call(*parts):
    return jnp.concatenate([*merge(parts), jnp.zeros((5, ROWS), F32)])


def finish_body(a, b, st, tid, mix, weight, pack, grad_mix):
    top, total, hit = merge([a[...], b[...]])
    lse = top + jnp.log(total)
    gap = hit - lse
    mixes = [mix[pl.ds(k, 1), :] for k in range(4)]
    big = functools.reduce(jnp.maximum, mixes)
    norm = big + jnp.log(sum(jnp.exp(m - big) for m in mixes))
    logm = [m - norm for m in mixes]
    score = [logm[k] + gap[:, k * 128 : (k + 1) * 128] for k in range(4)]
    big = functools.reduce(jnp.maximum, score)
    ex = [jnp.exp(s - big) for s in score]
    den = sum(ex)
    w = weight[...]
    scaled = []
    for k in range(4):
        resp = ex[k] / den
        grad_mix[pl.ds(k, 1), :] = w * (jnp.exp(logm[k]) - resp)
        scaled.append(w * resp)
    d = jnp.concatenate(scaled, axis=1)
    pack[...] = jnp.zeros((8, ROWS), F32)
    pack[pl.ds(0, TILES), :] = jnp.exp(st[pl.ds(0, TILES), :] - lse) * d
    pack[pl.ds(4, 1), :] = d
    pack[pl.ds(5, 1), :] = lse
    pack[pl.ds(6, 1), :] = tid[...].astype(F32)


def finish_call(a, b, st, tid, mix, weight):
    stat = pl.BlockSpec((8, ROWS), lambda i: (0, 0))
    part = pl.BlockSpec((4, 128), lambda i: (0, 0))
    return pl.pallas_call(
        finish_body,
        grid=(1,),
        in_specs=[stat] * 3
        + [pl.BlockSpec((1, ROWS), lambda i: (0, 0)), part, pl.BlockSpec((1, 128), lambda i: (0, 0))],
        out_specs=[stat, part],
        out_shape=[
            jax.ShapeDtypeStruct((8, ROWS), F32),
            jax.ShapeDtypeStruct((4, 128), F32),
        ],
        compiler_params=params(),
        cost_estimate=SMALL,
        name="finish",
    )(a, b, st, tid, mix, weight)


def token_grad(e, pack, scale, base):
    ids = lax.broadcasted_iota(jnp.int32, e.shape, 0) + base
    tid = pack[pl.ds(6, 1), :].astype(jnp.int32)
    g = e.astype(F32) * scale
    return (g - jnp.where(ids == tid, pack[pl.ds(4, 1), :], 0.0)).astype(BF)


def hidden_body(at, e, pack, w0, w1, w2, w3, keep, send0, send1, tgt_out, tg):
    @pl.when(pl.program_id(0) == 0)
    def _():
        for t in range(VOC // SUB):
            rows = pl.ds(t * SUB, SUB)
            g = token_grad(e[rows, :], pack, pack[pl.ds(t * SUB // TILE, 1), :], t * SUB)
            tgt_out[rows, :] = g
            tg[:, rows] = g.T

    w = jnp.concatenate([w0[...], w1[...], w2[...], w3[...]], axis=1)
    r = dot_nn(tg[...], w)
    first = at[2] == 0
    for k in range(4):
        cols = slice(k * 256, (k + 1) * 256)
        a, b = r[:HALF, cols], r[HALF:, cols]
        keep[0, k] = jnp.where(first, a, b).astype(BF)
        (send0, send1)[k // 2][k % 2, 0] = jnp.where(first, b, a).astype(BF)


def hidden_call(at, e, pack, emb):
    whole = lambda s: pl.BlockSpec(s, lambda i, at: (0,) * len(s))

    def weight(k):
        def index(i, at):
            dx = jnp.where(at[2] == 0, i, k)
            dz = jnp.where(at[2] == 0, k, i)
            return (0, ((at[0] + dx) & 3) * 4 + ((at[1] + dz) & 3))

        return pl.BlockSpec((VOC, 256), index)

    return pl.pallas_call(
        hidden_body,
        grid_spec=pltpu.PrefetchScalarGridSpec(
            num_scalar_prefetch=1,
            grid=(4,),
            in_specs=[whole((VOC, ROWS)), whole((8, ROWS))] + [weight(k) for k in range(4)],
            out_specs=[
                pl.BlockSpec((1, 4, HALF, 256), lambda i, at: (i, 0, 0, 0)),
            ]
            + [pl.BlockSpec((2, 1, HALF, 256), lambda i, at: (0, i, 0, 0))] * 2
            + [
                whole((VOC, ROWS)),
            ],
            scratch_shapes=[pltpu.VMEM((ROWS, VOC), BF)],
        ),
        out_shape=[
            jax.ShapeDtypeStruct((4, 4, HALF, 256), BF),
        ]
        + [jax.ShapeDtypeStruct((2, 4, HALF, 256), BF)] * 2
        + [jax.ShapeDtypeStruct((VOC, ROWS), BF)],
        compiler_params=params(),
        cost_estimate=SMALL,
        name="hidden",
    )(at, e, pack, emb, emb, emb, emb)


def add(*xs):
    return sum(x.astype(F32) for x in xs)


def scatter(keep, recv, c, first, second, others):
    b = [add(keep[d], recv[d // 2][d % 2]) for d in range(4)]
    u = [cross(b[d].astype(BF), 0, 4 - d) for d in (1, 2, 3)]
    u1, u2, u3, work, *others = gate(*u, first(), *others)
    t = add(b[0], u1, u2, u3)
    u = [cross(t[d].astype(BF), 1, 4 - d) for d in (1, 2, 3)]
    *u, work = gate(*u, second(work, *others))
    f = add(t[0], *u)
    low, high = f[:, :128], f[:, 128:]
    mine, other = jnp.where(c == 0, low, high), jnp.where(c == 0, high, low)
    got = sibling(other)
    return jnp.where(c == 0, jnp.concatenate([mine, got]), jnp.concatenate([got, mine])), work


def feature_spec(d):
    return pl.BlockSpec((1, 4, 2, ROWS, 128), lambda i, at: ((at[3] + d) & 3, 0, 0, 0, 0))


def columns(f):
    return jnp.concatenate([f[0, k // 2, k % 2] for k in range(8)], axis=1)


def embed_a_body(at, tgt, ep, em, pack_p, pack_m, f0, f1, f3, acc):
    i = pl.program_id(0)
    parts = [tgt[...]]
    for e, pack in ((ep, pack_p), (em, pack_m)):
        parts.append(token_grad(e[...], pack, pack[pl.ds(i, 1), :], i * TILE))
    q = jnp.concatenate([columns(f) for f in (f0, f1, f3)], axis=0)
    acc[...] = dot_nn(jnp.concatenate(parts, axis=1), q)


def embed_a_call(at, tgt, ep, em, packs, feats):
    tile = pl.BlockSpec((TILE, ROWS), lambda i, at: (i, 0))
    pack = pl.BlockSpec((8, ROWS), lambda i, at: (0, 0))
    return pl.pallas_call(
        embed_a_body,
        grid_spec=pltpu.PrefetchScalarGridSpec(
            num_scalar_prefetch=1,
            grid=(TILES,),
            in_specs=[tile, tile, tile, pack, pack] + [feature_spec(d) for d in (0, 1, 3)],
            out_specs=pl.BlockSpec((TILE, 1024), lambda i, at: (i, 0)),
        ),
        out_shape=jax.ShapeDtypeStruct((VOC, 1024), F32),
        compiler_params=params(),
        cost_estimate=SMALL,
        name="embed_a",
    )(at, tgt, ep, em, *packs, feats, feats, feats)


def embed_b_body(at, acc, low, high, pack, f2, out):
    i = pl.program_id(0)
    e = jnp.where(i < CUT // TILE, low[...], high[...])
    g = token_grad(e, pack, pack[pl.ds(i, 1), :], i * TILE)
    out[...] = (acc[...] + dot_nn(g, columns(f2))).astype(BF)


def embed_b_call(at, acc, low, high, pack, feats):
    n = CUT // TILE
    return pl.pallas_call(
        embed_b_body,
        grid_spec=pltpu.PrefetchScalarGridSpec(
            num_scalar_prefetch=1,
            grid=(TILES,),
            in_specs=[
                pl.BlockSpec((TILE, 1024), lambda i, at: (i, 0)),
                pl.BlockSpec((TILE, ROWS), lambda i, at: (jnp.minimum(i, n - 1), 0)),
                pl.BlockSpec((TILE, ROWS), lambda i, at: (jnp.maximum(i - n, 0), 0)),
                pl.BlockSpec((8, ROWS), lambda i, at: (0, 0)),
                feature_spec(2),
            ],
            out_specs=pl.BlockSpec((TILE, 1024), lambda i, at: (i, 0)),
        ),
        out_shape=jax.ShapeDtypeStruct((VOC, 1024), BF),
        compiler_params=params(),
        cost_estimate=SMALL,
        name="embed_b",
    )(at, acc, low, high, pack, feats)


def local(comp_hidden, embed, mix, targets, weight):
    x, z, c, y = (lax.axis_index(a).astype(jnp.int32) for a in ("x", "z", "c", "y"))
    at = jnp.stack([x, z, c, y])
    own = comp_hidden.reshape(ROWS, 128)
    tid = jnp.tile(targets - ((x * 4 + z) * 2 + c) * VOC, 4).reshape(1, ROWS)

    swap = [(a * 4 + b, b * 4 + a) for a in range(4) for b in range(4)]
    turned = lax.ppermute(own, ("x", "y"), swap)

    low, high = own[:HALF], own[HALF:]
    mine, other = jnp.where(c == 0, low, high), jnp.where(c == 0, high, low)
    got = sibling(other)
    block = jnp.where(c == 0, jnp.concatenate([mine, got], axis=1), jnp.concatenate([got, mine], axis=1))
    pieces, at, tid = gather_pieces(block, at, tid)
    pieces = pieces + [sibling(p) for p in pieces]

    e, st, loc = logits_call(at, pieces, tid, embed)
    loc, turned = gate(loc, turned)
    feats = lax.all_gather(turned, ("x", "z", "c")).reshape(4, 4, 2, ROWS, 128)
    ep, em = shift(e, "y", 1), shift(e, "y", 3)

    s = merge_call(loc, *(shift(loc, "x", d) for d in (1, 2, 3)))
    s = merge_call(s, *(shift(s, "z", d) for d in (1, 2, 3)))
    pack, grad_mix = finish_call(s, sibling(s), st, tid, mix, weight.reshape(1, 128))
    packs = [shift(pack, "y", d) for d in (1, 3, 2)]
    keep, send0, send1, tgt = hidden_call(at, e, pack, embed)
    send0, send1, ep, em, *packs = gate(send0, send1, ep, em, *packs)
    low, high = shift(ep[:CUT], "y", 1), shift(em[CUT:], "y", 3)
    recv = sibling(send0), sibling(send1)

    grad_hidden, grad_embed = scatter(
        keep,
        recv,
        c,
        lambda: embed_a_call(at, tgt, ep, em, packs[:2], feats),
        lambda acc, low, high: embed_b_call(at, acc, low, high, packs[2], feats),
        (low, high),
    )
    return grad_hidden.reshape(4, 128, 128), grad_embed, grad_mix


def solution(mesh):
    fine = Mesh(mesh.devices.reshape(4, 4, 2, 4), ("x", "z", "c", "y"))
    v = ("x", "z", "c")
    return jax.shard_map(
        local,
        mesh=fine,
        in_specs=(P(None, "y", v), P(v, None), P(None, "y"), P("y"), P("y")),
        out_specs=(P(None, "y", v), P(v, "y"), P(None, "y")),
        check_vma=False,
    )
```

```python
import functools

import jax
import jax.numpy as jnp
from jax import lax
from jax.experimental import pallas as pl
from jax.experimental.pallas import tpu as pltpu
from jax.sharding import Mesh, PartitionSpec as P

BF, F32 = jnp.bfloat16, jnp.float32
ROWS = 512
HALF = 256
WIDTH = 4096
VOC = 2048
TILE = 512
TILES = VOC // TILE
VMEM = 56 * 2**20


def shift(a, axis, d):
    return lax.ppermute(a, axis, [((i + d) % 4, i) for i in range(4)])


def sibling(a):
    return lax.ppermute(a, "c", [(0, 1), (1, 0)])


def cross(a, which, d):
    pairs = []
    for x in range(4):
        for z in range(4):
            for c in range(2):
                along_x = (c + which) % 2 == 0
                sx, sz = ((x + d) % 4, z) if along_x else (x, (z + d) % 4)
                pairs.append(((sx * 4 + sz) * 2 + c, (x * 4 + z) * 2 + c))
    return lax.ppermute(a, ("x", "z", "c"), pairs)


def dot_nt(a, b):
    return lax.dot_general(a, b, (((1,), (1,)), ((), ())), preferred_element_type=F32)


def dot_nn(a, b):
    return lax.dot_general(a, b, (((1,), (0,)), ((), ())), preferred_element_type=F32)


def params(**kw):
    return pltpu.CompilerParams(vmem_limit_bytes=VMEM, **kw)


SMALL = pl.CostEstimate(flops=1000, bytes_accessed=1000, transcendentals=0)
HBM = pl.BlockSpec(memory_space=pltpu.HBM)


def gate_body(*refs):
    pass


def gate(*arrays):
    n = len(arrays)
    return pl.pallas_call(
        gate_body,
        in_specs=[HBM] * n,
        out_specs=[HBM] * n,
        out_shape=[jax.ShapeDtypeStruct(a.shape, a.dtype) for a in arrays],
        input_output_aliases={i: i for i in range(n)},
        compiler_params=params(),
        cost_estimate=SMALL,
        name="gate",
    )(*arrays)


SUB = 256
CUT = VOC // 2


def onward_body(*refs):
    low, high, sem = refs[-3:]
    ep, em = refs[0], refs[1]
    copies = []
    for k in range(4):
        rows = pl.ds(k * SUB, SUB)
        copies.append(pltpu.make_async_copy(ep.at[rows], low.at[rows], sem.at[2 * k]))
        copies.append(pltpu.make_async_copy(em.at[pl.ds(CUT + k * SUB, SUB)], high.at[rows], sem.at[2 * k + 1]))
    for copy in copies:
        copy.start()
    for copy in copies:
        copy.wait()


def onward(ep, em, *others):
    arrays = (ep, em, *others)
    n = len(arrays)
    half = jax.ShapeDtypeStruct((CUT, ROWS), BF)
    return pl.pallas_call(
        onward_body,
        in_specs=[HBM] * n,
        out_specs=[HBM] * (n + 2),
        out_shape=[jax.ShapeDtypeStruct(a.shape, a.dtype) for a in arrays] + [half, half],
        input_output_aliases={i: i for i in range(n)},
        scratch_shapes=[pltpu.SemaphoreType.DMA((8,))],
        compiler_params=params(),
        cost_estimate=SMALL,
        name="onward",
    )(*arrays)


def gather_pieces(block, *early):
    near = [cross(block, 0, d) for d in (1, 2, 3)]
    near[2], *early = gate(near[2], *early)
    s = jnp.stack([block, *near])
    far = [cross(s, 1, d) for d in (1, 2, 3)]
    return [s] + far, *early


def logits_body(at, *refs):
    pieces, refs = refs[:8], refs[8:]
    tid, emb, e_out, st_out, loc_out, full = refs
    step = pl.program_id(0)
    x, z, c = at[0], at[1], at[2]

    @pl.when(step == 0)
    def _():
        for n in range(8):
            core = c if n < 4 else 1 - c
            row = pl.multiple_of(core * HALF, HALF)
            for b in range(4):
                dx = jnp.where(core == 0, b, n % 4)
                dz = jnp.where(core == 0, n % 4, b)
                col = pl.multiple_of((((x + dx) & 3) * 4 + ((z + dz) & 3)) * 256, 256)
                full[pl.ds(row, HALF), pl.ds(col, 256)] = pieces[n][b]
        st_out[...] = jnp.zeros((8, ROWS), F32)
        loc_out[...] = jnp.zeros((8, ROWS), F32)

    logits = dot_nt(emb[...], full[...])
    top = jnp.max(logits, axis=0, keepdims=True)
    ids = lax.broadcasted_iota(jnp.int32, logits.shape, 0) + step * TILE
    hit = jnp.sum(jnp.where(ids == tid[...], logits, 0.0), axis=0, keepdims=True)
    e = jnp.exp(logits - top)
    total = jnp.sum(e, axis=0, keepdims=True)
    e_out[...] = e.astype(BF)
    for s in range(TILES):

        @pl.when(step == s)
        def _():
            st_out[pl.ds(s, 1), :] = top

    @pl.when(step == 0)
    def _():
        loc_out[pl.ds(0, 1), :] = top
        loc_out[pl.ds(1, 1), :] = total
        loc_out[pl.ds(2, 1), :] = hit

    @pl.when(step > 0)
    def _():
        old = loc_out[pl.ds(0, 1), :]
        new = jnp.maximum(old, top)
        loc_out[pl.ds(1, 1), :] = loc_out[pl.ds(1, 1), :] * jnp.exp(old - new) + total * jnp.exp(top - new)
        loc_out[pl.ds(0, 1), :] = new
        loc_out[pl.ds(2, 1), :] = loc_out[pl.ds(2, 1), :] + hit


def logits_call(at, pieces, tid, emb):
    whole = pl.BlockSpec((8, ROWS), lambda i, at: (0, 0))
    return pl.pallas_call(
        logits_body,
        grid_spec=pltpu.PrefetchScalarGridSpec(
            num_scalar_prefetch=1,
            grid=(TILES,),
            in_specs=[pl.BlockSpec((4, HALF, 256), lambda i, at: (0, 0, 0))] * 8
            + [pl.BlockSpec((1, ROWS), lambda i, at: (0, 0)), pl.BlockSpec((TILE, WIDTH), lambda i, at: (i, 0))],
            out_specs=[
                pl.BlockSpec((TILE, ROWS), lambda i, at: (i, 0)),
                whole,
                whole,
            ],
            scratch_shapes=[pltpu.VMEM((ROWS, WIDTH), BF)],
        ),
        out_shape=[
            jax.ShapeDtypeStruct((VOC, ROWS), BF),
            jax.ShapeDtypeStruct((8, ROWS), F32),
            jax.ShapeDtypeStruct((8, ROWS), F32),
        ],
        compiler_params=params(),
        cost_estimate=SMALL,
        name="logits",
    )(at, *pieces, tid, emb)


def merge(parts):
    top = functools.reduce(jnp.maximum, [p[0:1] for p in parts])
    total = sum(p[1:2] * jnp.exp(p[0:1] - top) for p in parts)
    hit = sum(p[2:3] for p in parts)
    return top, total, hit


def merge_call(*parts):
    return jnp.concatenate([*merge(parts), jnp.zeros((5, ROWS), F32)])


def finish_body(a, b, st, tid, mix, weight, pack, grad_mix):
    top, total, hit = merge([a[...], b[...]])
    lse = top + jnp.log(total)
    gap = hit - lse
    mixes = [mix[pl.ds(k, 1), :] for k in range(4)]
    big = functools.reduce(jnp.maximum, mixes)
    norm = big + jnp.log(sum(jnp.exp(m - big) for m in mixes))
    logm = [m - norm for m in mixes]
    score = [logm[k] + gap[:, k * 128 : (k + 1) * 128] for k in range(4)]
    big = functools.reduce(jnp.maximum, score)
    ex = [jnp.exp(s - big) for s in score]
    den = sum(ex)
    w = weight[...]
    scaled = []
    for k in range(4):
        resp = ex[k] / den
        grad_mix[pl.ds(k, 1), :] = w * (jnp.exp(logm[k]) - resp)
        scaled.append(w * resp)
    d = jnp.concatenate(scaled, axis=1)
    pack[...] = jnp.zeros((8, ROWS), F32)
    pack[pl.ds(0, TILES), :] = jnp.exp(st[pl.ds(0, TILES), :] - lse) * d
    pack[pl.ds(4, 1), :] = d
    pack[pl.ds(5, 1), :] = lse
    pack[pl.ds(6, 1), :] = tid[...].astype(F32)


def finish_call(a, b, st, tid, mix, weight):
    stat = pl.BlockSpec((8, ROWS), lambda i: (0, 0))
    part = pl.BlockSpec((4, 128), lambda i: (0, 0))
    return pl.pallas_call(
        finish_body,
        grid=(1,),
        in_specs=[stat] * 3
        + [pl.BlockSpec((1, ROWS), lambda i: (0, 0)), part, pl.BlockSpec((1, 128), lambda i: (0, 0))],
        out_specs=[stat, part],
        out_shape=[
            jax.ShapeDtypeStruct((8, ROWS), F32),
            jax.ShapeDtypeStruct((4, 128), F32),
        ],
        compiler_params=params(),
        cost_estimate=SMALL,
        name="finish",
    )(a, b, st, tid, mix, weight)


def token_grad(e, pack, scale, base):
    ids = lax.broadcasted_iota(jnp.int32, e.shape, 0) + base
    tid = pack[pl.ds(6, 1), :].astype(jnp.int32)
    g = e.astype(F32) * scale
    return (g - jnp.where(ids == tid, pack[pl.ds(4, 1), :], 0.0)).astype(BF)


def hidden_body(at, e, pack, w0, w1, w2, w3, keep, send0, send1, tgt_out, tg):
    @pl.when(pl.program_id(0) == 0)
    def _():
        for t in range(VOC // SUB):
            rows = pl.ds(t * SUB, SUB)
            g = token_grad(e[rows, :], pack, pack[pl.ds(t * SUB // TILE, 1), :], t * SUB)
            tgt_out[rows, :] = g
            tg[:, rows] = g.T

    w = jnp.concatenate([w0[...], w1[...], w2[...], w3[...]], axis=1)
    r = dot_nn(tg[...], w)
    first = at[2] == 0
    for k in range(4):
        cols = slice(k * 256, (k + 1) * 256)
        a, b = r[:HALF, cols], r[HALF:, cols]
        keep[0, k] = jnp.where(first, a, b).astype(BF)
        (send0, send1)[k // 2][k % 2, 0] = jnp.where(first, b, a).astype(BF)


def hidden_call(at, e, pack, emb):
    whole = lambda s: pl.BlockSpec(s, lambda i, at: (0,) * len(s))

    def weight(k):
        def index(i, at):
            dx = jnp.where(at[2] == 0, i, k)
            dz = jnp.where(at[2] == 0, k, i)
            return (0, ((at[0] + dx) & 3) * 4 + ((at[1] + dz) & 3))

        return pl.BlockSpec((VOC, 256), index)

    return pl.pallas_call(
        hidden_body,
        grid_spec=pltpu.PrefetchScalarGridSpec(
            num_scalar_prefetch=1,
            grid=(4,),
            in_specs=[whole((VOC, ROWS)), whole((8, ROWS))] + [weight(k) for k in range(4)],
            out_specs=[
                pl.BlockSpec((1, 4, HALF, 256), lambda i, at: (i, 0, 0, 0)),
            ]
            + [pl.BlockSpec((2, 1, HALF, 256), lambda i, at: (0, i, 0, 0))] * 2
            + [
                whole((VOC, ROWS)),
            ],
            scratch_shapes=[pltpu.VMEM((ROWS, VOC), BF)],
        ),
        out_shape=[
            jax.ShapeDtypeStruct((4, 4, HALF, 256), BF),
        ]
        + [jax.ShapeDtypeStruct((2, 4, HALF, 256), BF)] * 2
        + [jax.ShapeDtypeStruct((VOC, ROWS), BF)],
        compiler_params=params(),
        cost_estimate=SMALL,
        name="hidden",
    )(at, e, pack, emb, emb, emb, emb)


def add(*xs):
    return sum(x.astype(F32) for x in xs)


def scatter(keep, recv, c, first, second, others):
    b = [add(keep[d], recv[d // 2][d % 2]) for d in range(4)]
    u = [cross(b[d].astype(BF), 0, 4 - d) for d in (1, 2, 3)]
    u1, u2, u3, work, *others = gate(*u, first(), *others)
    t = add(b[0], u1, u2, u3)
    u = [cross(t[d].astype(BF), 1, 4 - d) for d in (1, 2, 3)]
    *u, work = gate(*u, second(work, *others))
    f = add(t[0], *u)
    low, high = f[:, :128], f[:, 128:]
    mine, other = jnp.where(c == 0, low, high), jnp.where(c == 0, high, low)
    got = sibling(other)
    return jnp.where(c == 0, jnp.concatenate([mine, got]), jnp.concatenate([got, mine])), work


def feature_spec(d):
    return pl.BlockSpec((1, 4, 2, ROWS, 128), lambda i, at: ((at[3] + d) & 3, 0, 0, 0, 0))


def columns(f):
    return jnp.concatenate([f[0, k // 2, k % 2] for k in range(8)], axis=1)


def embed_a_body(at, tgt, ep, em, pack_p, pack_m, f0, f1, f3, acc):
    i = pl.program_id(0)
    parts = [tgt[...]]
    for e, pack in ((ep, pack_p), (em, pack_m)):
        parts.append(token_grad(e[...], pack, pack[pl.ds(i, 1), :], i * TILE))
    q = jnp.concatenate([columns(f) for f in (f0, f1, f3)], axis=0)
    acc[...] = dot_nn(jnp.concatenate(parts, axis=1), q).astype(BF)


def embed_a_call(at, tgt, ep, em, packs, feats):
    tile = pl.BlockSpec((TILE, ROWS), lambda i, at: (i, 0))
    pack = pl.BlockSpec((8, ROWS), lambda i, at: (0, 0))
    return pl.pallas_call(
        embed_a_body,
        grid_spec=pltpu.PrefetchScalarGridSpec(
            num_scalar_prefetch=1,
            grid=(TILES,),
            in_specs=[tile, tile, tile, pack, pack] + [feature_spec(d) for d in (0, 1, 3)],
            out_specs=pl.BlockSpec((TILE, 1024), lambda i, at: (i, 0)),
        ),
        out_shape=jax.ShapeDtypeStruct((VOC, 1024), BF),
        compiler_params=params(),
        cost_estimate=SMALL,
        name="embed_a",
    )(at, tgt, ep, em, *packs, feats, feats, feats)


def embed_b_body(at, acc, low, high, pack, f2, out):
    i = pl.program_id(0)
    e = jnp.where(i < CUT // TILE, low[...], high[...])
    g = token_grad(e, pack, pack[pl.ds(i, 1), :], i * TILE)
    out[...] = (acc[...].astype(F32) + dot_nn(g, columns(f2))).astype(BF)


def embed_b_call(at, acc, low, high, pack, feats):
    n = CUT // TILE
    return pl.pallas_call(
        embed_b_body,
        grid_spec=pltpu.PrefetchScalarGridSpec(
            num_scalar_prefetch=1,
            grid=(TILES,),
            in_specs=[
                pl.BlockSpec((TILE, 1024), lambda i, at: (i, 0)),
                pl.BlockSpec((TILE, ROWS), lambda i, at: (jnp.minimum(i, n - 1), 0)),
                pl.BlockSpec((TILE, ROWS), lambda i, at: (jnp.maximum(i - n, 0), 0)),
                pl.BlockSpec((8, ROWS), lambda i, at: (0, 0)),
                feature_spec(2),
            ],
            out_specs=pl.BlockSpec((TILE, 1024), lambda i, at: (i, 0)),
        ),
        out_shape=jax.ShapeDtypeStruct((VOC, 1024), BF),
        compiler_params=params(),
        cost_estimate=SMALL,
        name="embed_b",
    )(at, acc, low, high, pack, feats)


def local(comp_hidden, embed, mix, targets, weight):
    x, z, c, y = (lax.axis_index(a).astype(jnp.int32) for a in ("x", "z", "c", "y"))
    at = jnp.stack([x, z, c, y])
    own = comp_hidden.reshape(ROWS, 128)
    tid = jnp.tile(targets - ((x * 4 + z) * 2 + c) * VOC, 4).reshape(1, ROWS)

    swap = [(a * 4 + b, b * 4 + a) for a in range(4) for b in range(4)]
    turned = lax.ppermute(own, ("x", "y"), swap)

    low, high = own[:HALF], own[HALF:]
    mine, other = jnp.where(c == 0, low, high), jnp.where(c == 0, high, low)
    got = sibling(other)
    block = jnp.where(c == 0, jnp.concatenate([mine, got], axis=1), jnp.concatenate([got, mine], axis=1))
    pieces, at, tid = gather_pieces(block, at, tid)
    pieces = pieces + [sibling(p) for p in pieces]

    e, st, loc = logits_call(at, pieces, tid, embed)
    loc, turned = gate(loc, turned)
    feats = lax.all_gather(turned, ("x", "z", "c")).reshape(4, 4, 2, ROWS, 128)
    ep, em = shift(e, "y", 1), shift(e, "y", 3)

    s = merge_call(loc, *(shift(loc, "x", d) for d in (1, 2, 3)))
    s = merge_call(s, *(shift(s, "z", d) for d in (1, 2, 3)))
    pack, grad_mix = finish_call(s, sibling(s), st, tid, mix, weight.reshape(1, 128))
    packs = [shift(pack, "y", d) for d in (1, 3, 2)]
    keep, send0, send1, tgt = hidden_call(at, e, pack, embed)
    ep, em, send0, send1, *packs, low, high = onward(ep, em, send0, send1, *packs)
    low, high = shift(low, "y", 1), shift(high, "y", 3)
    recv = sibling(send0), sibling(send1)

    grad_hidden, grad_embed = scatter(
        keep,
        recv,
        c,
        lambda: embed_a_call(at, tgt, ep, em, packs[:2], feats),
        lambda acc, low, high: embed_b_call(at, acc, low, high, packs[2], feats),
        (low, high),
    )
    return grad_hidden.reshape(4, 128, 128), grad_embed, grad_mix


def solution(mesh):
    fine = Mesh(mesh.devices.reshape(4, 4, 2, 4), ("x", "z", "c", "y"))
    v = ("x", "z", "c")
    return jax.shard_map(
        local,
        mesh=fine,
        in_specs=(P(None, "y", v), P(v, None), P(None, "y"), P("y"), P("y")),
        out_specs=(P(None, "y", v), P(v, "y"), P(None, "y")),
        check_vma=False,
    )
```

```python
import functools

import jax
import jax.numpy as jnp
from jax import lax
from jax.experimental import pallas as pl
from jax.experimental.pallas import tpu as pltpu
from jax.sharding import Mesh, PartitionSpec as P

BF, F32 = jnp.bfloat16, jnp.float32
ROWS = 512
HALF = 256
WIDTH = 4096
VOC = 2048
TILE = 512
TILES = VOC // TILE
VMEM = 56 * 2**20


def shift(a, axis, d):
    return lax.ppermute(a, axis, [((i + d) % 4, i) for i in range(4)])


def sibling(a):
    return lax.ppermute(a, "c", [(0, 1), (1, 0)])


def cross(a, which, d):
    pairs = []
    for x in range(4):
        for z in range(4):
            for c in range(2):
                along_x = (c + which) % 2 == 0
                sx, sz = ((x + d) % 4, z) if along_x else (x, (z + d) % 4)
                pairs.append(((sx * 4 + sz) * 2 + c, (x * 4 + z) * 2 + c))
    return lax.ppermute(a, ("x", "z", "c"), pairs)


def dot_nt(a, b):
    return lax.dot_general(a, b, (((1,), (1,)), ((), ())), preferred_element_type=F32)


def dot_nn(a, b):
    return lax.dot_general(a, b, (((1,), (0,)), ((), ())), preferred_element_type=F32)


def params(**kw):
    return pltpu.CompilerParams(vmem_limit_bytes=VMEM, **kw)


SMALL = pl.CostEstimate(flops=1000, bytes_accessed=1000, transcendentals=0)
HBM = pl.BlockSpec(memory_space=pltpu.HBM)


def gate_body(*refs):
    pass


def gate(*arrays):
    n = len(arrays)
    return pl.pallas_call(
        gate_body,
        in_specs=[HBM] * n,
        out_specs=[HBM] * n,
        out_shape=[jax.ShapeDtypeStruct(a.shape, a.dtype) for a in arrays],
        input_output_aliases={i: i for i in range(n)},
        compiler_params=params(),
        cost_estimate=SMALL,
        name="gate",
    )(*arrays)


SUB = 256
CUT = VOC // 2


def onward_body(ep, em, *refs):
    low, high = refs[-2:]
    low[...] = ep[...]
    high[...] = em[...]


def onward(ep, em, *others):
    n = len(others)
    half = jax.ShapeDtypeStruct((CUT, ROWS), BF)
    part = lambda first: pl.BlockSpec((SUB, ROWS), lambda i: (i + first, 0))
    return pl.pallas_call(
        onward_body,
        grid=(CUT // SUB,),
        in_specs=[part(0), part(CUT // SUB)] + [HBM] * n,
        out_specs=[HBM] * n + [part(0), part(0)],
        out_shape=[jax.ShapeDtypeStruct(a.shape, a.dtype) for a in others] + [half, half],
        input_output_aliases={i + 2: i for i in range(n)},
        compiler_params=params(),
        cost_estimate=SMALL,
        name="onward",
    )(ep, em, *others)


def gather_pieces(block, *early):
    near = [cross(block, 0, d) for d in (1, 2, 3)]
    near[2], *early = gate(near[2], *early)
    s = jnp.stack([block, *near])
    far = [cross(s, 1, d) for d in (1, 2, 3)]
    return [s] + far, *early


def logits_body(at, *refs):
    pieces, refs = refs[:8], refs[8:]
    tid, emb, e_out, st_out, loc_out, full = refs
    step = pl.program_id(0)
    x, z, c = at[0], at[1], at[2]

    @pl.when(step == 0)
    def _():
        for n in range(8):
            core = c if n < 4 else 1 - c
            row = pl.multiple_of(core * HALF, HALF)
            for b in range(4):
                dx = jnp.where(core == 0, b, n % 4)
                dz = jnp.where(core == 0, n % 4, b)
                col = pl.multiple_of((((x + dx) & 3) * 4 + ((z + dz) & 3)) * 256, 256)
                full[pl.ds(row, HALF), pl.ds(col, 256)] = pieces[n][b]
        st_out[...] = jnp.zeros((8, ROWS), F32)
        loc_out[...] = jnp.zeros((8, ROWS), F32)

    logits = dot_nt(emb[...], full[...])
    top = jnp.max(logits, axis=0, keepdims=True)
    ids = lax.broadcasted_iota(jnp.int32, logits.shape, 0) + step * TILE
    hit = jnp.sum(jnp.where(ids == tid[...], logits, 0.0), axis=0, keepdims=True)
    e = jnp.exp(logits - top)
    total = jnp.sum(e, axis=0, keepdims=True)
    e_out[...] = e.astype(BF)
    for s in range(TILES):

        @pl.when(step == s)
        def _():
            st_out[pl.ds(s, 1), :] = top

    @pl.when(step == 0)
    def _():
        loc_out[pl.ds(0, 1), :] = top
        loc_out[pl.ds(1, 1), :] = total
        loc_out[pl.ds(2, 1), :] = hit

    @pl.when(step > 0)
    def _():
        old = loc_out[pl.ds(0, 1), :]
        new = jnp.maximum(old, top)
        loc_out[pl.ds(1, 1), :] = loc_out[pl.ds(1, 1), :] * jnp.exp(old - new) + total * jnp.exp(top - new)
        loc_out[pl.ds(0, 1), :] = new
        loc_out[pl.ds(2, 1), :] = loc_out[pl.ds(2, 1), :] + hit


def logits_call(at, pieces, tid, emb):
    whole = pl.BlockSpec((8, ROWS), lambda i, at: (0, 0))
    return pl.pallas_call(
        logits_body,
        grid_spec=pltpu.PrefetchScalarGridSpec(
            num_scalar_prefetch=1,
            grid=(TILES,),
            in_specs=[pl.BlockSpec((4, HALF, 256), lambda i, at: (0, 0, 0))] * 8
            + [pl.BlockSpec((1, ROWS), lambda i, at: (0, 0)), pl.BlockSpec((TILE, WIDTH), lambda i, at: (i, 0))],
            out_specs=[
                pl.BlockSpec((TILE, ROWS), lambda i, at: (i, 0)),
                whole,
                whole,
            ],
            scratch_shapes=[pltpu.VMEM((ROWS, WIDTH), BF)],
        ),
        out_shape=[
            jax.ShapeDtypeStruct((VOC, ROWS), BF),
            jax.ShapeDtypeStruct((8, ROWS), F32),
            jax.ShapeDtypeStruct((8, ROWS), F32),
        ],
        compiler_params=params(),
        cost_estimate=SMALL,
        name="logits",
    )(at, *pieces, tid, emb)


def merge(parts):
    top = functools.reduce(jnp.maximum, [p[0:1] for p in parts])
    total = sum(p[1:2] * jnp.exp(p[0:1] - top) for p in parts)
    hit = sum(p[2:3] for p in parts)
    return top, total, hit


def merge_call(*parts):
    return jnp.concatenate([*merge(parts), jnp.zeros((5, ROWS), F32)])


def finish_body(a, b, st, tid, mix, weight, pack, grad_mix):
    top, total, hit = merge([a[...], b[...]])
    lse = top + jnp.log(total)
    gap = hit - lse
    mixes = [mix[pl.ds(k, 1), :] for k in range(4)]
    big = functools.reduce(jnp.maximum, mixes)
    norm = big + jnp.log(sum(jnp.exp(m - big) for m in mixes))
    logm = [m - norm for m in mixes]
    score = [logm[k] + gap[:, k * 128 : (k + 1) * 128] for k in range(4)]
    big = functools.reduce(jnp.maximum, score)
    ex = [jnp.exp(s - big) for s in score]
    den = sum(ex)
    w = weight[...]
    scaled = []
    for k in range(4):
        resp = ex[k] / den
        grad_mix[pl.ds(k, 1), :] = w * (jnp.exp(logm[k]) - resp)
        scaled.append(w * resp)
    d = jnp.concatenate(scaled, axis=1)
    pack[...] = jnp.zeros((8, ROWS), F32)
    pack[pl.ds(0, TILES), :] = jnp.exp(st[pl.ds(0, TILES), :] - lse) * d
    pack[pl.ds(4, 1), :] = d
    pack[pl.ds(5, 1), :] = lse
    pack[pl.ds(6, 1), :] = tid[...].astype(F32)


def finish_call(a, b, st, tid, mix, weight):
    stat = pl.BlockSpec((8, ROWS), lambda i: (0, 0))
    part = pl.BlockSpec((4, 128), lambda i: (0, 0))
    return pl.pallas_call(
        finish_body,
        grid=(1,),
        in_specs=[stat] * 3
        + [pl.BlockSpec((1, ROWS), lambda i: (0, 0)), part, pl.BlockSpec((1, 128), lambda i: (0, 0))],
        out_specs=[stat, part],
        out_shape=[
            jax.ShapeDtypeStruct((8, ROWS), F32),
            jax.ShapeDtypeStruct((4, 128), F32),
        ],
        compiler_params=params(),
        cost_estimate=SMALL,
        name="finish",
    )(a, b, st, tid, mix, weight)


def token_grad(e, pack, scale, base):
    ids = lax.broadcasted_iota(jnp.int32, e.shape, 0) + base
    tid = pack[pl.ds(6, 1), :].astype(jnp.int32)
    g = e.astype(F32) * scale
    return (g - jnp.where(ids == tid, pack[pl.ds(4, 1), :], 0.0)).astype(BF)


def hidden_body(at, e, pack, w0, w1, w2, w3, keep, send0, send1, tgt_out, tg):
    @pl.when(pl.program_id(0) == 0)
    def _():
        for t in range(VOC // SUB):
            rows = pl.ds(t * SUB, SUB)
            g = token_grad(e[rows, :], pack, pack[pl.ds(t * SUB // TILE, 1), :], t * SUB)
            tgt_out[rows, :] = g
            tg[:, rows] = g.T

    w = jnp.concatenate([w0[...], w1[...], w2[...], w3[...]], axis=1)
    r = dot_nn(tg[...], w)
    first = at[2] == 0
    for k in range(4):
        cols = slice(k * 256, (k + 1) * 256)
        a, b = r[:HALF, cols], r[HALF:, cols]
        keep[0, k] = jnp.where(first, a, b).astype(BF)
        (send0, send1)[k // 2][k % 2, 0] = jnp.where(first, b, a).astype(BF)


def hidden_call(at, e, pack, emb):
    whole = lambda s: pl.BlockSpec(s, lambda i, at: (0,) * len(s))

    def weight(k):
        def index(i, at):
            dx = jnp.where(at[2] == 0, i, k)
            dz = jnp.where(at[2] == 0, k, i)
            return (0, ((at[0] + dx) & 3) * 4 + ((at[1] + dz) & 3))

        return pl.BlockSpec((VOC, 256), index)

    return pl.pallas_call(
        hidden_body,
        grid_spec=pltpu.PrefetchScalarGridSpec(
            num_scalar_prefetch=1,
            grid=(4,),
            in_specs=[whole((VOC, ROWS)), whole((8, ROWS))] + [weight(k) for k in range(4)],
            out_specs=[
                pl.BlockSpec((1, 4, HALF, 256), lambda i, at: (i, 0, 0, 0)),
            ]
            + [pl.BlockSpec((2, 1, HALF, 256), lambda i, at: (0, i, 0, 0))] * 2
            + [
                whole((VOC, ROWS)),
            ],
            scratch_shapes=[pltpu.VMEM((ROWS, VOC), BF)],
        ),
        out_shape=[
            jax.ShapeDtypeStruct((4, 4, HALF, 256), BF),
        ]
        + [jax.ShapeDtypeStruct((2, 4, HALF, 256), BF)] * 2
        + [jax.ShapeDtypeStruct((VOC, ROWS), BF)],
        compiler_params=params(),
        cost_estimate=SMALL,
        name="hidden",
    )(at, e, pack, emb, emb, emb, emb)


def add(*xs):
    return sum(x.astype(F32) for x in xs)


def scatter(keep, recv, c, first, second):
    b = [add(keep[d], recv[d // 2][d % 2]) for d in range(4)]
    u = [cross(b[d].astype(BF), 0, 4 - d) for d in (1, 2, 3)]
    u1, u2, u3, work = gate(*u, first())
    t = add(b[0], u1, u2, u3)
    u = [cross(t[d].astype(BF), 1, 4 - d) for d in (1, 2, 3)]
    *u, work = gate(*u, second(work))
    f = add(t[0], *u)
    low, high = f[:, :128], f[:, 128:]
    mine, other = jnp.where(c == 0, low, high), jnp.where(c == 0, high, low)
    got = sibling(other)
    return jnp.where(c == 0, jnp.concatenate([mine, got]), jnp.concatenate([got, mine])), work


def feature_spec(d):
    return pl.BlockSpec((1, 4, 2, ROWS, 128), lambda i, at: ((at[3] + d) & 3, 0, 0, 0, 0))


def columns(f):
    return jnp.concatenate([f[0, k // 2, k % 2] for k in range(8)], axis=1)


def embed_a_body(at, tgt, ep, em, pack_p, pack_m, f0, f1, f3, acc):
    i = pl.program_id(0)
    parts = [tgt[...]]
    for e, pack in ((ep, pack_p), (em, pack_m)):
        parts.append(token_grad(e[...], pack, pack[pl.ds(i, 1), :], i * TILE))
    q = jnp.concatenate([columns(f) for f in (f0, f1, f3)], axis=0)
    acc[...] = dot_nn(jnp.concatenate(parts, axis=1), q).astype(BF)


def embed_a_call(at, tgt, ep, em, packs, feats):
    tile = pl.BlockSpec((TILE, ROWS), lambda i, at: (i, 0))
    pack = pl.BlockSpec((8, ROWS), lambda i, at: (0, 0))
    return pl.pallas_call(
        embed_a_body,
        grid_spec=pltpu.PrefetchScalarGridSpec(
            num_scalar_prefetch=1,
            grid=(TILES,),
            in_specs=[tile, tile, tile, pack, pack] + [feature_spec(d) for d in (0, 1, 3)],
            out_specs=pl.BlockSpec((TILE, 1024), lambda i, at: (i, 0)),
        ),
        out_shape=jax.ShapeDtypeStruct((VOC, 1024), BF),
        compiler_params=params(),
        cost_estimate=SMALL,
        name="embed_a",
    )(at, tgt, ep, em, *packs, feats, feats, feats)


def embed_b_body(at, acc, low, high, pack, f2, out):
    i = pl.program_id(0)
    e = jnp.where(i < CUT // TILE, low[...], high[...])
    g = token_grad(e, pack, pack[pl.ds(i, 1), :], i * TILE)
    out[...] = (acc[...].astype(F32) + dot_nn(g, columns(f2))).astype(BF)


def embed_b_call(at, acc, low, high, pack, feats):
    n = CUT // TILE
    return pl.pallas_call(
        embed_b_body,
        grid_spec=pltpu.PrefetchScalarGridSpec(
            num_scalar_prefetch=1,
            grid=(TILES,),
            in_specs=[
                pl.BlockSpec((TILE, 1024), lambda i, at: (i, 0)),
                pl.BlockSpec((TILE, ROWS), lambda i, at: (jnp.minimum(i, n - 1), 0)),
                pl.BlockSpec((TILE, ROWS), lambda i, at: (jnp.maximum(i - n, 0), 0)),
                pl.BlockSpec((8, ROWS), lambda i, at: (0, 0)),
                feature_spec(2),
            ],
            out_specs=pl.BlockSpec((TILE, 1024), lambda i, at: (i, 0)),
        ),
        out_shape=jax.ShapeDtypeStruct((VOC, 1024), BF),
        compiler_params=params(),
        cost_estimate=SMALL,
        name="embed_b",
    )(at, acc, low, high, pack, feats)


def local(comp_hidden, embed, mix, targets, weight):
    x, z, c, y = (lax.axis_index(a).astype(jnp.int32) for a in ("x", "z", "c", "y"))
    at = jnp.stack([x, z, c, y])
    own = comp_hidden.reshape(ROWS, 128)
    tid = jnp.tile(targets - ((x * 4 + z) * 2 + c) * VOC, 4).reshape(1, ROWS)

    swap = [(a * 4 + b, b * 4 + a) for a in range(4) for b in range(4)]
    turned = lax.ppermute(own, ("x", "y"), swap)

    low, high = own[:HALF], own[HALF:]
    mine, other = jnp.where(c == 0, low, high), jnp.where(c == 0, high, low)
    got = sibling(other)
    block = jnp.where(c == 0, jnp.concatenate([mine, got], axis=1), jnp.concatenate([got, mine], axis=1))
    pieces, at, tid = gather_pieces(block, at, tid)
    pieces = pieces + [sibling(p) for p in pieces]

    e, st, loc = logits_call(at, pieces, tid, embed)
    loc, turned = gate(loc, turned)
    feats = lax.all_gather(turned, ("x", "z", "c")).reshape(4, 4, 2, ROWS, 128)
    ep, em = shift(e, "y", 1), shift(e, "y", 3)

    s = merge_call(loc, *(shift(loc, "x", d) for d in (1, 2, 3)))
    s = merge_call(s, *(shift(s, "z", d) for d in (1, 2, 3)))
    pack, grad_mix = finish_call(s, sibling(s), st, tid, mix, weight.reshape(1, 128))
    packs = [shift(pack, "y", d) for d in (1, 3, 2)]
    keep, send0, send1, tgt = hidden_call(at, e, pack, embed)
    pack_p, pack_m, low, high = onward(ep, em, packs[0], packs[1])
    low, high = shift(low, "y", 1), shift(high, "y", 3)
    recv = sibling(send0), sibling(send1)

    grad_hidden, grad_embed = scatter(
        keep,
        recv,
        c,
        lambda: embed_a_call(at, tgt, ep, em, (pack_p, pack_m), feats),
        lambda acc: embed_b_call(at, acc, low, high, packs[2], feats),
    )
    return grad_hidden.reshape(4, 128, 128), grad_embed, grad_mix


def solution(mesh):
    fine = Mesh(mesh.devices.reshape(4, 4, 2, 4), ("x", "z", "c", "y"))
    v = ("x", "z", "c")
    return jax.shard_map(
        local,
        mesh=fine,
        in_specs=(P(None, "y", v), P(v, None), P(None, "y"), P("y"), P("y")),
        out_specs=(P(None, "y", v), P(v, "y"), P(None, "y")),
        check_vma=False,
    )
```

```python
import functools

import jax
import jax.numpy as jnp
from jax import lax
from jax.experimental import pallas as pl
from jax.experimental.pallas import tpu as pltpu
from jax.sharding import Mesh, PartitionSpec as P

BF, F32 = jnp.bfloat16, jnp.float32
ROWS = 512
HALF = 256
WIDTH = 4096
VOC = 2048
TILE = 512
TILES = VOC // TILE
VMEM = 56 * 2**20


def shift(a, axis, d):
    return lax.ppermute(a, axis, [((i + d) % 4, i) for i in range(4)])


def sibling(a):
    return lax.ppermute(a, "c", [(0, 1), (1, 0)])


def cross(a, which, d):
    pairs = []
    for x in range(4):
        for z in range(4):
            for c in range(2):
                along_x = (c + which) % 2 == 0
                sx, sz = ((x + d) % 4, z) if along_x else (x, (z + d) % 4)
                pairs.append(((sx * 4 + sz) * 2 + c, (x * 4 + z) * 2 + c))
    return lax.ppermute(a, ("x", "z", "c"), pairs)


def dot_nt(a, b):
    return lax.dot_general(a, b, (((1,), (1,)), ((), ())), preferred_element_type=F32)


def dot_nn(a, b):
    return lax.dot_general(a, b, (((1,), (0,)), ((), ())), preferred_element_type=F32)


def params(**kw):
    return pltpu.CompilerParams(vmem_limit_bytes=VMEM, **kw)


SMALL = pl.CostEstimate(flops=1000, bytes_accessed=1000, transcendentals=0)
HBM = pl.BlockSpec(memory_space=pltpu.HBM)


def gate_body(*refs):
    pass


def gate(*arrays):
    n = len(arrays)
    return pl.pallas_call(
        gate_body,
        in_specs=[HBM] * n,
        out_specs=[HBM] * n,
        out_shape=[jax.ShapeDtypeStruct(a.shape, a.dtype) for a in arrays],
        input_output_aliases={i: i for i in range(n)},
        compiler_params=params(),
        cost_estimate=SMALL,
        name="gate",
    )(*arrays)


SUB = 256
CUT = VOC // 2


def onward_body(ep, em, *refs):
    low, high, held, get_sem, put_sem = refs[-5:]
    gets, puts = [], []
    for n in range(2 * CUT // SUB):
        k = n // 2
        rows = pl.ds(k * SUB, SUB)
        src = ep.at[rows] if n % 2 == 0 else em.at[pl.ds(CUT + k * SUB, SUB)]
        dst = (low, high)[n % 2].at[rows]
        gets.append(pltpu.make_async_copy(src, held.at[n], get_sem.at[n]))
        puts.append(pltpu.make_async_copy(held.at[n], dst, put_sem.at[n]))
    for copy in gets:
        copy.start()
    for get, put in zip(gets, puts):
        get.wait()
        put.start()
    for copy in puts:
        copy.wait()


def onward(ep, em, *others):
    n = len(others)
    chunks = 2 * CUT // SUB
    half = jax.ShapeDtypeStruct((CUT, ROWS), BF)
    return pl.pallas_call(
        onward_body,
        in_specs=[HBM] * (n + 2),
        out_specs=[HBM] * (n + 2),
        out_shape=[jax.ShapeDtypeStruct(a.shape, a.dtype) for a in others] + [half, half],
        input_output_aliases={i + 2: i for i in range(n)},
        scratch_shapes=[
            pltpu.VMEM((chunks, SUB, ROWS), BF),
            pltpu.SemaphoreType.DMA((chunks,)),
            pltpu.SemaphoreType.DMA((chunks,)),
        ],
        compiler_params=params(),
        cost_estimate=SMALL,
        name="onward",
    )(ep, em, *others)


def gather_pieces(block, *early):
    near = [cross(block, 0, d) for d in (1, 2, 3)]
    near[2], *early = gate(near[2], *early)
    s = jnp.stack([block, *near])
    far = [cross(s, 1, d) for d in (1, 2, 3)]
    return [s] + far, *early


def logits_body(at, *refs):
    pieces, refs = refs[:8], refs[8:]
    tid, emb, e_out, st_out, loc_out, full = refs
    step = pl.program_id(0)
    x, z, c = at[0], at[1], at[2]

    @pl.when(step == 0)
    def _():
        for n in range(8):
            core = c if n < 4 else 1 - c
            row = pl.multiple_of(core * HALF, HALF)
            for b in range(4):
                dx = jnp.where(core == 0, b, n % 4)
                dz = jnp.where(core == 0, n % 4, b)
                col = pl.multiple_of((((x + dx) & 3) * 4 + ((z + dz) & 3)) * 256, 256)
                full[pl.ds(row, HALF), pl.ds(col, 256)] = pieces[n][b]
        st_out[...] = jnp.zeros((8, ROWS), F32)
        loc_out[...] = jnp.zeros((8, ROWS), F32)

    logits = dot_nt(emb[...], full[...])
    top = jnp.max(logits, axis=0, keepdims=True)
    ids = lax.broadcasted_iota(jnp.int32, logits.shape, 0) + step * TILE
    hit = jnp.sum(jnp.where(ids == tid[...], logits, 0.0), axis=0, keepdims=True)
    e = jnp.exp(logits - top)
    total = jnp.sum(e, axis=0, keepdims=True)
    e_out[...] = e.astype(BF)
    for s in range(TILES):

        @pl.when(step == s)
        def _():
            st_out[pl.ds(s, 1), :] = top

    @pl.when(step == 0)
    def _():
        loc_out[pl.ds(0, 1), :] = top
        loc_out[pl.ds(1, 1), :] = total
        loc_out[pl.ds(2, 1), :] = hit

    @pl.when(step > 0)
    def _():
        old = loc_out[pl.ds(0, 1), :]
        new = jnp.maximum(old, top)
        loc_out[pl.ds(1, 1), :] = loc_out[pl.ds(1, 1), :] * jnp.exp(old - new) + total * jnp.exp(top - new)
        loc_out[pl.ds(0, 1), :] = new
        loc_out[pl.ds(2, 1), :] = loc_out[pl.ds(2, 1), :] + hit


def logits_call(at, pieces, tid, emb):
    whole = pl.BlockSpec((8, ROWS), lambda i, at: (0, 0))
    return pl.pallas_call(
        logits_body,
        grid_spec=pltpu.PrefetchScalarGridSpec(
            num_scalar_prefetch=1,
            grid=(TILES,),
            in_specs=[pl.BlockSpec((4, HALF, 256), lambda i, at: (0, 0, 0))] * 8
            + [pl.BlockSpec((1, ROWS), lambda i, at: (0, 0)), pl.BlockSpec((TILE, WIDTH), lambda i, at: (i, 0))],
            out_specs=[
                pl.BlockSpec((TILE, ROWS), lambda i, at: (i, 0)),
                whole,
                whole,
            ],
            scratch_shapes=[pltpu.VMEM((ROWS, WIDTH), BF)],
        ),
        out_shape=[
            jax.ShapeDtypeStruct((VOC, ROWS), BF),
            jax.ShapeDtypeStruct((8, ROWS), F32),
            jax.ShapeDtypeStruct((8, ROWS), F32),
        ],
        compiler_params=params(),
        cost_estimate=SMALL,
        name="logits",
    )(at, *pieces, tid, emb)


def merge(parts):
    top = functools.reduce(jnp.maximum, [p[0:1] for p in parts])
    total = sum(p[1:2] * jnp.exp(p[0:1] - top) for p in parts)
    hit = sum(p[2:3] for p in parts)
    return top, total, hit


def merge_call(*parts):
    return jnp.concatenate([*merge(parts), jnp.zeros((5, ROWS), F32)])


def finish_body(a, b, st, tid, mix, weight, pack, grad_mix):
    top, total, hit = merge([a[...], b[...]])
    lse = top + jnp.log(total)
    gap = hit - lse
    mixes = [mix[pl.ds(k, 1), :] for k in range(4)]
    big = functools.reduce(jnp.maximum, mixes)
    norm = big + jnp.log(sum(jnp.exp(m - big) for m in mixes))
    logm = [m - norm for m in mixes]
    score = [logm[k] + gap[:, k * 128 : (k + 1) * 128] for k in range(4)]
    big = functools.reduce(jnp.maximum, score)
    ex = [jnp.exp(s - big) for s in score]
    den = sum(ex)
    w = weight[...]
    scaled = []
    for k in range(4):
        resp = ex[k] / den
        grad_mix[pl.ds(k, 1), :] = w * (jnp.exp(logm[k]) - resp)
        scaled.append(w * resp)
    d = jnp.concatenate(scaled, axis=1)
    pack[...] = jnp.zeros((8, ROWS), F32)
    pack[pl.ds(0, TILES), :] = jnp.exp(st[pl.ds(0, TILES), :] - lse) * d
    pack[pl.ds(4, 1), :] = d
    pack[pl.ds(5, 1), :] = lse
    pack[pl.ds(6, 1), :] = tid[...].astype(F32)


def finish_call(a, b, st, tid, mix, weight):
    stat = pl.BlockSpec((8, ROWS), lambda i: (0, 0))
    part = pl.BlockSpec((4, 128), lambda i: (0, 0))
    return pl.pallas_call(
        finish_body,
        grid=(1,),
        in_specs=[stat] * 3
        + [pl.BlockSpec((1, ROWS), lambda i: (0, 0)), part, pl.BlockSpec((1, 128), lambda i: (0, 0))],
        out_specs=[stat, part],
        out_shape=[
            jax.ShapeDtypeStruct((8, ROWS), F32),
            jax.ShapeDtypeStruct((4, 128), F32),
        ],
        compiler_params=params(),
        cost_estimate=SMALL,
        name="finish",
    )(a, b, st, tid, mix, weight)


def token_grad(e, pack, scale, base):
    ids = lax.broadcasted_iota(jnp.int32, e.shape, 0) + base
    tid = pack[pl.ds(6, 1), :].astype(jnp.int32)
    g = e.astype(F32) * scale
    return (g - jnp.where(ids == tid, pack[pl.ds(4, 1), :], 0.0)).astype(BF)


def hidden_body(at, e, pack, w0, w1, w2, w3, keep, send0, send1, tgt_out, tg):
    @pl.when(pl.program_id(0) == 0)
    def _():
        for t in range(VOC // SUB):
            rows = pl.ds(t * SUB, SUB)
            g = token_grad(e[rows, :], pack, pack[pl.ds(t * SUB // TILE, 1), :], t * SUB)
            tgt_out[rows, :] = g
            tg[:, rows] = g.T

    w = jnp.concatenate([w0[...], w1[...], w2[...], w3[...]], axis=1)
    r = dot_nn(tg[...], w)
    first = at[2] == 0
    for k in range(4):
        cols = slice(k * 256, (k + 1) * 256)
        a, b = r[:HALF, cols], r[HALF:, cols]
        keep[0, k] = jnp.where(first, a, b).astype(BF)
        (send0, send1)[k // 2][k % 2, 0] = jnp.where(first, b, a).astype(BF)


def hidden_call(at, e, pack, emb):
    whole = lambda s: pl.BlockSpec(s, lambda i, at: (0,) * len(s))

    def weight(k):
        def index(i, at):
            dx = jnp.where(at[2] == 0, i, k)
            dz = jnp.where(at[2] == 0, k, i)
            return (0, ((at[0] + dx) & 3) * 4 + ((at[1] + dz) & 3))

        return pl.BlockSpec((VOC, 256), index)

    return pl.pallas_call(
        hidden_body,
        grid_spec=pltpu.PrefetchScalarGridSpec(
            num_scalar_prefetch=1,
            grid=(4,),
            in_specs=[whole((VOC, ROWS)), whole((8, ROWS))] + [weight(k) for k in range(4)],
            out_specs=[
                pl.BlockSpec((1, 4, HALF, 256), lambda i, at: (i, 0, 0, 0)),
            ]
            + [pl.BlockSpec((2, 1, HALF, 256), lambda i, at: (0, i, 0, 0))] * 2
            + [
                whole((VOC, ROWS)),
            ],
            scratch_shapes=[pltpu.VMEM((ROWS, VOC), BF)],
        ),
        out_shape=[
            jax.ShapeDtypeStruct((4, 4, HALF, 256), BF),
        ]
        + [jax.ShapeDtypeStruct((2, 4, HALF, 256), BF)] * 2
        + [jax.ShapeDtypeStruct((VOC, ROWS), BF)],
        compiler_params=params(),
        cost_estimate=SMALL,
        name="hidden",
    )(at, e, pack, emb, emb, emb, emb)


def add(*xs):
    return sum(x.astype(F32) for x in xs)


def scatter(keep, recv, c, first, second):
    b = [add(keep[d], recv[d // 2][d % 2]) for d in range(4)]
    u = [cross(b[d].astype(BF), 0, 4 - d) for d in (1, 2, 3)]
    u1, u2, u3, work = gate(*u, first())
    t = add(b[0], u1, u2, u3)
    u = [cross(t[d].astype(BF), 1, 4 - d) for d in (1, 2, 3)]
    *u, work = gate(*u, second(work))
    f = add(t[0], *u)
    low, high = f[:, :128], f[:, 128:]
    mine, other = jnp.where(c == 0, low, high), jnp.where(c == 0, high, low)
    got = sibling(other)
    return jnp.where(c == 0, jnp.concatenate([mine, got]), jnp.concatenate([got, mine])), work


def feature_spec(d):
    return pl.BlockSpec((1, 4, 2, ROWS, 128), lambda i, at: ((at[3] + d) & 3, 0, 0, 0, 0))


def columns(f):
    return jnp.concatenate([f[0, k // 2, k % 2] for k in range(8)], axis=1)


def embed_a_body(at, tgt, ep, em, pack_p, pack_m, f0, f1, f3, acc):
    i = pl.program_id(0)
    parts = [tgt[...]]
    for e, pack in ((ep, pack_p), (em, pack_m)):
        parts.append(token_grad(e[...], pack, pack[pl.ds(i, 1), :], i * TILE))
    q = jnp.concatenate([columns(f) for f in (f0, f1, f3)], axis=0)
    acc[...] = dot_nn(jnp.concatenate(parts, axis=1), q).astype(BF)


def embed_a_call(at, tgt, ep, em, packs, feats):
    tile = pl.BlockSpec((TILE, ROWS), lambda i, at: (i, 0))
    pack = pl.BlockSpec((8, ROWS), lambda i, at: (0, 0))
    return pl.pallas_call(
        embed_a_body,
        grid_spec=pltpu.PrefetchScalarGridSpec(
            num_scalar_prefetch=1,
            grid=(TILES,),
            in_specs=[tile, tile, tile, pack, pack] + [feature_spec(d) for d in (0, 1, 3)],
            out_specs=pl.BlockSpec((TILE, 1024), lambda i, at: (i, 0)),
        ),
        out_shape=jax.ShapeDtypeStruct((VOC, 1024), BF),
        compiler_params=params(),
        cost_estimate=SMALL,
        name="embed_a",
    )(at, tgt, ep, em, *packs, feats, feats, feats)


def embed_b_body(at, acc, low, high, pack, f2, out):
    i = pl.program_id(0)
    e = jnp.where(i < CUT // TILE, low[...], high[...])
    g = token_grad(e, pack, pack[pl.ds(i, 1), :], i * TILE)
    out[...] = (acc[...].astype(F32) + dot_nn(g, columns(f2))).astype(BF)


def embed_b_call(at, acc, low, high, pack, feats):
    n = CUT // TILE
    return pl.pallas_call(
        embed_b_body,
        grid_spec=pltpu.PrefetchScalarGridSpec(
            num_scalar_prefetch=1,
            grid=(TILES,),
            in_specs=[
                pl.BlockSpec((TILE, 1024), lambda i, at: (i, 0)),
                pl.BlockSpec((TILE, ROWS), lambda i, at: (jnp.minimum(i, n - 1), 0)),
                pl.BlockSpec((TILE, ROWS), lambda i, at: (jnp.maximum(i - n, 0), 0)),
                pl.BlockSpec((8, ROWS), lambda i, at: (0, 0)),
                feature_spec(2),
            ],
            out_specs=pl.BlockSpec((TILE, 1024), lambda i, at: (i, 0)),
        ),
        out_shape=jax.ShapeDtypeStruct((VOC, 1024), BF),
        compiler_params=params(),
        cost_estimate=SMALL,
        name="embed_b",
    )(at, acc, low, high, pack, feats)


def local(comp_hidden, embed, mix, targets, weight):
    x, z, c, y = (lax.axis_index(a).astype(jnp.int32) for a in ("x", "z", "c", "y"))
    at = jnp.stack([x, z, c, y])
    own = comp_hidden.reshape(ROWS, 128)
    tid = jnp.tile(targets - ((x * 4 + z) * 2 + c) * VOC, 4).reshape(1, ROWS)

    swap = [(a * 4 + b, b * 4 + a) for a in range(4) for b in range(4)]
    turned = lax.ppermute(own, ("x", "y"), swap)

    low, high = own[:HALF], own[HALF:]
    mine, other = jnp.where(c == 0, low, high), jnp.where(c == 0, high, low)
    got = sibling(other)
    block = jnp.where(c == 0, jnp.concatenate([mine, got], axis=1), jnp.concatenate([got, mine], axis=1))
    pieces, at, tid = gather_pieces(block, at, tid)
    pieces = pieces + [sibling(p) for p in pieces]

    e, st, loc = logits_call(at, pieces, tid, embed)
    loc, turned = gate(loc, turned)
    feats = lax.all_gather(turned, ("x", "z", "c")).reshape(4, 4, 2, ROWS, 128)
    ep, em = shift(e, "y", 1), shift(e, "y", 3)

    s = merge_call(loc, *(shift(loc, "x", d) for d in (1, 2, 3)))
    s = merge_call(s, *(shift(s, "z", d) for d in (1, 2, 3)))
    pack, grad_mix = finish_call(s, sibling(s), st, tid, mix, weight.reshape(1, 128))
    packs = [shift(pack, "y", d) for d in (1, 3, 2)]
    keep, *send, tgt = hidden_call(at, e, pack, embed)
    pack_p, pack_m, low, high = onward(ep, em, packs[0], packs[1])
    low, high = shift(low, "y", 1), shift(high, "y", 3)

    grad_hidden, grad_embed = scatter(
        keep,
        [sibling(t) for t in send],
        c,
        lambda: embed_a_call(at, tgt, ep, em, (pack_p, pack_m), feats),
        lambda acc: embed_b_call(at, acc, low, high, packs[2], feats),
    )
    return grad_hidden.reshape(4, 128, 128), grad_embed, grad_mix


def solution(mesh):
    fine = Mesh(mesh.devices.reshape(4, 4, 2, 4), ("x", "z", "c", "y"))
    v = ("x", "z", "c")
    return jax.shard_map(
        local,
        mesh=fine,
        in_specs=(P(None, "y", v), P(v, None), P(None, "y"), P("y"), P("y")),
        out_specs=(P(None, "y", v), P(v, "y"), P(None, "y")),
        check_vma=False,
    )
```

```python
import functools

import jax
import jax.numpy as jnp
from jax import lax
from jax.experimental import pallas as pl
from jax.experimental.pallas import tpu as pltpu
from jax.sharding import Mesh, PartitionSpec as P

BF, F32 = jnp.bfloat16, jnp.float32
ROWS = 512
HALF = 256
WIDTH = 4096
VOC = 2048
TILE = 512
TILES = VOC // TILE
VMEM = 56 * 2**20
MOST = 63 * 2**20


def shift(a, axis, d):
    return lax.ppermute(a, axis, [((i + d) % 4, i) for i in range(4)])


def sibling(a):
    return lax.ppermute(a, "c", [(0, 1), (1, 0)])


def cross(a, which, d):
    pairs = []
    for x in range(4):
        for z in range(4):
            for c in range(2):
                along_x = (c + which) % 2 == 0
                sx, sz = ((x + d) % 4, z) if along_x else (x, (z + d) % 4)
                pairs.append(((sx * 4 + sz) * 2 + c, (x * 4 + z) * 2 + c))
    return lax.ppermute(a, ("x", "z", "c"), pairs)


def dot_nt(a, b):
    return lax.dot_general(a, b, (((1,), (1,)), ((), ())), preferred_element_type=F32)


def dot_nn(a, b):
    return lax.dot_general(a, b, (((1,), (0,)), ((), ())), preferred_element_type=F32)


def params(limit=VMEM):
    return pltpu.CompilerParams(vmem_limit_bytes=limit)


SMALL = pl.CostEstimate(flops=1000, bytes_accessed=1000, transcendentals=0)
HBM = pl.BlockSpec(memory_space=pltpu.HBM)


def gate_body(*refs):
    pass


def gate(*arrays):
    n = len(arrays)
    return pl.pallas_call(
        gate_body,
        in_specs=[HBM] * n,
        out_specs=[HBM] * n,
        out_shape=[jax.ShapeDtypeStruct(a.shape, a.dtype) for a in arrays],
        input_output_aliases={i: i for i in range(n)},
        compiler_params=params(),
        cost_estimate=SMALL,
        name="gate",
    )(*arrays)


SUB = 256
CUT = VOC // 2


def onward_body(ep, em, *refs):
    low, high, held, get_sem, put_sem = refs[-5:]
    gets, puts = [], []
    for n in range(2 * CUT // SUB):
        k = n // 2
        rows = pl.ds(k * SUB, SUB)
        src = ep.at[rows] if n % 2 == 0 else em.at[pl.ds(CUT + k * SUB, SUB)]
        dst = (low, high)[n % 2].at[rows]
        gets.append(pltpu.make_async_copy(src, held.at[n], get_sem.at[n]))
        puts.append(pltpu.make_async_copy(held.at[n], dst, put_sem.at[n]))
    for copy in gets:
        copy.start()
    for get, put in zip(gets, puts):
        get.wait()
        put.start()
    for copy in puts:
        copy.wait()


def onward(ep, em, *others):
    n = len(others)
    chunks = 2 * CUT // SUB
    half = jax.ShapeDtypeStruct((CUT, ROWS), BF)
    return pl.pallas_call(
        onward_body,
        in_specs=[HBM] * (n + 2),
        out_specs=[HBM] * (n + 2),
        out_shape=[jax.ShapeDtypeStruct(a.shape, a.dtype) for a in others] + [half, half],
        input_output_aliases={i + 2: i for i in range(n)},
        scratch_shapes=[
            pltpu.VMEM((chunks, SUB, ROWS), BF),
            pltpu.SemaphoreType.DMA((chunks,)),
            pltpu.SemaphoreType.DMA((chunks,)),
        ],
        compiler_params=params(MOST),
        cost_estimate=SMALL,
        name="onward",
    )(ep, em, *others)


def gather_pieces(block, *early):
    near = [cross(block, 0, d) for d in (1, 2, 3)]
    near[2], *early = gate(near[2], *early)
    s = jnp.stack([block, *near])
    far = [cross(s, 1, d) for d in (1, 2, 3)]
    return [s] + far, *early


def logits_body(at, *refs):
    pieces, refs = refs[:8], refs[8:]
    tid, emb, e_out, st_out, loc_out, full = refs
    step = pl.program_id(0)
    x, z, c = at[0], at[1], at[2]

    @pl.when(step == 0)
    def _():
        for n in range(8):
            core = c if n < 4 else 1 - c
            row = pl.multiple_of(core * HALF, HALF)
            for b in range(4):
                dx = jnp.where(core == 0, b, n % 4)
                dz = jnp.where(core == 0, n % 4, b)
                col = pl.multiple_of((((x + dx) & 3) * 4 + ((z + dz) & 3)) * 256, 256)
                full[pl.ds(row, HALF), pl.ds(col, 256)] = pieces[n][b]
        st_out[...] = jnp.zeros((8, ROWS), F32)
        loc_out[...] = jnp.zeros((8, ROWS), F32)

    logits = dot_nt(emb[...], full[...])
    top = jnp.max(logits, axis=0, keepdims=True)
    ids = lax.broadcasted_iota(jnp.int32, logits.shape, 0) + step * TILE
    hit = jnp.sum(jnp.where(ids == tid[...], logits, 0.0), axis=0, keepdims=True)
    e = jnp.exp(logits - top)
    total = jnp.sum(e, axis=0, keepdims=True)
    e_out[...] = e.astype(BF)
    for s in range(TILES):

        @pl.when(step == s)
        def _():
            st_out[pl.ds(s, 1), :] = top

    @pl.when(step == 0)
    def _():
        loc_out[pl.ds(0, 1), :] = top
        loc_out[pl.ds(1, 1), :] = total
        loc_out[pl.ds(2, 1), :] = hit

    @pl.when(step > 0)
    def _():
        old = loc_out[pl.ds(0, 1), :]
        new = jnp.maximum(old, top)
        loc_out[pl.ds(1, 1), :] = loc_out[pl.ds(1, 1), :] * jnp.exp(old - new) + total * jnp.exp(top - new)
        loc_out[pl.ds(0, 1), :] = new
        loc_out[pl.ds(2, 1), :] = loc_out[pl.ds(2, 1), :] + hit


def logits_call(at, pieces, tid, emb):
    whole = pl.BlockSpec((8, ROWS), lambda i, at: (0, 0))
    return pl.pallas_call(
        logits_body,
        grid_spec=pltpu.PrefetchScalarGridSpec(
            num_scalar_prefetch=1,
            grid=(TILES,),
            in_specs=[pl.BlockSpec((4, HALF, 256), lambda i, at: (0, 0, 0))] * 8
            + [pl.BlockSpec((1, ROWS), lambda i, at: (0, 0)), pl.BlockSpec((TILE, WIDTH), lambda i, at: (i, 0))],
            out_specs=[
                pl.BlockSpec((TILE, ROWS), lambda i, at: (i, 0)),
                whole,
                whole,
            ],
            scratch_shapes=[pltpu.VMEM((ROWS, WIDTH), BF)],
        ),
        out_shape=[
            jax.ShapeDtypeStruct((VOC, ROWS), BF),
            jax.ShapeDtypeStruct((8, ROWS), F32),
            jax.ShapeDtypeStruct((8, ROWS), F32),
        ],
        compiler_params=params(),
        cost_estimate=SMALL,
        name="logits",
    )(at, *pieces, tid, emb)


def merge(parts):
    top = functools.reduce(jnp.maximum, [p[0:1] for p in parts])
    total = sum(p[1:2] * jnp.exp(p[0:1] - top) for p in parts)
    hit = sum(p[2:3] for p in parts)
    return top, total, hit


def merge_call(*parts):
    return jnp.concatenate([*merge(parts), jnp.zeros((5, ROWS), F32)])


def finish_body(a, b, st, tid, mix, weight, pack, grad_mix):
    top, total, hit = merge([a[...], b[...]])
    lse = top + jnp.log(total)
    gap = hit - lse
    mixes = [mix[pl.ds(k, 1), :] for k in range(4)]
    big = functools.reduce(jnp.maximum, mixes)
    norm = big + jnp.log(sum(jnp.exp(m - big) for m in mixes))
    logm = [m - norm for m in mixes]
    score = [logm[k] + gap[:, k * 128 : (k + 1) * 128] for k in range(4)]
    big = functools.reduce(jnp.maximum, score)
    ex = [jnp.exp(s - big) for s in score]
    den = sum(ex)
    w = weight[...]
    scaled = []
    for k in range(4):
        resp = ex[k] / den
        grad_mix[pl.ds(k, 1), :] = w * (jnp.exp(logm[k]) - resp)
        scaled.append(w * resp)
    d = jnp.concatenate(scaled, axis=1)
    pack[...] = jnp.zeros((8, ROWS), F32)
    pack[pl.ds(0, TILES), :] = jnp.exp(st[pl.ds(0, TILES), :] - lse) * d
    pack[pl.ds(4, 1), :] = d
    pack[pl.ds(5, 1), :] = lse
    pack[pl.ds(6, 1), :] = tid[...].astype(F32)


def finish_call(a, b, st, tid, mix, weight):
    stat = pl.BlockSpec((8, ROWS), lambda i: (0, 0))
    part = pl.BlockSpec((4, 128), lambda i: (0, 0))
    return pl.pallas_call(
        finish_body,
        grid=(1,),
        in_specs=[stat] * 3
        + [pl.BlockSpec((1, ROWS), lambda i: (0, 0)), part, pl.BlockSpec((1, 128), lambda i: (0, 0))],
        out_specs=[stat, part],
        out_shape=[
            jax.ShapeDtypeStruct((8, ROWS), F32),
            jax.ShapeDtypeStruct((4, 128), F32),
        ],
        compiler_params=params(),
        cost_estimate=SMALL,
        name="finish",
    )(a, b, st, tid, mix, weight)


def token_grad(e, pack, scale, base):
    ids = lax.broadcasted_iota(jnp.int32, e.shape, 0) + base
    tid = pack[pl.ds(6, 1), :].astype(jnp.int32)
    g = e.astype(F32) * scale
    return (g - jnp.where(ids == tid, pack[pl.ds(4, 1), :], 0.0)).astype(BF)


def hidden_body(at, e, pack, w0, w1, w2, w3, keep, send0, send1, tgt_out, tg):
    @pl.when(pl.program_id(0) == 0)
    def _():
        for t in range(VOC // SUB):
            rows = pl.ds(t * SUB, SUB)
            g = token_grad(e[rows, :], pack, pack[pl.ds(t * SUB // TILE, 1), :], t * SUB)
            tgt_out[rows, :] = g
            tg[:, rows] = g.T

    w = jnp.concatenate([w0[...], w1[...], w2[...], w3[...]], axis=1)
    r = dot_nn(tg[...], w)
    first = at[2] == 0
    for k in range(4):
        cols = slice(k * 256, (k + 1) * 256)
        a, b = r[:HALF, cols], r[HALF:, cols]
        keep[0, k] = jnp.where(first, a, b).astype(BF)
        (send0, send1)[k // 2][k % 2, 0] = jnp.where(first, b, a).astype(BF)


def hidden_call(at, e, pack, emb):
    whole = lambda s: pl.BlockSpec(s, lambda i, at: (0,) * len(s))

    def weight(k):
        def index(i, at):
            dx = jnp.where(at[2] == 0, i, k)
            dz = jnp.where(at[2] == 0, k, i)
            return (0, ((at[0] + dx) & 3) * 4 + ((at[1] + dz) & 3))

        return pl.BlockSpec((VOC, 256), index)

    return pl.pallas_call(
        hidden_body,
        grid_spec=pltpu.PrefetchScalarGridSpec(
            num_scalar_prefetch=1,
            grid=(4,),
            in_specs=[whole((VOC, ROWS)), whole((8, ROWS))] + [weight(k) for k in range(4)],
            out_specs=[
                pl.BlockSpec((1, 4, HALF, 256), lambda i, at: (i, 0, 0, 0)),
            ]
            + [pl.BlockSpec((2, 1, HALF, 256), lambda i, at: (0, i, 0, 0))] * 2
            + [
                whole((VOC, ROWS)),
            ],
            scratch_shapes=[pltpu.VMEM((ROWS, VOC), BF)],
        ),
        out_shape=[
            jax.ShapeDtypeStruct((4, 4, HALF, 256), BF),
        ]
        + [jax.ShapeDtypeStruct((2, 4, HALF, 256), BF)] * 2
        + [jax.ShapeDtypeStruct((VOC, ROWS), BF)],
        compiler_params=params(),
        cost_estimate=SMALL,
        name="hidden",
    )(at, e, pack, emb, emb, emb, emb)


def add(*xs):
    return sum(x.astype(F32) for x in xs)


def second_sum_body(at, t, u1, u2, u3, _, mine, other, _out):
    total = add(t[0], u1[...], u2[...], u3[...])
    low, high = total[:, :128], total[:, 128:]
    first = at[2] == 0
    mine[...] = jnp.where(first, low, high)
    other[...] = jnp.where(first, high, low)


def second_sum(at, t, us, work):
    part = pl.BlockSpec((HALF, 256), lambda i, at: (0, 0))
    out = pl.BlockSpec((HALF, 128), lambda i, at: (0, 0))
    return pl.pallas_call(
        second_sum_body,
        grid_spec=pltpu.PrefetchScalarGridSpec(
            num_scalar_prefetch=1,
            grid=(1,),
            in_specs=[pl.BlockSpec((1, HALF, 256), lambda i, at: (0, 0, 0)), part, part, part, HBM],
            out_specs=[out, out, HBM],
        ),
        out_shape=[jax.ShapeDtypeStruct((HALF, 128), F32)] * 2 + [jax.ShapeDtypeStruct(work.shape, work.dtype)],
        input_output_aliases={5: 2},
        compiler_params=params(MOST),
        cost_estimate=SMALL,
        name="second_sum",
    )(at, t, *us, work)


def scatter(at, keep, recv, c, first, second):
    b = [add(keep[d], recv[d // 2][d % 2]) for d in range(4)]
    u = [cross(b[d].astype(BF), 0, 4 - d) for d in (1, 2, 3)]
    u1, u2, u3, work = gate(*u, first())
    t = add(b[0], u1, u2, u3)
    u = [cross(t[d].astype(BF), 1, 4 - d) for d in (1, 2, 3)]
    mine, other, work = second_sum(at, t, u, second(work))
    got = sibling(other)
    return jnp.where(c == 0, jnp.concatenate([mine, got]), jnp.concatenate([got, mine])), work


def feature_spec(d):
    return pl.BlockSpec((1, 4, 2, ROWS, 128), lambda i, at: ((at[3] + d) & 3, 0, 0, 0, 0))


def columns(f):
    return jnp.concatenate([f[0, k // 2, k % 2] for k in range(8)], axis=1)


def embed_a_body(at, tgt, ep, em, pack_p, pack_m, f0, f1, f3, acc):
    i = pl.program_id(0)
    parts = [tgt[...]]
    for e, pack in ((ep, pack_p), (em, pack_m)):
        parts.append(token_grad(e[...], pack, pack[pl.ds(i, 1), :], i * TILE))
    q = jnp.concatenate([columns(f) for f in (f0, f1, f3)], axis=0)
    acc[...] = dot_nn(jnp.concatenate(parts, axis=1), q).astype(BF)


def embed_a_call(at, tgt, ep, em, packs, feats):
    tile = pl.BlockSpec((TILE, ROWS), lambda i, at: (i, 0))
    pack = pl.BlockSpec((8, ROWS), lambda i, at: (0, 0))
    return pl.pallas_call(
        embed_a_body,
        grid_spec=pltpu.PrefetchScalarGridSpec(
            num_scalar_prefetch=1,
            grid=(TILES,),
            in_specs=[tile, tile, tile, pack, pack] + [feature_spec(d) for d in (0, 1, 3)],
            out_specs=pl.BlockSpec((TILE, 1024), lambda i, at: (i, 0)),
        ),
        out_shape=jax.ShapeDtypeStruct((VOC, 1024), BF),
        compiler_params=params(MOST),
        cost_estimate=SMALL,
        name="embed_a",
    )(at, tgt, ep, em, *packs, feats, feats, feats)


def embed_b_body(at, acc, low, high, pack, f2, out):
    i = pl.program_id(0)
    e = jnp.where(i < CUT // TILE, low[...], high[...])
    g = token_grad(e, pack, pack[pl.ds(i, 1), :], i * TILE)
    out[...] = (acc[...].astype(F32) + dot_nn(g, columns(f2))).astype(BF)


def embed_b_call(at, acc, low, high, pack, feats):
    n = CUT // TILE
    return pl.pallas_call(
        embed_b_body,
        grid_spec=pltpu.PrefetchScalarGridSpec(
            num_scalar_prefetch=1,
            grid=(TILES,),
            in_specs=[
                pl.BlockSpec((TILE, 1024), lambda i, at: (i, 0)),
                pl.BlockSpec((TILE, ROWS), lambda i, at: (jnp.minimum(i, n - 1), 0)),
                pl.BlockSpec((TILE, ROWS), lambda i, at: (jnp.maximum(i - n, 0), 0)),
                pl.BlockSpec((8, ROWS), lambda i, at: (0, 0)),
                feature_spec(2),
            ],
            out_specs=pl.BlockSpec((TILE, 1024), lambda i, at: (i, 0)),
        ),
        out_shape=jax.ShapeDtypeStruct((VOC, 1024), BF),
        compiler_params=params(MOST),
        cost_estimate=SMALL,
        name="embed_b",
    )(at, acc, low, high, pack, feats)


def local(comp_hidden, embed, mix, targets, weight):
    x, z, c, y = (lax.axis_index(a).astype(jnp.int32) for a in ("x", "z", "c", "y"))
    at = jnp.stack([x, z, c, y])
    own = comp_hidden.reshape(ROWS, 128)
    tid = jnp.tile(targets - ((x * 4 + z) * 2 + c) * VOC, 4).reshape(1, ROWS)

    swap = [(a * 4 + b, b * 4 + a) for a in range(4) for b in range(4)]
    turned = lax.ppermute(own, ("x", "y"), swap)

    low, high = own[:HALF], own[HALF:]
    mine, other = jnp.where(c == 0, low, high), jnp.where(c == 0, high, low)
    got = sibling(other)
    block = jnp.where(c == 0, jnp.concatenate([mine, got], axis=1), jnp.concatenate([got, mine], axis=1))
    pieces, at, tid = gather_pieces(block, at, tid)
    pieces = pieces + [sibling(p) for p in pieces]

    e, st, loc = logits_call(at, pieces, tid, embed)
    loc, turned = gate(loc, turned)
    feats = lax.all_gather(turned, ("x", "z", "c")).reshape(4, 4, 2, ROWS, 128)
    ep, em = shift(e, "y", 1), shift(e, "y", 3)

    s = merge_call(loc, *(shift(loc, "x", d) for d in (1, 2, 3)))
    s = merge_call(s, *(shift(s, "z", d) for d in (1, 2, 3)))
    pack, grad_mix = finish_call(s, sibling(s), st, tid, mix, weight.reshape(1, 128))
    packs = [shift(pack, "y", d) for d in (1, 3, 2)]
    keep, *send, tgt = hidden_call(at, e, pack, embed)
    pack_p, pack_m, low, high = onward(ep, em, packs[0], packs[1])
    low, high = shift(low, "y", 1), shift(high, "y", 3)

    grad_hidden, grad_embed = scatter(
        at,
        keep,
        [sibling(t) for t in send],
        c,
        lambda: embed_a_call(at, tgt, ep, em, (pack_p, pack_m), feats),
        lambda acc: embed_b_call(at, acc, low, high, packs[2], feats),
    )
    return grad_hidden.reshape(4, 128, 128), grad_embed, grad_mix


def solution(mesh):
    fine = Mesh(mesh.devices.reshape(4, 4, 2, 4), ("x", "z", "c", "y"))
    v = ("x", "z", "c")
    return jax.shard_map(
        local,
        mesh=fine,
        in_specs=(P(None, "y", v), P(v, None), P(None, "y"), P("y"), P("y")),
        out_specs=(P(None, "y", v), P(v, "y"), P(None, "y")),
        check_vma=False,
    )
```

```python
import functools

import jax
import jax.numpy as jnp
from jax import lax
from jax.experimental import pallas as pl
from jax.experimental.pallas import tpu as pltpu
from jax.sharding import Mesh, PartitionSpec as P

BF, F32 = jnp.bfloat16, jnp.float32
ROWS = 512
HALF = 256
WIDTH = 4096
VOC = 2048
TILE = 512
TILES = VOC // TILE
VMEM = 56 * 2**20
MOST = 63 * 2**20


def shift(a, axis, d):
    return lax.ppermute(a, axis, [((i + d) % 4, i) for i in range(4)])


def sibling(a):
    return lax.ppermute(a, "c", [(0, 1), (1, 0)])


def cross(a, which, d):
    pairs = []
    for x in range(4):
        for z in range(4):
            for c in range(2):
                along_x = (c + which) % 2 == 0
                sx, sz = ((x + d) % 4, z) if along_x else (x, (z + d) % 4)
                pairs.append(((sx * 4 + sz) * 2 + c, (x * 4 + z) * 2 + c))
    return lax.ppermute(a, ("x", "z", "c"), pairs)


def dot_nt(a, b):
    return lax.dot_general(a, b, (((1,), (1,)), ((), ())), preferred_element_type=F32)


def dot_nn(a, b):
    return lax.dot_general(a, b, (((1,), (0,)), ((), ())), preferred_element_type=F32)


def params(limit=VMEM):
    return pltpu.CompilerParams(vmem_limit_bytes=limit)


SMALL = pl.CostEstimate(flops=1000, bytes_accessed=1000, transcendentals=0)
HBM = pl.BlockSpec(memory_space=pltpu.HBM)


def gate_body(*refs):
    pass


def gate(*arrays):
    n = len(arrays)
    return pl.pallas_call(
        gate_body,
        in_specs=[HBM] * n,
        out_specs=[HBM] * n,
        out_shape=[jax.ShapeDtypeStruct(a.shape, a.dtype) for a in arrays],
        input_output_aliases={i: i for i in range(n)},
        compiler_params=params(),
        cost_estimate=SMALL,
        name="gate",
    )(*arrays)


SUB = 256
CUT = VOC // 2


def onward_body(ep, em, *refs):
    low, high, held, get_sem, put_sem = refs[-5:]
    gets, puts = [], []
    for n in range(2 * CUT // SUB):
        k = n // 2
        rows = pl.ds(k * SUB, SUB)
        src = ep.at[rows] if n % 2 == 0 else em.at[pl.ds(CUT + k * SUB, SUB)]
        dst = (low, high)[n % 2].at[rows]
        gets.append(pltpu.make_async_copy(src, held.at[n], get_sem.at[n]))
        puts.append(pltpu.make_async_copy(held.at[n], dst, put_sem.at[n]))
    for copy in gets:
        copy.start()
    for get, put in zip(gets, puts):
        get.wait()
        put.start()
    for copy in puts:
        copy.wait()


def onward(ep, em, *others):
    n = len(others)
    chunks = 2 * CUT // SUB
    half = jax.ShapeDtypeStruct((CUT, ROWS), BF)
    return pl.pallas_call(
        onward_body,
        in_specs=[HBM] * (n + 2),
        out_specs=[HBM] * (n + 2),
        out_shape=[jax.ShapeDtypeStruct(a.shape, a.dtype) for a in others] + [half, half],
        input_output_aliases={i + 2: i for i in range(n)},
        scratch_shapes=[
            pltpu.VMEM((chunks, SUB, ROWS), BF),
            pltpu.SemaphoreType.DMA((chunks,)),
            pltpu.SemaphoreType.DMA((chunks,)),
        ],
        compiler_params=params(MOST),
        cost_estimate=SMALL,
        name="onward",
    )(ep, em, *others)


def gather_pieces(block, *early):
    near = [cross(block, 0, d) for d in (1, 2, 3)]
    near[2], *early = gate(near[2], *early)
    s = jnp.stack([block, *near])
    far = [cross(s, 1, d) for d in (1, 2, 3)]
    return [s] + far, *early


def logits_body(at, *refs):
    pieces, refs = refs[:8], refs[8:]
    tid, emb, e_out, st_out, loc_out, full = refs
    step = pl.program_id(0)
    x, z, c = at[0], at[1], at[2]

    @pl.when(step == 0)
    def _():
        for n in range(8):
            core = c if n < 4 else 1 - c
            row = pl.multiple_of(core * HALF, HALF)
            for b in range(4):
                dx = jnp.where(core == 0, b, n % 4)
                dz = jnp.where(core == 0, n % 4, b)
                col = pl.multiple_of((((x + dx) & 3) * 4 + ((z + dz) & 3)) * 256, 256)
                full[pl.ds(row, HALF), pl.ds(col, 256)] = pieces[n][b]
        st_out[...] = jnp.zeros((8, ROWS), F32)
        loc_out[...] = jnp.zeros((8, ROWS), F32)

    logits = dot_nt(emb[...], full[...])
    top = jnp.max(logits, axis=0, keepdims=True)
    ids = lax.broadcasted_iota(jnp.int32, logits.shape, 0) + step * TILE
    hit = jnp.sum(jnp.where(ids == tid[...], logits, 0.0), axis=0, keepdims=True)
    e = jnp.exp(logits - top)
    total = jnp.sum(e, axis=0, keepdims=True)
    e_out[...] = e.astype(BF)
    for s in range(TILES):

        @pl.when(step == s)
        def _():
            st_out[pl.ds(s, 1), :] = top

    @pl.when(step == 0)
    def _():
        loc_out[pl.ds(0, 1), :] = top
        loc_out[pl.ds(1, 1), :] = total
        loc_out[pl.ds(2, 1), :] = hit

    @pl.when(step > 0)
    def _():
        old = loc_out[pl.ds(0, 1), :]
        new = jnp.maximum(old, top)
        loc_out[pl.ds(1, 1), :] = loc_out[pl.ds(1, 1), :] * jnp.exp(old - new) + total * jnp.exp(top - new)
        loc_out[pl.ds(0, 1), :] = new
        loc_out[pl.ds(2, 1), :] = loc_out[pl.ds(2, 1), :] + hit


def logits_call(at, pieces, tid, emb):
    whole = pl.BlockSpec((8, ROWS), lambda i, at: (0, 0))
    return pl.pallas_call(
        logits_body,
        grid_spec=pltpu.PrefetchScalarGridSpec(
            num_scalar_prefetch=1,
            grid=(TILES,),
            in_specs=[pl.BlockSpec((4, HALF, 256), lambda i, at: (0, 0, 0))] * 8
            + [pl.BlockSpec((1, ROWS), lambda i, at: (0, 0)), pl.BlockSpec((TILE, WIDTH), lambda i, at: (i, 0))],
            out_specs=[
                pl.BlockSpec((TILE, ROWS), lambda i, at: (i, 0)),
                whole,
                whole,
            ],
            scratch_shapes=[pltpu.VMEM((ROWS, WIDTH), BF)],
        ),
        out_shape=[
            jax.ShapeDtypeStruct((VOC, ROWS), BF),
            jax.ShapeDtypeStruct((8, ROWS), F32),
            jax.ShapeDtypeStruct((8, ROWS), F32),
        ],
        compiler_params=params(),
        cost_estimate=SMALL,
        name="logits",
    )(at, *pieces, tid, emb)


def merge(parts):
    top = functools.reduce(jnp.maximum, [p[0:1] for p in parts])
    total = sum(p[1:2] * jnp.exp(p[0:1] - top) for p in parts)
    hit = sum(p[2:3] for p in parts)
    return top, total, hit


def merge_call(*parts):
    return jnp.concatenate([*merge(parts), jnp.zeros((5, ROWS), F32)])


def finish_body(a, b, st, tid, mix, weight, pack, grad_mix):
    top, total, hit = merge([a[...], b[...]])
    lse = top + jnp.log(total)
    gap = hit - lse
    mixes = [mix[pl.ds(k, 1), :] for k in range(4)]
    big = functools.reduce(jnp.maximum, mixes)
    norm = big + jnp.log(sum(jnp.exp(m - big) for m in mixes))
    logm = [m - norm for m in mixes]
    score = [logm[k] + gap[:, k * 128 : (k + 1) * 128] for k in range(4)]
    big = functools.reduce(jnp.maximum, score)
    ex = [jnp.exp(s - big) for s in score]
    den = sum(ex)
    w = weight[...]
    scaled = []
    for k in range(4):
        resp = ex[k] / den
        grad_mix[pl.ds(k, 1), :] = w * (jnp.exp(logm[k]) - resp)
        scaled.append(w * resp)
    d = jnp.concatenate(scaled, axis=1)
    pack[...] = jnp.zeros((8, ROWS), F32)
    pack[pl.ds(0, TILES), :] = jnp.exp(st[pl.ds(0, TILES), :] - lse) * d
    pack[pl.ds(4, 1), :] = d
    pack[pl.ds(5, 1), :] = lse
    pack[pl.ds(6, 1), :] = tid[...].astype(F32)


def finish_call(a, b, st, tid, mix, weight):
    stat = pl.BlockSpec((8, ROWS), lambda i: (0, 0))
    part = pl.BlockSpec((4, 128), lambda i: (0, 0))
    return pl.pallas_call(
        finish_body,
        grid=(1,),
        in_specs=[stat] * 3
        + [pl.BlockSpec((1, ROWS), lambda i: (0, 0)), part, pl.BlockSpec((1, 128), lambda i: (0, 0))],
        out_specs=[stat, part],
        out_shape=[
            jax.ShapeDtypeStruct((8, ROWS), F32),
            jax.ShapeDtypeStruct((4, 128), F32),
        ],
        compiler_params=params(),
        cost_estimate=SMALL,
        name="finish",
    )(a, b, st, tid, mix, weight)


def token_grad(e, pack, scale, base):
    ids = lax.broadcasted_iota(jnp.int32, e.shape, 0) + base
    tid = pack[pl.ds(6, 1), :].astype(jnp.int32)
    g = e.astype(F32) * scale
    return (g - jnp.where(ids == tid, pack[pl.ds(4, 1), :], 0.0)).astype(BF)


def hidden_body(at, e, pack, w0, w1, w2, w3, keep, send0, send1, tgt_out, tg):
    @pl.when(pl.program_id(0) == 0)
    def _():
        for t in range(VOC // SUB):
            rows = pl.ds(t * SUB, SUB)
            g = token_grad(e[rows, :], pack, pack[pl.ds(t * SUB // TILE, 1), :], t * SUB)
            tgt_out[rows, :] = g
            tg[:, rows] = g.T

    w = jnp.concatenate([w0[...], w1[...], w2[...], w3[...]], axis=1)
    r = dot_nn(tg[...], w)
    first = at[2] == 0
    for k in range(4):
        cols = slice(k * 256, (k + 1) * 256)
        a, b = r[:HALF, cols], r[HALF:, cols]
        keep[0, k] = jnp.where(first, a, b).astype(BF)
        (send0, send1)[k // 2][k % 2, 0] = jnp.where(first, b, a).astype(BF)


def hidden_call(at, e, pack, emb):
    whole = lambda s: pl.BlockSpec(s, lambda i, at: (0,) * len(s))

    def weight(k):
        def index(i, at):
            dx = jnp.where(at[2] == 0, i, k)
            dz = jnp.where(at[2] == 0, k, i)
            return (0, ((at[0] + dx) & 3) * 4 + ((at[1] + dz) & 3))

        return pl.BlockSpec((VOC, 256), index)

    return pl.pallas_call(
        hidden_body,
        grid_spec=pltpu.PrefetchScalarGridSpec(
            num_scalar_prefetch=1,
            grid=(4,),
            in_specs=[whole((VOC, ROWS)), whole((8, ROWS))] + [weight(k) for k in range(4)],
            out_specs=[
                pl.BlockSpec((1, 4, HALF, 256), lambda i, at: (i, 0, 0, 0)),
            ]
            + [pl.BlockSpec((2, 1, HALF, 256), lambda i, at: (0, i, 0, 0))] * 2
            + [
                whole((VOC, ROWS)),
            ],
            scratch_shapes=[pltpu.VMEM((ROWS, VOC), BF)],
        ),
        out_shape=[
            jax.ShapeDtypeStruct((4, 4, HALF, 256), BF),
        ]
        + [jax.ShapeDtypeStruct((2, 4, HALF, 256), BF)] * 2
        + [jax.ShapeDtypeStruct((VOC, ROWS), BF)],
        compiler_params=params(),
        cost_estimate=SMALL,
        name="hidden",
    )(at, e, pack, emb, emb, emb, emb)


def add(*xs):
    return sum(x.astype(F32) for x in xs)


def scatter(keep, recv, c, first, second):
    b = [add(keep[d], recv[d // 2][d % 2]) for d in range(4)]
    u = [cross(b[d].astype(BF), 0, 4 - d) for d in (1, 2, 3)]
    u1, u2, u3, work = gate(*u, first())
    t = add(b[0], u1, u2, u3)
    u = [cross(t[d].astype(BF), 1, 4 - d) for d in (1, 2, 3)]
    u1, u2, u3, work = gate(*u, second(work))
    f = add(t[0], u1, u2, u3)
    low, high = f[:, :128], f[:, 128:]
    mine, other = jnp.where(c == 0, low, high), jnp.where(c == 0, high, low)
    got = sibling(other)
    return jnp.where(c == 0, jnp.concatenate([mine, got]), jnp.concatenate([got, mine])), work


def feature_spec(d):
    return pl.BlockSpec((1, 4, 2, ROWS, 128), lambda i, at: ((at[3] + d) & 3, 0, 0, 0, 0))


def columns(f):
    return jnp.concatenate([f[0, k // 2, k % 2] for k in range(8)], axis=1)


def embed_a_body(at, tgt, ep, em, pack_p, pack_m, f0, f1, f3, acc):
    i = pl.program_id(0)
    parts = [tgt[...]]
    for e, pack in ((ep, pack_p), (em, pack_m)):
        parts.append(token_grad(e[...], pack, pack[pl.ds(i, 1), :], i * TILE))
    q = jnp.concatenate([columns(f) for f in (f0, f1, f3)], axis=0)
    acc[...] = dot_nn(jnp.concatenate(parts, axis=1), q).astype(BF)


def embed_a_call(at, tgt, ep, em, packs, feats):
    tile = pl.BlockSpec((TILE, ROWS), lambda i, at: (i, 0))
    pack = pl.BlockSpec((8, ROWS), lambda i, at: (0, 0))
    return pl.pallas_call(
        embed_a_body,
        grid_spec=pltpu.PrefetchScalarGridSpec(
            num_scalar_prefetch=1,
            grid=(TILES,),
            in_specs=[tile, tile, tile, pack, pack] + [feature_spec(d) for d in (0, 1, 3)],
            out_specs=pl.BlockSpec((TILE, 1024), lambda i, at: (i, 0)),
        ),
        out_shape=jax.ShapeDtypeStruct((VOC, 1024), BF),
        compiler_params=params(MOST),
        cost_estimate=SMALL,
        name="embed_a",
    )(at, tgt, ep, em, *packs, feats, feats, feats)


def embed_b_body(at, acc, low, high, pack, f2, out):
    i = pl.program_id(0)
    e = jnp.where(i < CUT // TILE, low[...], high[...])
    g = token_grad(e, pack, pack[pl.ds(i, 1), :], i * TILE)
    out[...] = (acc[...].astype(F32) + dot_nn(g, columns(f2))).astype(BF)


def embed_b_call(at, acc, low, high, pack, feats):
    n = CUT // TILE
    return pl.pallas_call(
        embed_b_body,
        grid_spec=pltpu.PrefetchScalarGridSpec(
            num_scalar_prefetch=1,
            grid=(TILES,),
            in_specs=[
                pl.BlockSpec((TILE, 1024), lambda i, at: (i, 0)),
                pl.BlockSpec((TILE, ROWS), lambda i, at: (jnp.minimum(i, n - 1), 0)),
                pl.BlockSpec((TILE, ROWS), lambda i, at: (jnp.maximum(i - n, 0), 0)),
                pl.BlockSpec((8, ROWS), lambda i, at: (0, 0)),
                feature_spec(2),
            ],
            out_specs=pl.BlockSpec((TILE, 1024), lambda i, at: (i, 0)),
        ),
        out_shape=jax.ShapeDtypeStruct((VOC, 1024), BF),
        compiler_params=params(MOST),
        cost_estimate=SMALL,
        name="embed_b",
    )(at, acc, low, high, pack, feats)


def local(comp_hidden, embed, mix, targets, weight):
    x, z, c, y = (lax.axis_index(a).astype(jnp.int32) for a in ("x", "z", "c", "y"))
    at = jnp.stack([x, z, c, y])
    own = comp_hidden.reshape(ROWS, 128)
    tid = jnp.tile(targets - ((x * 4 + z) * 2 + c) * VOC, 4).reshape(1, ROWS)

    swap = [(a * 4 + b, b * 4 + a) for a in range(4) for b in range(4)]
    turned = lax.ppermute(own, ("x", "y"), swap)

    low, high = own[:HALF], own[HALF:]
    mine, other = jnp.where(c == 0, low, high), jnp.where(c == 0, high, low)
    got = sibling(other)
    block = jnp.where(c == 0, jnp.concatenate([mine, got], axis=1), jnp.concatenate([got, mine], axis=1))
    pieces, at, tid = gather_pieces(block, at, tid)
    pieces = pieces + [sibling(p) for p in pieces]

    e, st, loc = logits_call(at, pieces, tid, embed)
    loc, turned = gate(loc, turned)
    feats = lax.all_gather(turned, ("x", "z", "c")).reshape(4, 4, 2, ROWS, 128)
    ep, em = shift(e, "y", 1), shift(e, "y", 3)

    s = merge_call(loc, *(shift(loc, "x", d) for d in (1, 2, 3)))
    s = merge_call(s, *(shift(s, "z", d) for d in (1, 2, 3)))
    pack, grad_mix = finish_call(s, sibling(s), st, tid, mix, weight.reshape(1, 128))
    packs = [shift(pack, "y", d) for d in (1, 3, 2)]
    keep, *send, tgt = hidden_call(at, e, pack, embed)
    pack_p, pack_m, low, high = onward(ep, em, packs[0], packs[1])
    low, high = shift(low, "y", 1), shift(high, "y", 3)

    grad_hidden, grad_embed = scatter(
        keep,
        [sibling(t) for t in send],
        c,
        lambda: embed_a_call(at, tgt, ep, em, (pack_p, pack_m), feats),
        lambda acc: embed_b_call(at, acc, low, high, packs[2], feats),
    )
    return grad_hidden.reshape(4, 128, 128), grad_embed, grad_mix


def solution(mesh):
    fine = Mesh(mesh.devices.reshape(4, 4, 2, 4), ("x", "z", "c", "y"))
    v = ("x", "z", "c")
    return jax.shard_map(
        local,
        mesh=fine,
        in_specs=(P(None, "y", v), P(v, None), P(None, "y"), P("y"), P("y")),
        out_specs=(P(None, "y", v), P(v, "y"), P(None, "y")),
        check_vma=False,
    )
```
